32 devices in a mesh: grp: 4 (over y, x), shard: 8 (over z, core).
Axes of the slice: x: 2, y: 2, z: 4, core: 2. Of those that a mesh axis runs over, the one named last changes fastest.
Arguments:
- latents: float32 [256, 256, 16], P(('grp', 'shard')), may hold values from -6 to 6
- noise: float32 [256, 256, 16], P(('grp', 'shard')), may hold values from -6 to 6
- velocity: float32 [256, 256, 32], P(('grp', 'shard')), may hold values from -6 to 6
- labels: int32 [256], P(('grp', 'shard')), may hold values from 0 to 1000
- time_index: int32 [256], P(('grp', 'shard')), may hold values from 0 to 999
- times: float32 [1000], replicated, may hold values from 0 to 1, as said below
- in_mats: float32 [1, 768, 9984], P(None, 'shard'), may hold values from -0.21875 to 0.21875
- out_mats: float32 [1, 3840, 768], P(None, 'shard'), may hold values from -0.3125 to 0.3125
- embed_mats: float32 [1040, 768], P(None, 'shard'), may hold values from -0.75 to 0.75
- class_table: float32 [1001, 768], P(None, 'shard'), may hold values from -0.625 to 0.625
- final_ada: float32 [768, 1536], P('shard'), may hold values from -0.21875 to 0.21875
- head_mat: float32 [769, 32], replicated, may hold values from -0.21875 to 0.21875
- bias_vec: float32 [14592], P('shard'), may hold values from -0.625 to 0.625
- in_mats_first: float32 [1, 768, 9984], P(None, 'shard'), may hold values from -1.9073486e-06 to 1.9073486e-06
- out_mats_first: float32 [1, 3840, 768], P(None, 'shard'), may hold values from -1.9073486e-06 to 1.9073486e-06
- embed_first: float32 [1040, 768], P(None, 'shard'), may hold values from -1.9073486e-06 to 1.9073486e-06
- table_first: float32 [1001, 768], P(None, 'shard'), may hold values from -9.313226e-09 to 9.313226e-09
- final_first: float32 [768, 1536], P('shard'), may hold values from -1.9073486e-06 to 1.9073486e-06
- head_first: float32 [769, 32], replicated, may hold values from -1.9073486e-06 to 1.9073486e-06
- bias_first: float32 [14592], P('shard'), may hold values from -1.9073486e-06 to 1.9073486e-06
- in_mats_second: float32 [1, 768, 9984], P(None, 'shard'), may hold values from 7.460923e-15 to 2.984369e-14
- out_mats_second: float32 [1, 3840, 768], P(None, 'shard'), may hold values from 7.460923e-15 to 2.984369e-14
- embed_second: float32 [1040, 768], P(None, 'shard'), may hold values from 7.460923e-15 to 2.984369e-14
- table_second: float32 [1001, 768], P(None, 'shard'), may hold values from 1.7932872e-19 to 7.173149e-19
- final_second: float32 [768, 1536], P('shard'), may hold values from 7.460923e-15 to 2.984369e-14
- head_second: float32 [769, 32], replicated, may hold values from 7.460923e-15 to 2.984369e-14
- bias_second: float32 [14592], P('shard'), may hold values from 7.460923e-15 to 2.984369e-14
Outputs:
- in_mats_new: float32 [1, 768, 9984], P(None, 'shard')
- out_mats_new: float32 [1, 3840, 768], P(None, 'shard')
- embed_new: float32 [1040, 768], P(None, 'shard')
- table_new: float32 [1001, 768], P(None, 'shard')
- final_new: float32 [768, 1536], P('shard')
- head_new: float32 [769, 32], replicated
- bias_new: float32 [14592], P('shard')
- in_mats_first_new: float32 [1, 768, 9984], P(None, 'shard')
- out_mats_first_new: float32 [1, 3840, 768], P(None, 'shard')
- embed_first_new: float32 [1040, 768], P(None, 'shard')
- table_first_new: float32 [1001, 768], P(None, 'shard')
- final_first_new: float32 [768, 1536], P('shard')
- head_first_new: float32 [769, 32], replicated
- bias_first_new: float32 [14592], P('shard')
- in_mats_second_new: float32 [1, 768, 9984], P(None, 'shard')
- out_mats_second_new: float32 [1, 3840, 768], P(None, 'shard')
- embed_second_new: float32 [1040, 768], P(None, 'shard')
- table_second_new: float32 [1001, 768], P(None, 'shard')
- final_second_new: float32 [768, 1536], P('shard')
- head_second_new: float32 [769, 32], replicated
- bias_second_new: float32 [14592], P('shard')
- loss_sum: float32 [], replicated
- grad_norm: float32 [], replicated
The draws below stay inside these ranges and needn't reach their ends.
Inputs may be any that keep to these rules, and one draw needn't show every extreme that they name: `times`: increasing.
All inputs are finite; a program needn't handle non-finite values.
Results may differ from the reference program's by a relative error of at most 0.012.
The reference program's roundings to bfloat16 on the way count: a program that leaves them out, or rounds other values in their place, can miss the bound.
Values may be sent and summed in bfloat16 or wider, within the bound.
No kernel may reach another device: no remote copies, remote signals or barrier semaphores. Data moves between devices by JAX's collectives and lax.ppermute only.
A program may use at most 320 MiB of HBM per device.

```python
import math
import jax
import jax.numpy as jnp
from jax import lax

D = 768
HEADS = 12
HDIM = 64
FF = 3072
PATCH = 16
TFREQ = 256
NCLASS = 1001
OUT = 32
GRID = 16
SEQ = 256
LAYERS = 1
STEP = 10
NT = 1000
IMAGES = 256
NBIAS = 14592
NPARAM = 13403168


def draw_times(key, part):
    key = jax.random.fold_in(key, 11)
    jitter = jax.random.uniform(key, (NT,), jnp.float32, 0.05, 0.95)
    return (jnp.arange(NT, dtype=jnp.float32) + jitter) / NT


def draw_time_index(key, part):
    key = jax.random.fold_in(key, 12)
    ranked = jnp.arange(IMAGES, dtype=jnp.int32)
    lowest = ranked * NT // (2 * IMAGES)
    chosen = lowest + jax.random.randint(key, (IMAGES,), 0, NT // 2, dtype=jnp.int32)
    chosen = jnp.where(ranked == 0, 0, chosen)
    return jnp.where(ranked == IMAGES - 1, NT - 1, chosen).astype(jnp.int32)


def place_ends(array, own_key, smallest, high):
    dims = array.shape
    spot = [jax.random.randint(jax.random.fold_in(own_key, axis), (), 0, dims[axis]) for axis in range(len(dims))]
    array = array.at[tuple(spot)].set(smallest)
    longest = dims.index(max(dims))
    spot[longest] = (spot[longest] + 1) % dims[longest]
    return array.at[tuple(spot)].set(high)


def steps_of(own_key, extent, cuts, smallest, high):
    factor_of, own = 1.0, jax.random.fold_in(own_key, 6)
    for dim, shards_of in cuts:
        draws = jnp.exp(jax.random.uniform(jax.random.fold_in(own, dim), (shards_of,), jnp.float32, smallest / len(cuts), high / len(cuts)))
        factor_of = factor_of * jnp.repeat(draws, extent[dim] // shards_of).reshape([-1 if axis == dim else 1 for axis in range(len(extent))])
    return factor_of


def gaussian(rng, shape, deviation, limit, pieces=(), kind=jnp.bfloat16):
    entries = deviation * jax.random.normal(rng, shape, jnp.float32)
    if pieces:
        entries = entries * steps_of(rng, shape, pieces, -0.22, 0.18)
    return jnp.clip(entries, -limit, limit).astype(kind)


def setup_inputs(seed: int = 0) -> dict:
    key_of = jax.random.split(jax.random.key(seed), 28)
    latents = gaussian(key_of[0], (IMAGES, SEQ, PATCH), 1.0, 6.0, ((0, 32),), jnp.float32)
    noise = gaussian(key_of[1], (IMAGES, SEQ, PATCH), 1.0, 6.0, ((0, 32),), jnp.float32)
    velocity = gaussian(key_of[2], (IMAGES, SEQ, OUT), 1.0, 6.0, ((0, 32),), jnp.float32)
    labels = place_ends(jax.random.randint(key_of[3], (IMAGES,), 0, NCLASS), jax.random.fold_in(key_of[3], 1), 0, NCLASS - 1).astype(jnp.int32)
    time_index = draw_time_index(jax.random.fold_in(key_of[27], 71), 0)
    times = draw_times(jax.random.fold_in(key_of[27], 71), 0)
    in_mats = gaussian(key_of[6], (LAYERS, D, 9 * D + FF), D ** -0.5, 0.21875, ((1, 8),), jnp.float32)
    out_mats = gaussian(key_of[7], (LAYERS, D + FF, D), (D // 2) ** -0.5, 0.3125, ((1, 8),), jnp.float32)
    embed_mats = gaussian(key_of[8], (PATCH + TFREQ + D, D), 0.12, 0.75, ((1, 8),), jnp.float32)
    class_table = gaussian(key_of[9], (NCLASS, D), 0.1, 0.625, ((1, 8),), jnp.float32)
    final_ada = gaussian(key_of[10], (D, 2 * D), D ** -0.5, 0.21875, ((0, 8),), jnp.float32)
    head_mat = gaussian(key_of[11], (D + 1, OUT), D ** -0.5, 0.21875, (), jnp.float32)
    bias_vec = gaussian(key_of[12], (NBIAS,), 0.1, 0.625, ((0, 8),), jnp.float32)
    in_mats_first = gaussian(key_of[13], (LAYERS, D, 9 * D + FF), (0.0011 / NPARAM ** 0.5), 1.9073486328125e-06, ((1, 8),), jnp.float32)
    out_mats_first = gaussian(key_of[14], (LAYERS, D + FF, D), (0.0011 / NPARAM ** 0.5), 1.9073486328125e-06, ((1, 8),), jnp.float32)
    embed_first = gaussian(key_of[15], (PATCH + TFREQ + D, D), (0.0011 / NPARAM ** 0.5), 1.9073486328125e-06, ((1, 8),), jnp.float32)
    table_first = gaussian(key_of[16], (NCLASS, D), (0.000077 * ((1 + IMAGES / NCLASS) / IMAGES) ** 0.5 / NPARAM ** 0.5), 9.313225746154785e-09, ((1, 8),), jnp.float32)
    final_first = gaussian(key_of[17], (D, 2 * D), (0.0011 / NPARAM ** 0.5), 1.9073486328125e-06, ((0, 8),), jnp.float32)
    head_first = gaussian(key_of[18], (D + 1, OUT), (0.0011 / NPARAM ** 0.5), 1.9073486328125e-06, (), jnp.float32)
    bias_first = gaussian(key_of[19], (NBIAS,), (0.0011 / NPARAM ** 0.5), 1.9073486328125e-06, ((0, 8),), jnp.float32)
    in_mats_second = jnp.clip(jnp.exp(math.log(2.984369140159558e-14) - 1.3862944 * jax.random.uniform(key_of[20], (LAYERS, D, 9 * D + FF), jnp.float32) ** steps_of(key_of[20], (LAYERS, D, 9 * D + FF), ((1, 8),), -0.2, 0.2)), 7.460922850398895e-15, 2.984369140159558e-14)
    out_mats_second = jnp.clip(jnp.exp(math.log(2.984369140159558e-14) - 1.3862944 * jax.random.uniform(key_of[21], (LAYERS, D + FF, D), jnp.float32) ** steps_of(key_of[21], (LAYERS, D + FF, D), ((1, 8),), -0.2, 0.2)), 7.460922850398895e-15, 2.984369140159558e-14)
    embed_second = jnp.clip(jnp.exp(math.log(2.984369140159558e-14) - 1.3862944 * jax.random.uniform(key_of[22], (PATCH + TFREQ + D, D), jnp.float32) ** steps_of(key_of[22], (PATCH + TFREQ + D, D), ((1, 8),), -0.2, 0.2)), 7.460922850398895e-15, 2.984369140159558e-14)
    table_second = jnp.clip(jnp.exp(math.log(7.173148971840408e-19) - 1.3862944 * jax.random.uniform(key_of[23], (NCLASS, D), jnp.float32) ** steps_of(key_of[23], (NCLASS, D), ((1, 8),), -0.2, 0.2)), 1.793287242960102e-19, 7.173148971840408e-19)
    final_second = jnp.clip(jnp.exp(math.log(2.984369140159558e-14) - 1.3862944 * jax.random.uniform(key_of[24], (D, 2 * D), jnp.float32) ** steps_of(key_of[24], (D, 2 * D), ((0, 8),), -0.2, 0.2)), 7.460922850398895e-15, 2.984369140159558e-14)
    head_second = jnp.clip(jnp.exp(jax.random.uniform(key_of[25], (D + 1, OUT), jnp.float32, math.log(7.460922850398895e-15), math.log(2.984369140159558e-14))), 7.460922850398895e-15, 2.984369140159558e-14)
    bias_second = jnp.clip(jnp.exp(math.log(2.984369140159558e-14) - 1.3862944 * jax.random.uniform(key_of[26], (NBIAS,), jnp.float32) ** steps_of(key_of[26], (NBIAS,), ((0, 8),), -0.2, 0.2)), 7.460922850398895e-15, 2.984369140159558e-14)
    return dict(latents=latents, noise=noise, velocity=velocity, labels=labels, time_index=time_index, times=times, in_mats=in_mats, out_mats=out_mats, embed_mats=embed_mats, class_table=class_table, final_ada=final_ada, head_mat=head_mat, bias_vec=bias_vec, in_mats_first=in_mats_first, out_mats_first=out_mats_first, embed_first=embed_first, table_first=table_first, final_first=final_first, head_first=head_first, bias_first=bias_first, in_mats_second=in_mats_second, out_mats_second=out_mats_second, embed_second=embed_second, table_second=table_second, final_second=final_second, head_second=head_second, bias_second=bias_second)


@jax.custom_vjp
def low(v):
    return lax.optimization_barrier(v.astype(jnp.bfloat16)).astype(jnp.float32)

@jax.custom_vjp
def low_back(v):
    return v

def low_keep(v):
    return (low(v), None)

def low_pass(kept, grad):
    return (grad,)

def back_keep(v):
    return (v, None)

def back_low(kept, grad):
    return (low(grad),)
low.defvjp(low_keep, low_pass)
low_back.defvjp(back_keep, back_low)
EPS_NORM = 1e-06
BETA_ONE = 0.9
BETA_TWO = 0.999
LEARN_RATE = 0.05
WEIGHT_DECAY = 0.05
EPS_ADAM = 1e-08
CLIP_NORM = 0.01

def product(formula, left, right):
    return jnp.einsum(formula, left, right, precision=lax.Precision.HIGHEST)

def layer_norm(array_in):
    centre = array_in - lax.optimization_barrier(jnp.mean(array_in, -1, keepdims=True))
    return centre * lax.rsqrt(lax.optimization_barrier(jnp.mean(centre * centre, -1, keepdims=True)) + EPS_NORM)

def modulate(array_in, shift, scale):
    return layer_norm(array_in) * (1.0 + scale[:, None, :]) + shift[:, None, :]

def position_table(grid_side, width_all):
    quarter = width_all // 4
    angular = jnp.exp(-math.log(10000.0) * jnp.arange(quarter, dtype=jnp.float32) / quarter)
    position = jnp.arange(grid_side * grid_side, dtype=jnp.int32)
    column = (position % grid_side).astype(jnp.float32)[:, None] * angular
    row_pos = (position // grid_side).astype(jnp.float32)[:, None] * angular
    return jnp.concatenate([jnp.sin(column), jnp.cos(column), jnp.sin(row_pos), jnp.cos(row_pos)], 1)

def time_features(moment, feature_count):
    half_count = feature_count // 2
    frequency = jnp.exp(-math.log(10000.0) * jnp.arange(half_count, dtype=jnp.float32) / half_count)
    angles = moment[:, None] * frequency
    return jnp.concatenate([jnp.cos(angles), jnp.sin(angles)], 1)

def pick_times(time_index, times):
    matches = time_index[:, None] == jnp.arange(times.shape[0], dtype=jnp.int32)[None, :]
    return lax.optimization_barrier(jnp.sum(jnp.where(matches, times[None, :], 0.0), 1))

def forward(weights_in, noisy_in, moment, labels, velocity):
    in_mats, out_mats, embed_mats, class_table, final_ada, head_mat, bias_vec = [low(weight) for weight in weights_in]
    images = noisy_in.shape[0]
    embedded = low_back(product('bsp,pd->bsd', low(noisy_in), embed_mats[:PATCH]) + bias_vec[:D])
    stream = embedded + position_table(GRID, D)[None]
    time_pre = low_back(product('bf,fd->bd', low(time_features(moment, TFREQ)), embed_mats[PATCH:PATCH + TFREQ]) + bias_vec[D:2 * D])
    cond_time = product('bd,de->be', low(jax.nn.silu(time_pre)), embed_mats[PATCH + TFREQ:]) + bias_vec[2 * D:3 * D]
    onehot = (labels[:, None] == jnp.arange(NCLASS, dtype=jnp.int32)[None, :]).astype(jnp.float32)
    condition = low_back(cond_time + product('bn,nd->bd', onehot, class_table))
    cond_act = low(jax.nn.silu(condition))
    head_shape = (images, SEQ, HEADS, HDIM)
    for layer_index in range(LAYERS):
        offset = 3 * D + layer_index * (10 * D + FF)
        in_block = in_mats[layer_index]
        out_block = out_mats[layer_index]
        modulation = low_back(product('bd,de->be', cond_act, in_block[:, :6 * D]) + bias_vec[offset:offset + 6 * D])
        shift_attn, scale_attn, gate_attn, shift_feed, scale_feed, gate_feed = jnp.split(modulation, 6, 1)
        normed = low(modulate(stream, shift_attn, scale_attn))
        qkv_bias = jnp.concatenate([bias_vec[offset + 6 * D:offset + 7 * D], jnp.zeros((D,), jnp.float32), bias_vec[offset + 7 * D:offset + 8 * D]])
        projected = low(low_back(product('bsd,de->bse', normed, in_block[:, 6 * D:9 * D]) + qkv_bias))
        queries = projected[..., :D].reshape(head_shape)
        keys_all = projected[..., D:2 * D].reshape(head_shape)
        values = projected[..., 2 * D:].reshape(head_shape)
        scores = low_back(product('bqhd,bkhd->bhqk', queries, keys_all) * HDIM ** (-0.5))
        probabilities = low(jax.nn.softmax(scores, -1))
        mixed_heads = low(low_back(product('bhqk,bkhd->bqhd', probabilities, values))).reshape(images, SEQ, D)
        attn_out = low_back(product('bsd,de->bse', mixed_heads, out_block[:D]) + bias_vec[offset + 8 * D:offset + 9 * D])
        stream = stream + gate_attn[:, None, :] * attn_out
        normed = low(modulate(stream, shift_feed, scale_feed))
        upper_pre = low_back(product('bsd,df->bsf', normed, in_block[:, 9 * D:]) + bias_vec[offset + 9 * D:offset + 9 * D + FF])
        feed_out = low_back(product('bsf,fd->bsd', low(jax.nn.gelu(upper_pre, approximate=True)), out_block[D:]) + bias_vec[offset + 9 * D + FF:offset + 10 * D + FF])
        stream = stream + gate_feed[:, None, :] * feed_out
    final_base = 3 * D + LAYERS * (10 * D + FF)
    final = low_back(product('bd,de->be', cond_act, final_ada) + bias_vec[final_base:final_base + 2 * D])
    shift_final, scale_final = jnp.split(final, 2, 1)
    predicted = low_back(product('bsd,do->bso', low(modulate(stream, shift_final, scale_final)), head_mat[:D]) + head_mat[D])
    residual = predicted - velocity
    loss_total = jnp.sum(moment[:, None, None] * residual * residual)
    return (loss_total / (IMAGES * SEQ * OUT), loss_total)

def adamw(weight, moment_one, moment_two, gradient, factor):
    gradient = gradient * factor
    moment_one = BETA_ONE * moment_one + (1.0 - BETA_ONE) * gradient
    moment_two = BETA_TWO * moment_two + (1.0 - BETA_TWO) * gradient * gradient
    fix_one = 1.0 - BETA_ONE ** STEP
    fix_two = 1.0 - BETA_TWO ** STEP
    update = moment_one / fix_one / (jnp.sqrt(moment_two / fix_two) + EPS_ADAM) + WEIGHT_DECAY * weight
    return (weight - LEARN_RATE * update, moment_one, moment_two)

def reference(latents, noise, velocity, labels, time_index, times, in_mats, out_mats, embed_mats, class_table, final_ada, head_mat, bias_vec, in_mats_first, out_mats_first, embed_first, table_first, final_first, head_first, bias_first, in_mats_second, out_mats_second, embed_second, table_second, final_second, head_second, bias_second):
    weights = (in_mats, out_mats, embed_mats, class_table, final_ada, head_mat, bias_vec)
    firsts = (in_mats_first, out_mats_first, embed_first, table_first, final_first, head_first, bias_first)
    seconds = (in_mats_second, out_mats_second, embed_second, table_second, final_second, head_second, bias_second)
    moment_all = pick_times(time_index, times)
    noisy_all = (1.0 - moment_all)[:, None, None] * latents + moment_all[:, None, None] * noise
    block_size = math.gcd(IMAGES, 16)
    block_count = IMAGES // block_size

    def visit(carry, block_index):
        grads, loss_total = carry
        first_row = block_index * block_size

        def take_rows(array_in):
            return lax.dynamic_slice_in_dim(array_in, first_row, block_size, 0)

        def objective(*weights_in):
            return forward(weights_in, take_rows(noisy_all), take_rows(moment_all), take_rows(labels), take_rows(velocity))
        loss_value, pullback, part_sum = jax.vjp(objective, *weights, has_aux=True)
        additional = pullback(jnp.ones((), jnp.float32))
        return ((tuple((old_grad + new_grad for old_grad, new_grad in zip(grads, additional))), loss_total + part_sum), None)
    start = (tuple((jnp.zeros_like(weight) for weight in weights)), jnp.zeros((), jnp.float32))
    (grads, loss_sum), unused = lax.scan(visit, start, jnp.arange(block_count, dtype=jnp.int32))
    squares = sum((jnp.sum(gradient * gradient) for gradient in grads))
    grad_norm = jnp.sqrt(squares)
    factor = CLIP_NORM / jnp.maximum(grad_norm, CLIP_NORM)
    stepped = [adamw(weight, moment_one, moment_two, gradient, factor) for weight, moment_one, moment_two, gradient in zip(weights, firsts, seconds, grads)]
    return (stepped[0][0], stepped[1][0], stepped[2][0], stepped[3][0], stepped[4][0], stepped[5][0], stepped[6][0], stepped[0][1], stepped[1][1], stepped[2][1], stepped[3][1], stepped[4][1], stepped[5][1], stepped[6][1], stepped[0][2], stepped[1][2], stepped[2][2], stepped[3][2], stepped[4][2], stepped[5][2], stepped[6][2], loss_sum, grad_norm)
```

```python
import math
from functools import partial
import jax
import jax.numpy as jnp
from jax import lax
from jax.sharding import PartitionSpec as P
from jax.experimental import pallas as pl
from jax.experimental.pallas import tpu as pltpu

D = 768
HEADS = 12
HDIM = 64
FF = 3072
PATCH = 16
SEQ = 256
OUT = 32
TFREQ = 256
NCLASS = 1001
GRID = 16
STEP = 10
BETA_ONE = 0.9
BETA_TWO = 0.999
LEARN_RATE = 0.05
WEIGHT_DECAY = 0.05
EPS_ADAM = 1e-08
CLIP_NORM = 0.01
EPS_NORM = 1e-06
BF = jnp.bfloat16
F32 = jnp.float32
VMEM_LIMIT = 60 * 1024 * 1024
PAIR = 2 * HDIM
PAIRS = HEADS // 2


def dot(left, right):
    return jnp.dot(left, right, preferred_element_type=F32)


def dot_nt(left, right):
    return lax.dot_general(left, right, (((1,), (1,)), ((), ())), preferred_element_type=F32)


def dot_tn(left, right):
    return lax.dot_general(left, right, (((0,), (0,)), ((), ())), preferred_element_type=F32)


def whole(shape):
    zeros = (0,) * len(shape)
    return pl.BlockSpec(shape, lambda step: zeros, pipeline_mode=pl.Buffered(1))


def fixed(shape):
    zeros = (0,) * len(shape)
    return pl.BlockSpec(shape, lambda step: zeros)


def rows(count, *rest):
    zeros = (0,) * len(rest)
    return pl.BlockSpec((count,) + rest, lambda step: (step,) + zeros)


def shape_of(shape, dtype):
    return jax.ShapeDtypeStruct(shape, dtype)


def norm_parts(array_in):
    centre = array_in - jnp.mean(array_in, -1, keepdims=True)
    inverse = lax.rsqrt(jnp.mean(centre * centre, -1, keepdims=True) + EPS_NORM)
    return centre * inverse, inverse


def norm_back(grad_normed, normed, inverse):
    first = jnp.mean(grad_normed, -1, keepdims=True)
    second = jnp.mean(grad_normed * normed, -1, keepdims=True)
    return inverse * (grad_normed - first - normed * second)


def head_masks():
    lane = lax.broadcasted_iota(jnp.int32, (1, PAIR), 1)
    return (lane < HDIM, lane >= HDIM)


def attend_kernel(
    noisy_ref, pos_ref, wpatch_ref, mod_ref, wqkv_ref, bqkv_ref, a_ref, qkv_ref, o_ref, *, images
):
    masks = head_masks()

    def image(index, carry):
        stream = dot(noisy_ref[index], wpatch_ref[...]) + pos_ref[...]
        normed, unused = norm_parts(stream)
        a = (normed * (1.0 + mod_ref[index, :, D : 2 * D]) + mod_ref[index, :, :D]).astype(BF)
        a_ref[index] = a
        qkv_ref[index] = (dot(a, wqkv_ref[...]) + bqkv_ref[...]).astype(BF)
        for pair in range(PAIRS):
            base = pair * PAIR
            queries = qkv_ref[index, :, base : base + PAIR]
            keys = qkv_ref[index, :, D + base : D + base + PAIR]
            values = qkv_ref[index, :, 2 * D + base : 2 * D + base + PAIR]
            mixed = []
            for mask in masks:
                part = jnp.where(mask, queries * jnp.asarray(HDIM**-0.5, BF), jnp.zeros_like(queries))
                scores = dot_nt(part, keys)
                power = jnp.exp(scores - jnp.max(scores, -1, keepdims=True))
                total = jnp.sum(power, -1, keepdims=True)
                prob = (power * (1.0 / total)).astype(BF)
                mixed.append(dot(prob, values))
            o_ref[index, :, base : base + PAIR] = jnp.where(masks[0], mixed[0], mixed[1]).astype(BF)
        return carry

    lax.fori_loop(0, images, image, 0)


def attend(noisy, pos, wpatch, mod, wqkv, bqkv, images=2):
    batch = noisy.shape[0]
    return pl.pallas_call(
        partial(attend_kernel, images=images),
        grid=(batch // images,),
        in_specs=[
            rows(images, SEQ, PATCH),
            whole((SEQ, D)),
            whole((PATCH, D)),
            rows(images, 1, 3 * D),
            whole((D, 3 * D)),
            whole((1, 3 * D)),
        ],
        out_specs=[rows(images, SEQ, D), rows(images, SEQ, 3 * D), rows(images, SEQ, D)],
        out_shape=[
            shape_of((batch, SEQ, D), BF),
            shape_of((batch, SEQ, 3 * D), BF),
            shape_of((batch, SEQ, D), BF),
        ],
        compiler_params=pltpu.CompilerParams(vmem_limit_bytes=VMEM_LIMIT),
        name="attend",
    )(noisy, pos, wpatch, mod, wqkv, bqkv)


GELU_A = math.sqrt(2.0 / math.pi)
GELU_B = 0.044715


def gelu_both(u):
    square = u * u
    turn = jnp.tanh(u * (GELU_A + (GELU_A * GELU_B) * square))
    half = 0.5 + 0.5 * turn
    slope = half + (0.5 * u) * (1.0 - turn * turn) * (GELU_A + (3.0 * GELU_A * GELU_B) * square)
    return u * half, slope


def feed_kernel(
    noisy_ref, pos_ref, wpatch_ref, o_ref, mod_ref, bproj_ref, w1_ref, b1_ref, wout_ref, b2_ref,
    head_ref, hbias_ref, vel_ref, t_ref,
    mid_ref, y_ref, m_ref, g_ref, slope_ref, df_ref, ds_ref, dmod_ref, whead_ref, bhead_ref, bdown_ref, loss_ref,
    *, images, chunk, count_all
):
    step = pl.program_id(0)

    @pl.when(step == 0)
    def _():
        whead_ref[...] = jnp.zeros_like(whead_ref)
        bhead_ref[...] = jnp.zeros_like(bhead_ref)
        bdown_ref[...] = jnp.zeros_like(bdown_ref)
        loss_ref[...] = jnp.zeros_like(loss_ref)

    tokens = images * SEQ

    def spread(first, last):
        parts = [
            jnp.broadcast_to(mod_ref[index, :, first * D : last * D], (SEQ, (last - first) * D))
            for index in range(images)
        ]
        return jnp.concatenate(parts, 0)

    position = jnp.concatenate([pos_ref[...]] * images, 0)
    stream = dot(noisy_ref[...].reshape(tokens, PATCH), wpatch_ref[...]) + position
    y = dot(o_ref[...].reshape(tokens, D), wout_ref[:D]) + bproj_ref[...]
    y_ref[...] = y.astype(BF).reshape(images, SEQ, D)
    mid = stream + spread(0, 1) * y
    mid_ref[...] = mid.reshape(images, SEQ, D)
    normed, unused = norm_parts(mid)
    m = (normed * (1.0 + spread(2, 3)) + spread(1, 2)).astype(BF)
    m_ref[...] = m.reshape(images, SEQ, D)
    feed = jnp.broadcast_to(b2_ref[...], (tokens, D))
    for j in range(FF // chunk):
        cut = slice(j * chunk, (j + 1) * chunk)
        g, slope = gelu_both(dot(m, w1_ref[:, cut]) + b1_ref[:, cut])
        g = g.astype(BF)
        g_ref[:, cut] = g
        slope_ref[:, cut] = slope.astype(BF)
        feed = feed + dot(g, wout_ref[D + j * chunk : D + (j + 1) * chunk, :])
    gate = spread(3, 4)
    stream = mid + gate * feed
    normed, inverse = norm_parts(stream)
    scale = 1.0 + spread(5, 6)
    z = (normed * scale + spread(4, 5)).astype(BF)
    predicted = dot(z, head_ref[...]) + hbias_ref[...]
    t = t_ref[...].reshape(tokens, 1)
    residual = predicted - vel_ref[...].reshape(tokens, OUT)
    weighted = t * residual
    loss_ref[...] += jnp.sum(jnp.sum(weighted * residual, 0, keepdims=True), 1, keepdims=True)
    grad_pred = (2.0 * weighted / count_all).astype(BF)
    bhead_ref[...] += jnp.sum(grad_pred.astype(F32), 0, keepdims=True)
    whead_ref[...] += dot_tn(grad_pred, z)
    dz = dot_nt(grad_pred, head_ref[...])
    ds = norm_back(dz * scale, normed, inverse)
    ds_ref[...] = ds.reshape(images, SEQ, D)
    df = (ds * gate).astype(BF)
    df_ref[...] = df.reshape(images, SEQ, D)
    bdown_ref[...] += jnp.sum(df.astype(F32), 0, keepdims=True)
    for index in range(images):
        cut = slice(index * SEQ, (index + 1) * SEQ)
        dmod_ref[index, :, :D] = jnp.sum(ds[cut] * feed[cut], 0, keepdims=True)
        dmod_ref[index, :, D : 2 * D] = jnp.sum(dz[cut], 0, keepdims=True)
        dmod_ref[index, :, 2 * D :] = jnp.sum(dz[cut] * normed[cut], 0, keepdims=True)


def feed(noisy, pos, wpatch, o, mod, bproj, w1, b1, wout, b2, head, hbias, velocity, t, count_all, images=2, chunk=512):
    batch = o.shape[0]
    tokens = batch * SEQ
    return pl.pallas_call(
        partial(feed_kernel, images=images, chunk=chunk, count_all=count_all),
        grid=(batch // images,),
        in_specs=[
            rows(images, SEQ, PATCH),
            whole((SEQ, D)),
            whole((PATCH, D)),
            rows(images, SEQ, D),
            rows(images, 1, 6 * D),
            whole((1, D)),
            whole((D, FF)),
            whole((1, FF)),
            whole((D + FF, D)),
            whole((1, D)),
            whole((D, OUT)),
            whole((1, OUT)),
            rows(images, SEQ, OUT),
            rows(images, SEQ, 1),
        ],
        out_specs=[
            rows(images, SEQ, D),
            rows(images, SEQ, D),
            rows(images, SEQ, D),
            rows(images * SEQ, FF),
            rows(images * SEQ, FF),
            rows(images, SEQ, D),
            rows(images, SEQ, D),
            rows(images, 1, 3 * D),
            fixed((OUT, D)),
            fixed((1, OUT)),
            fixed((1, D)),
            fixed((1, 1)),
        ],
        out_shape=[
            shape_of((batch, SEQ, D), F32),
            shape_of((batch, SEQ, D), BF),
            shape_of((batch, SEQ, D), BF),
            shape_of((tokens, FF), BF),
            shape_of((tokens, FF), BF),
            shape_of((batch, SEQ, D), BF),
            shape_of((batch, SEQ, D), F32),
            shape_of((batch, 1, 3 * D), F32),
            shape_of((OUT, D), F32),
            shape_of((1, OUT), F32),
            shape_of((1, D), F32),
            shape_of((1, 1), F32),
        ],
        compiler_params=pltpu.CompilerParams(vmem_limit_bytes=VMEM_LIMIT),
        name="feed",
    )(noisy, pos, wpatch, o, mod, bproj, w1, b1, wout, b2, head, hbias, velocity, t)


def feed_back_kernel(
    m_ref, df_ref, g_ref, slope_ref, w1_ref, w2_ref, wup_ref, wdown_ref, bup_ref, dm_ref, mt, dft, *, tile
):
    step = pl.program_id(0)

    @pl.when(step == 0)
    def _():
        mt[...] = m_ref[...].T
        dft[...] = df_ref[...].T
        dm_ref[...] = jnp.zeros_like(dm_ref)

    tokens = m_ref.shape[0]
    chunk = w1_ref.shape[1]
    w1 = w1_ref[...]
    w2 = w2_ref[...]
    du_parts = []
    for i in range(tokens // tile):
        cut = slice(i * tile, (i + 1) * tile)
        du = (dot_nt(df_ref[cut, :], w2) * slope_ref[cut, :].astype(F32)).astype(BF)
        du_parts.append(du)
        dm_ref[cut, :] += dot_nt(du, w1)
    du = jnp.concatenate(du_parts, 0)
    bup_ref[...] = jnp.sum(du.astype(F32), 0, keepdims=True)
    wup_ref[...] = dot(mt[...], du).astype(BF)
    wdown_ref[...] = dot(dft[...], g_ref[...]).T.astype(BF)


def feed_back(m, df, g, slope, w1, wout, first, last, chunk=768, tile=512):
    tokens = m.shape[0]
    steps = (last - first) // chunk
    base = first // chunk
    return pl.pallas_call(
        partial(feed_back_kernel, tile=tile),
        grid=(steps,),
        in_specs=[
            whole((tokens, D)),
            whole((tokens, D)),
            pl.BlockSpec((tokens, chunk), lambda step: (0, step + base)),
            pl.BlockSpec((tokens, chunk), lambda step: (0, step + base)),
            pl.BlockSpec((D, chunk), lambda step: (0, step + base)),
            pl.BlockSpec((chunk, D), lambda step: (step + base + D // chunk, 0)),
        ],
        out_specs=[
            pl.BlockSpec((D, chunk), lambda step: (0, step)),
            pl.BlockSpec((chunk, D), lambda step: (step + base + D // chunk, 0)),
            pl.BlockSpec((1, chunk), lambda step: (0, step)),
            pl.BlockSpec((tokens, D), lambda step: (0, 0), pipeline_mode=pl.Buffered(1)),
        ],
        out_shape=[
            shape_of((D, last - first), BF),
            shape_of((D + FF, D), BF),
            shape_of((1, last - first), F32),
            shape_of((tokens, D), F32),
        ],
        scratch_shapes=[pltpu.VMEM((D, tokens), BF), pltpu.VMEM((D, tokens), BF)],
        compiler_params=pltpu.CompilerParams(vmem_limit_bytes=VMEM_LIMIT),
        name="feed_back",
    )(m, df, g, slope, w1, wout)


def middle_back_kernel(
    mid_ref, dm_ref, ds_ref, y_ref, o_ref, mod_ref, wproj_ref, gout_ref,
    dmid_ref, do_ref, dmod_ref, wproj_out_ref, bproj_ref, total, *, images
):
    step = pl.program_id(0)

    @pl.when(step == 0)
    def _():
        total[...] = jnp.zeros_like(total)
        bproj_ref[...] = jnp.zeros_like(bproj_ref)

    tokens = images * SEQ
    dy_parts = []
    for index in range(images):
        normed, inverse = norm_parts(mid_ref[index])
        dm = dm_ref[index]
        dmid = ds_ref[index] + norm_back(dm * (1.0 + mod_ref[index, :, D:]), normed, inverse)
        dmid_ref[index] = dmid
        dmod_ref[index, :, :D] = jnp.sum(dmid * y_ref[index].astype(F32), 0, keepdims=True)
        dmod_ref[index, :, D : 2 * D] = jnp.sum(dm, 0, keepdims=True)
        dmod_ref[index, :, 2 * D :] = jnp.sum(dm * normed, 0, keepdims=True)
        dy_parts.append((dmid * mod_ref[index, :, :D]).astype(BF))
    dy = jnp.concatenate(dy_parts, 0)
    bproj_ref[...] += jnp.sum(dy.astype(F32), 0, keepdims=True)
    do_ref[...] = dot_nt(dy, wproj_ref[...]).astype(BF).reshape(images, SEQ, D)
    total[...] += dot_tn(o_ref[...].reshape(tokens, D), dy)

    @pl.when(step == pl.num_programs(0) - 1)
    def _():
        wproj_out_ref[...] = total[...].astype(BF)


def middle_back(mid, dm, ds, y, o, mod, wout, gout, images=2):
    batch = mid.shape[0]
    return pl.pallas_call(
        partial(middle_back_kernel, images=images),
        grid=(batch // images,),
        in_specs=[
            rows(images, SEQ, D),
            rows(images, SEQ, D),
            rows(images, SEQ, D),
            rows(images, SEQ, D),
            rows(images, SEQ, D),
            rows(images, 1, 2 * D),
            whole((D, D)),
            pl.BlockSpec(memory_space=pl.ANY),
        ],
        out_specs=[
            rows(images, SEQ, D),
            rows(images, SEQ, D),
            rows(images, 1, 3 * D),
            fixed((D, D)),
            fixed((1, D)),
        ],
        out_shape=[
            shape_of((batch, SEQ, D), F32),
            shape_of((batch, SEQ, D), BF),
            shape_of((batch, 1, 3 * D), F32),
            shape_of((D + FF, D), BF),
            shape_of((1, D), F32),
        ],
        input_output_aliases={7: 3},
        scratch_shapes=[pltpu.VMEM((D, D), F32)],
        compiler_params=pltpu.CompilerParams(vmem_limit_bytes=VMEM_LIMIT),
        name="middle_back",
    )(mid, dm, ds, y, o, mod, wout, gout)


def attend_back_kernel(qkv_ref, do_ref, a_ref, dqkv_ref, wqkv_ref, bqkv_ref, total, *, images):
    step = pl.program_id(0)

    @pl.when(step == 0)
    def _():
        total[...] = jnp.zeros_like(total)
        bqkv_ref[...] = jnp.zeros_like(bqkv_ref)

    masks = head_masks()
    tokens = images * SEQ

    def image(index, carry):
        for pair in range(PAIRS):
            base = pair * PAIR
            queries = qkv_ref[index, :, base : base + PAIR] * jnp.asarray(HDIM**-0.5, BF)
            keys = qkv_ref[index, :, D + base : D + base + PAIR]
            values = qkv_ref[index, :, 2 * D + base : 2 * D + base + PAIR]
            grads = do_ref[index, :, base : base + PAIR]
            zeros = jnp.zeros_like(queries)
            dq, dk, dv = 0.0, 0.0, 0.0
            for mask in masks:
                part_q = jnp.where(mask, queries, zeros)
                part_g = jnp.where(mask, grads, zeros)
                part_k = jnp.where(mask, keys * jnp.asarray(HDIM**-0.5, BF), zeros)
                scores = dot_nt(keys, part_q)
                power = jnp.exp(scores - jnp.max(scores, 0, keepdims=True))
                prob = power * (1.0 / jnp.sum(power, 0, keepdims=True))
                dprob = dot_nt(values, part_g)
                delta = jnp.sum(prob * dprob, 0, keepdims=True)
                dscore = (prob * (dprob - delta)).astype(BF)
                dv = dv + dot(prob.astype(BF), part_g)
                dk = dk + dot(dscore, part_q)
                dq = dq + dot_tn(dscore, part_k)
            dqkv_ref[index, :, base : base + PAIR] = dq.astype(BF)
            dqkv_ref[index, :, D + base : D + base + PAIR] = dk.astype(BF)
            dqkv_ref[index, :, 2 * D + base : 2 * D + base + PAIR] = dv.astype(BF)
        return carry

    lax.fori_loop(0, images, image, 0)
    dqkv = dqkv_ref[...].reshape(tokens, 3 * D)
    total[...] += dot_tn(a_ref[...].reshape(tokens, D), dqkv)
    bqkv_ref[...] += jnp.sum(dqkv.astype(F32), 0, keepdims=True)

    @pl.when(step == pl.num_programs(0) - 1)
    def _():
        wqkv_ref[...] = total[...].astype(BF)


def attend_back(qkv, do, a, images=2):
    batch = qkv.shape[0]
    return pl.pallas_call(
        partial(attend_back_kernel, images=images),
        grid=(batch // images,),
        in_specs=[rows(images, SEQ, 3 * D), rows(images, SEQ, D), rows(images, SEQ, D)],
        out_specs=[rows(images, SEQ, 3 * D), fixed((D, 3 * D)), fixed((1, 3 * D))],
        out_shape=[
            shape_of((batch, SEQ, 3 * D), BF),
            shape_of((D, 3 * D), BF),
            shape_of((1, 3 * D), F32),
        ],
        scratch_shapes=[pltpu.VMEM((D, 3 * D), F32)],
        compiler_params=pltpu.CompilerParams(vmem_limit_bytes=VMEM_LIMIT),
        name="attend_back",
    )(qkv, do, a)


def stream_back_kernel(
    dqkv_ref, dmid_ref, noisy_ref, pos_ref, wpatch_ref, mod_ref, wqkv_ref,
    dmod_ref, wpatch_out_ref, bpatch_ref, *, images
):
    step = pl.program_id(0)

    @pl.when(step == 0)
    def _():
        wpatch_out_ref[...] = jnp.zeros_like(wpatch_out_ref)
        bpatch_ref[...] = jnp.zeros_like(bpatch_ref)

    tokens = images * SEQ
    da = dot_nt(dqkv_ref[...].reshape(tokens, 3 * D), wqkv_ref[...])
    for index in range(images):
        noisy = noisy_ref[index]
        stream = dot(noisy, wpatch_ref[...]) + pos_ref[...]
        normed, inverse = norm_parts(stream)
        part = da[index * SEQ : (index + 1) * SEQ]
        dmod_ref[index, :, :D] = jnp.sum(part, 0, keepdims=True)
        dmod_ref[index, :, D:] = jnp.sum(part * normed, 0, keepdims=True)
        dstream = dmid_ref[index] + norm_back(part * (1.0 + mod_ref[index]), normed, inverse)
        embedded = dstream.astype(BF)
        bpatch_ref[...] += jnp.sum(embedded.astype(F32), 0, keepdims=True)
        wpatch_out_ref[...] += dot_tn(noisy, embedded)


def stream_back(dqkv, dmid, noisy, pos, wpatch, mod, wqkv, images=2):
    batch = dqkv.shape[0]
    return pl.pallas_call(
        partial(stream_back_kernel, images=images),
        grid=(batch // images,),
        in_specs=[
            rows(images, SEQ, 3 * D),
            rows(images, SEQ, D),
            rows(images, SEQ, PATCH),
            whole((SEQ, D)),
            whole((PATCH, D)),
            rows(images, 1, D),
            whole((D, 3 * D)),
        ],
        out_specs=[rows(images, 1, 2 * D), fixed((PATCH, D)), fixed((1, D))],
        out_shape=[
            shape_of((batch, 1, 2 * D), F32),
            shape_of((PATCH, D), F32),
            shape_of((1, D), F32),
        ],
        compiler_params=pltpu.CompilerParams(vmem_limit_bytes=VMEM_LIMIT),
        name="stream_back",
    )(dqkv, dmid, noisy, pos, wpatch, mod, wqkv)


def spread(array_in, axis):
    count = lax.axis_size(axis)
    return lax.all_to_all(
        jnp.broadcast_to(array_in[None], (count,) + array_in.shape), axis, 0, 0, tiled=True
    )


def exchange(array_in, axis):
    return lax.all_to_all(array_in, axis, 0, 0, tiled=True)


def matmul(formula, left, right):
    return jnp.einsum(formula, left, right, preferred_element_type=F32)


def lower(array_in):
    return array_in.astype(BF)


def summed(array_in, axes):
    return jnp.sum(array_in.astype(F32), axes)


def position_table():
    quarter = D // 4
    angular = jnp.exp(-math.log(10000.0) * jnp.arange(quarter, dtype=F32) / quarter)
    position = jnp.arange(GRID * GRID, dtype=jnp.int32)
    column = (position % GRID).astype(F32)[:, None] * angular
    row_pos = (position // GRID).astype(F32)[:, None] * angular
    return jnp.concatenate(
        [jnp.sin(column), jnp.cos(column), jnp.sin(row_pos), jnp.cos(row_pos)], 1
    )


def time_features(moment):
    half_count = TFREQ // 2
    frequency = jnp.exp(-math.log(10000.0) * jnp.arange(half_count, dtype=F32) / half_count)
    angles = moment[:, None] * frequency
    return jnp.concatenate([jnp.cos(angles), jnp.sin(angles)], 1)


def pick_times(time_index, times):
    matches = time_index[:, None] == jnp.arange(times.shape[0], dtype=jnp.int32)[None, :]
    return jnp.sum(jnp.where(matches, times[None, :], 0.0), 1)


def adamw(weight, moment_one, moment_two, gradient, factor):
    gradient = gradient * factor
    moment_one = BETA_ONE * moment_one + (1.0 - BETA_ONE) * gradient
    moment_two = BETA_TWO * moment_two + (1.0 - BETA_TWO) * gradient * gradient
    fix_one = 1.0 - BETA_ONE**STEP
    fix_two = 1.0 - BETA_TWO**STEP
    update = (
        moment_one / fix_one / (jnp.sqrt(moment_two / fix_two) + EPS_ADAM) + WEIGHT_DECAY * weight
    )
    return (weight - LEARN_RATE * update, moment_one, moment_two)


def per_device(
    latents, noise, velocity, labels, time_index, times,
    in_mats, out_mats, embed_mats, class_table, final_ada, head_mat, bias_vec,
    in_mats_first, out_mats_first, embed_first, table_first, final_first, head_first, bias_first,
    in_mats_second, out_mats_second, embed_second, table_second, final_second, head_second, bias_second,
):
    shards = lax.axis_size("shard")
    groups = lax.axis_size("grp")
    me = lax.axis_index("shard")
    mine = lax.axis_index("grp")
    batch = latents.shape[0]
    width = embed_mats.shape[1]
    team = shards * batch

    in_low = lower(in_mats[0])
    wqkv = lax.all_gather(in_low[:, 6 * D : 9 * D], "shard", axis=0, tiled=True)
    wup = lax.all_gather(in_low[:, 9 * D :], "shard", axis=0, tiled=True)
    wout = lax.all_gather(lower(out_mats[0]), "shard", axis=0, tiled=True)
    embed_low = lower(embed_mats)
    table_low = lower(class_table)
    ada_low = jnp.concatenate([in_low[:, : 6 * D], lower(final_ada)], 1)

    marks = jnp.concatenate([time_index, labels])
    marks = jnp.concatenate([marks // 32, marks % 32]).astype(BF)
    early = PATCH + TFREQ
    message = jnp.concatenate([embed_low[:early].reshape(-1), lower(bias_vec), marks])
    arrived = spread(message, "shard")
    first_weights = (
        arrived[:, : early * width].reshape(shards, early, width).transpose(1, 0, 2).reshape(early, D)
    )
    wpatch = first_weights[:PATCH]
    wtime = first_weights[PATCH:]
    biases = arrived[:, early * width : early * width + bias_vec.shape[0]].reshape(-1).astype(F32)
    marks_team = arrived[:, early * width + bias_vec.shape[0] :].astype(jnp.int32)
    marks_team = marks_team[:, : 2 * batch] * 32 + marks_team[:, 2 * batch :]

    cond_bias = lax.dynamic_slice_in_dim(biases, 2 * D + me * width, width, 0)
    wtime_two = embed_low[early:]

    def condition_of(marks_in):
        index_in = marks_in[:, :batch].reshape(-1)
        labels_in = marks_in[:, batch:].reshape(-1)
        features = lower(time_features(pick_times(index_in, times)))
        time_pre = matmul("bf,fd->bd", features, wtime) + biases[D : 2 * D]
        time_act = lower(jax.nn.silu(time_pre))
        onehot = lower(
            (labels_in[:, None] == jnp.arange(NCLASS, dtype=jnp.int32)[None, :]).astype(F32)
        )
        condition = (
            matmul("bd,de->be", time_act, wtime_two)
            + cond_bias
            + matmul("bn,nd->bd", onehot, table_low)
        )
        return features, time_pre, time_act, onehot, condition

    condition = condition_of(marks_team)[4]
    cond_act = lower(jax.nn.silu(condition))
    moment = pick_times(time_index, times)

    def modulation_of(first, last):
        part = matmul("bd,de->be", cond_act, ada_low[:, first:last])
        return jnp.sum(exchange(part.reshape(shards, batch, last - first), "shard"), 0)

    offset = 3 * D
    final_base = 3 * D + 10 * D + FF
    mod_attn = modulation_of(0, 3 * D) + biases[offset : offset + 3 * D]
    mod_rest = modulation_of(3 * D, 8 * D) + jnp.concatenate(
        [biases[offset + 3 * D : offset + 6 * D], biases[final_base:]]
    )
    layer_bias = biases[offset + 6 * D : final_base]
    bqkv = jnp.concatenate([layer_bias[:D], jnp.zeros((D,), F32), layer_bias[D : 2 * D]])[None]

    noisy = lower((1.0 - moment)[:, None, None] * latents + moment[:, None, None] * noise)
    pos = position_table() + biases[:D]
    mod_attn = mod_attn[:, None, :]
    mod_rest = mod_rest[:, None, :]
    a, qkv, o = attend(noisy, pos, wpatch, mod_attn, wqkv, bqkv)
    count_all = float(groups * shards * batch * SEQ * OUT)
    mod_feed = jnp.concatenate([mod_attn[:, :, 2 * D :], mod_rest], 2)
    t_rows = jnp.broadcast_to(moment[:, None, None], (batch, SEQ, 1))
    head_low = lower(head_mat)
    mid, y, m, g, slope, df, ds, dmod_feed, whead, bhead, bdown, loss = feed(
        noisy, pos, wpatch, o, mod_feed, layer_bias[2 * D : 3 * D][None], wup,
        layer_bias[3 * D : 3 * D + FF][None], wout, layer_bias[3 * D + FF :][None],
        head_low[:D], head_low[D:].astype(F32), velocity, t_rows, count_all,
    )
    tokens = batch * SEQ
    gup, gout, bup, dm = feed_back(
        m.reshape(tokens, D), df.reshape(tokens, D), g, slope, wup, wout, 0, FF
    )
    gup = lax.psum_scatter(gup, "shard", scatter_dimension=0, tiled=True)
    mod_mid = jnp.concatenate([mod_attn[:, :, 2 * D :], mod_rest[:, :, D : 2 * D]], 2)
    dmid, do, dmod_mid, gout, bproj = middle_back(
        mid, dm.reshape(batch, SEQ, D), ds, y, o, mod_mid, wout, gout
    )
    gout = lax.psum_scatter(gout, "shard", scatter_dimension=0, tiled=True)
    dqkv, gqkv, bqkv_sum = attend_back(qkv, do, a)
    gqkv = lax.psum_scatter(gqkv, "shard", scatter_dimension=0, tiled=True)
    dmod_attn, gpatch, bpatch = stream_back(
        dqkv, dmid, noisy, pos, wpatch, mod_attn[:, :, D : 2 * D], wqkv
    )

    marks_all = spread(marks_team, "grp").reshape(groups * shards, 2 * batch)
    features, time_pre, time_act, onehot, condition = condition_of(marks_all)
    cond_act = lower(jax.nn.silu(condition))
    dmod_mid = dmod_mid[:, 0]
    dmod_feed = dmod_feed[:, 0]
    grad_rest = spread(spread(lower(jnp.concatenate([dmod_mid, dmod_feed], 1)), "shard"), "grp")
    grad_attn = spread(spread(lower(dmod_attn[:, 0]), "shard"), "grp")
    grad_rest = grad_rest.reshape(groups * team, 6 * D)
    grad_attn = grad_attn.reshape(groups * team, 2 * D)
    grad_ada = jnp.concatenate([grad_attn, grad_rest], 1)
    gada = matmul("bd,be->de", cond_act, grad_ada)
    bada = summed(grad_ada, (0,))
    grad_cond = matmul("be,de->bd", grad_ada, ada_low)
    unused, silu_pull = jax.vjp(jax.nn.silu, condition)
    grad_condition = lower(silu_pull(grad_cond)[0])
    gtable = matmul("bn,bd->nd", onehot, grad_condition)
    gtime_two = matmul("bd,be->de", time_act, grad_condition)
    btime_two = summed(grad_condition, (0,))
    own_condition = lax.dynamic_slice_in_dim(grad_condition, mine * team, team, 0)
    grad_act = matmul("be,de->bd", own_condition, wtime_two).reshape(team, shards, width)
    grad_act = jnp.sum(exchange(grad_act.transpose(1, 0, 2), "shard"), 0)
    own_pre = lax.dynamic_slice(time_pre, (mine * team, me * width), (team, width))
    unused, time_pull = jax.vjp(jax.nn.silu, own_pre)
    grad_time = spread(lower(time_pull(grad_act)[0]), "grp").reshape(groups * team, width)
    gtime_one = matmul("bf,bd->fd", features, grad_time)
    btime_one = summed(grad_time, (0,))
    btime = jnp.concatenate([btime_one, btime_two])

    head_part = jnp.concatenate(
        [whead.reshape(-1), bhead[0], bproj[0], bup[0], bdown[0], loss[0]]
    )
    head_part = jnp.sum(spread(head_part, "shard"), 0)
    head_part = jnp.sum(spread(head_part, "grp"), 0)
    late = jnp.concatenate(
        [
            gpatch.reshape(PATCH, shards, width).transpose(1, 0, 2).reshape(shards, -1),
            jnp.broadcast_to(
                jnp.concatenate([bpatch[0], bqkv_sum[0, :D], bqkv_sum[0, 2 * D :]]), (shards, 3 * D)
            ),
        ],
        1,
    )
    late = jnp.sum(exchange(late, "shard"), 0)
    late = jnp.sum(spread(late, "grp"), 0)
    gpatch = late[: PATCH * width].reshape(PATCH, width)
    late = late[PATCH * width :]
    head_grad = jnp.concatenate(
        [head_part[: D * OUT].reshape(OUT, D).T, head_part[D * OUT : D * OUT + OUT][None]], 0
    )
    head_part = head_part[D * OUT + OUT :]
    loss_sum = head_part[-1]
    bias_grad = jnp.concatenate(
        [
            late[:D],
            jnp.zeros((2 * D,), F32),
            bada[: 6 * D],
            late[D:],
            head_part[:-1],
            bada[6 * D :],
        ]
    )
    share = bias_vec.shape[0]
    bias_grad = lax.dynamic_slice_in_dim(bias_grad, me * share, share, 0)
    btime_all = spread(btime, "shard").reshape(shards, 2, width).transpose(1, 0, 2).reshape(-1)
    btime_all = jnp.concatenate([jnp.zeros((D,), F32), btime_all, jnp.zeros((12 * D + FF,), F32)])
    full_bias_grad = bias_grad + lax.dynamic_slice_in_dim(btime_all, me * share, share, 0)

    def over_groups(part):
        return summed(spread(part, "grp"), (0,))

    gqkv = over_groups(gqkv)
    gup = over_groups(gup)
    gout = over_groups(gout)
    squares = sum(
        jnp.sum(part * part)
        for part in (gada, gqkv, gup, gout, gpatch, gtime_one, gtime_two, gtable, bias_grad, btime)
    )
    total_squares = jnp.sum(spread(squares[None], "shard")) + jnp.sum(head_grad * head_grad)
    grad_norm = jnp.sqrt(total_squares)
    factor = CLIP_NORM / jnp.maximum(grad_norm, CLIP_NORM)
    grads = (
        jnp.concatenate([gada[:, : 6 * D], gqkv, gup], 1)[None],
        gout[None],
        jnp.concatenate([gpatch, gtime_one, gtime_two], 0),
        gtable,
        gada[:, 6 * D :],
        head_grad,
        full_bias_grad,
    )
    weights = (in_mats, out_mats, embed_mats, class_table, final_ada, head_mat, bias_vec)
    firsts = (in_mats_first, out_mats_first, embed_first, table_first, final_first, head_first, bias_first)
    seconds = (
        in_mats_second, out_mats_second, embed_second, table_second, final_second, head_second, bias_second
    )
    stepped = [
        adamw(weight, moment_one, moment_two, gradient, factor)
        for weight, moment_one, moment_two, gradient in zip(weights, firsts, seconds, grads)
    ]
    return tuple(part[0] for part in stepped) + tuple(part[1] for part in stepped) + tuple(
        part[2] for part in stepped
    ) + (loss_sum, grad_norm)


def solution(mesh):
    images = P(("grp", "shard"))
    placed = (
        P(None, "shard", None),
        P(None, "shard", None),
        P(None, "shard"),
        P(None, "shard"),
        P("shard", None),
        P(),
        P("shard"),
    )
    return jax.shard_map(
        per_device,
        mesh=mesh,
        in_specs=(images,) * 5 + (P(),) + placed * 3,
        out_specs=placed * 3 + (P(), P()),
        check_vma=False,
    )
```

```python
import math
from functools import partial
import jax
import jax.numpy as jnp
from jax import lax
from jax.sharding import PartitionSpec as P
from jax.experimental import pallas as pl
from jax.experimental.pallas import tpu as pltpu

D = 768
HEADS = 12
HDIM = 64
FF = 3072
PATCH = 16
SEQ = 256
OUT = 32
GRID = 16
STEP = 10
BETA_ONE = 0.9
BETA_TWO = 0.999
LEARN_RATE = 0.05
WEIGHT_DECAY = 0.05
EPS_ADAM = 1e-08
CLIP_NORM = 0.01
TFREQ = 256
NCLASS = 1001
EPS_NORM = 1e-06
BF = jnp.bfloat16
F32 = jnp.float32
VMEM_LIMIT = 60 * 1024 * 1024
COST = 3 * 10**8
PAIR = 2 * HDIM
PAIRS = HEADS // 2
BIASES = 19
B_PATCH, B_TIME, B_CLASS, B_ADA, B_QUERY, B_VALUE, B_PROJ, B_UP, B_DOWN, B_FINAL = 0, 1, 2, 3, 9, 10, 11, 12, 16, 17


def dot(left, right):
    return jnp.dot(left, right, preferred_element_type=F32)


def dot_nt(left, right):
    return lax.dot_general(left, right, (((1,), (1,)), ((), ())), preferred_element_type=F32)


def dot_tn(left, right):
    return lax.dot_general(left, right, (((0,), (0,)), ((), ())), preferred_element_type=F32)


def whole(shape):
    zeros = (0,) * len(shape)
    return pl.BlockSpec(shape, lambda step: zeros, pipeline_mode=pl.Buffered(1))


def fixed(shape):
    zeros = (0,) * len(shape)
    return pl.BlockSpec(shape, lambda step: zeros)


def rows(count, *rest):
    zeros = (0,) * len(rest)
    return pl.BlockSpec((count,) + rest, lambda step: (step,) + zeros)


def shape_of(shape, dtype):
    return jax.ShapeDtypeStruct(shape, dtype)


def norm_parts(array_in):
    centre = array_in - jnp.mean(array_in, -1, keepdims=True)
    inverse = lax.rsqrt(jnp.mean(centre * centre, -1, keepdims=True) + EPS_NORM)
    return centre * inverse, inverse


def norm_back(grad_normed, normed, inverse):
    first = jnp.mean(grad_normed, -1, keepdims=True)
    second = jnp.mean(grad_normed * normed, -1, keepdims=True)
    return inverse * (grad_normed - first - normed * second)


def cost(microseconds):
    return pl.CostEstimate(flops=microseconds * COST, bytes_accessed=0, transcendentals=0)


def head_masks():
    lane = lax.broadcasted_iota(jnp.int32, (1, PAIR), 1)
    return (lane < HDIM, lane >= HDIM)


def weight_copies(spot_ref, pieces, target, sem):
    if len(pieces) == 1:
        return [(None, pltpu.make_async_copy(pieces[0], target, sem))]
    own, near, far1, far2, far3, pair, other = pieces
    shard, group = spot_ref[0], spot_ref[1]
    quarter = near.shape[1]
    rest = target.shape[1] - 3 * quarter
    made = [
        (None, pltpu.make_async_copy(own, target.at[shard], sem)),
        (None, pltpu.make_async_copy(pair, target.at[shard ^ 1], sem)),
    ]
    for step, part in enumerate((near, far1, far2, far3)):
        block = group ^ step
        start = pl.multiple_of(block * quarter, quarter)
        for core in range(2):
            for hop in range(3):
                slot = shard ^ (2 * hop + 2 + core)
                source = other.at[3 * step + hop] if core else part.at[hop]
                whole_copy = pltpu.make_async_copy(source, target.at[slot, pl.ds(start, quarter)], sem)
                if rest == quarter:
                    made.append((None, whole_copy))
                else:
                    last = pltpu.make_async_copy(
                        source.at[quarter - rest :], target.at[slot, 3 * quarter :], sem
                    )
                    made.append((block != 3, whole_copy))
                    made.append((block == 3, last))
    return made


def run_copies(made, start):
    for condition, copy in made:
        if condition is None:
            copy.start() if start else copy.wait()
        else:

            @pl.when(condition)
            def _():
                copy.start() if start else copy.wait()


def part_of(weights, part, count):
    width = weights.shape[1] // count
    return weights[:, part * width : (part + 1) * width, :].reshape(D, D)


def attend_kernel(
    spot_ref, noisy_ref, pos_ref, wpatch_ref, mod_ref, bias_ref, *refs, images
):
    pieces, (a_ref, qkv_ref, o_ref, kept_ref, wqkv_ref, sem, out_sem) = refs[:-7], refs[-7:]
    step = pl.program_id(0)
    made = weight_copies(spot_ref, pieces, wqkv_ref, sem)
    keep = pltpu.make_async_copy(wqkv_ref, kept_ref, out_sem)

    @pl.when(step == 0)
    def _():
        run_copies(made, True)
        run_copies(made, False)
        keep.start()

    @pl.when(step == pl.num_programs(0) - 1)
    def _():
        keep.wait()

    masks = head_masks()

    def bias(row):
        return bias_ref[row : row + 1, :]

    def image(index, carry):
        stream = dot(noisy_ref[index], wpatch_ref[...]) + (pos_ref[...] + bias(B_PATCH))
        normed, unused = norm_parts(stream)
        scale = 1.0 + (mod_ref[index, :, D : 2 * D] + bias(B_ADA + 1))
        a = (normed * scale + (mod_ref[index, :, :D] + bias(B_ADA))).astype(BF)
        a_ref[index] = a
        for part in range(3):
            cut = slice(part * D, (part + 1) * D)
            product = dot(a, part_of(wqkv_ref, part, 3))
            if part != 1:
                product = product + bias(B_QUERY if part == 0 else B_VALUE)
            qkv_ref[index, :, cut] = product.astype(BF)
        for pair in range(PAIRS):
            base = pair * PAIR
            queries = qkv_ref[index, :, base : base + PAIR]
            keys = qkv_ref[index, :, D + base : D + base + PAIR]
            values = qkv_ref[index, :, 2 * D + base : 2 * D + base + PAIR]
            mixed = []
            for mask in masks:
                part = jnp.where(mask, queries * jnp.asarray(HDIM**-0.5, BF), jnp.zeros_like(queries))
                scores = dot_nt(part, keys)
                power = jnp.exp(scores - jnp.max(scores, -1, keepdims=True))
                total = jnp.sum(power, -1, keepdims=True)
                prob = (power * (1.0 / total)).astype(BF)
                mixed.append(dot(prob, values))
            o_ref[index, :, base : base + PAIR] = jnp.where(masks[0], mixed[0], mixed[1]).astype(BF)
        return carry

    lax.fori_loop(0, images, image, 0)


ANYWHERE = pl.BlockSpec(memory_space=pl.ANY)


def attend(spot, noisy, pos, wpatch, mod, bias, pieces, shards, images=2):
    batch = noisy.shape[0]
    kept = (shards, 3 * D // shards, D)
    return pl.pallas_call(
        partial(attend_kernel, images=images),
        grid=(batch // images,),
        in_specs=[
            pl.BlockSpec(memory_space=pltpu.SMEM),
            rows(images, SEQ, PATCH),
            whole((SEQ, D)),
            whole((PATCH, D)),
            rows(images, 1, 3 * D),
            whole((BIASES, D)),
        ]
        + [ANYWHERE] * len(pieces),
        out_specs=[rows(images, SEQ, D), rows(images, SEQ, 3 * D), rows(images, SEQ, D), ANYWHERE],
        out_shape=[
            shape_of((batch, SEQ, D), BF),
            shape_of((batch, SEQ, 3 * D), BF),
            shape_of((batch, SEQ, D), BF),
            shape_of(kept, BF),
        ],
        scratch_shapes=[pltpu.VMEM(kept, BF), pltpu.SemaphoreType.DMA, pltpu.SemaphoreType.DMA],
        compiler_params=pltpu.CompilerParams(vmem_limit_bytes=VMEM_LIMIT),
        name="attend",
        cost_estimate=cost(32),
    )(spot, noisy, pos, wpatch, mod, bias, *pieces)


GELU_A = math.sqrt(2.0 / math.pi)
GELU_B = 0.044715


def gelu_both(u):
    square = u * u
    turn = jnp.tanh(u * (GELU_A + (GELU_A * GELU_B) * square))
    half = 0.5 + 0.5 * turn
    slope = half + (0.5 * u) * (1.0 - turn * turn) * (GELU_A + (3.0 * GELU_A * GELU_B) * square)
    return u * half, slope


def feed_kernel(
    spot_ref, t_ref, noisy_ref, pos_ref, wpatch_ref, o_ref, gate_ref, mod_ref, bias_ref,
    head_ref, hbias_ref, vel_ref, *refs, images, count_all
):
    pieces, refs = refs[:-18], refs[-18:]
    mid_ref, y_ref, m_ref, g_ref, slope_ref, df_ref, ds_ref, dmod_ref, near_ref, far_ref, bdown_ref = refs[:11]
    kept1_ref, kept2_ref, weights_ref, tail_ref, order, sem, out_sem = refs[11:]
    step = pl.program_id(0)
    made = weight_copies(spot_ref, pieces, weights_ref, sem)
    up_width, out_width = kept1_ref.shape[1], kept2_ref.shape[1]
    keeps = [
        pltpu.make_async_copy(weights_ref.at[:, :up_width], kept1_ref, out_sem.at[0]),
        pltpu.make_async_copy(weights_ref.at[:, up_width:], kept2_ref, out_sem.at[1]),
    ]

    @pl.when(step == 0)
    def _():
        run_copies(made, True)
        run_copies(made, False)
        for keep in keeps:
            keep.start()

    @pl.when(step == pl.num_programs(0) - 1)
    def _():
        for keep in keeps:
            keep.wait()

    @pl.when(step == 0)
    def _():
        tail_ref[...] = jnp.zeros_like(tail_ref)
        bdown_ref[...] = jnp.zeros_like(bdown_ref)

    tokens = images * SEQ

    def bias(row):
        return bias_ref[row : row + 1, :]

    def spread(part):
        parts = []
        for index in range(images):
            if part == 0:
                row = gate_ref[index, :, 2 * D :] + bias(B_ADA + 2)
            else:
                row = mod_ref[index, :, (part - 1) * D : part * D]
                row = row + bias(B_ADA + 2 + part if part < 4 else B_FINAL + part - 4)
            parts.append(jnp.broadcast_to(row, (SEQ, D)))
        return jnp.concatenate(parts, 0)

    def up_part(part):
        rows_of = up_width * D // FF
        return weights_ref[:, part * rows_of : (part + 1) * rows_of, :].reshape(D, D)

    def out_rows(part):
        first, taken = part * D, []
        while first < (part + 1) * D:
            place_of, row = first // out_width, first % out_width
            count = min(out_width - row, (part + 1) * D - first)
            taken.append(weights_ref[place_of, up_width + row : up_width + row + count, :])
            first += count
        return jnp.concatenate(taken, 0)

    position = jnp.concatenate([pos_ref[...] + bias(B_PATCH)] * images, 0)
    stream = dot(noisy_ref[...].reshape(tokens, PATCH), wpatch_ref[...]) + position
    y = dot(o_ref[...].reshape(tokens, D), out_rows(0)) + bias(B_PROJ)
    y_ref[...] = y.astype(BF).reshape(images, SEQ, D)
    mid = stream + spread(0) * y
    mid_ref[...] = mid.reshape(images, SEQ, D)
    normed, unused = norm_parts(mid)
    m = (normed * (1.0 + spread(2)) + spread(1)).astype(BF)
    m_ref[...] = m.reshape(images, SEQ, D)
    feed = jnp.broadcast_to(bias(B_DOWN), (tokens, D))
    for j in range(FF // D):
        cut = slice(j * D, (j + 1) * D)
        g, slope = gelu_both(dot(m, up_part(j)) + bias(B_UP + j))
        g = g.astype(BF)
        g_ref[:, cut] = g
        slope_ref[:, cut] = slope.astype(BF)
        feed = feed + dot(g, out_rows(j + 1))
    gate = spread(3)
    stream = mid + gate * feed
    normed, inverse = norm_parts(stream)
    scale = 1.0 + spread(5)
    z = (normed * scale + spread(4)).astype(BF)
    predicted = dot(z, head_ref[...]) + hbias_ref[...]
    t = jnp.concatenate(
        [jnp.full((SEQ, 1), t_ref[step * images + index], F32) for index in range(images)], 0
    )
    residual = predicted - vel_ref[...].reshape(tokens, OUT)
    weighted = t * residual
    loss = jnp.sum(jnp.sum(weighted * residual, 0, keepdims=True), 1, keepdims=True)
    tail_ref[OUT + 1 : OUT + 2, :] += jnp.broadcast_to(loss, (1, D))
    grad_pred = (2.0 * weighted / count_all).astype(BF)
    tail_ref[OUT : OUT + 1, :OUT] += jnp.sum(grad_pred.astype(F32), 0, keepdims=True)
    tail_ref[:OUT, :] += dot_tn(grad_pred, z)
    dz = dot_nt(grad_pred, head_ref[...])
    ds = norm_back(dz * scale, normed, inverse)
    ds_ref[...] = ds.reshape(images, SEQ, D)
    df = (ds * gate).astype(BF)
    df_ref[...] = df.reshape(images, SEQ, D)
    bdown_ref[...] += jnp.sum(df.astype(F32), 0, keepdims=True)
    for index in range(images):
        cut = slice(index * SEQ, (index + 1) * SEQ)
        dmod_ref[index, :, :D] = jnp.sum(ds[cut] * feed[cut], 0, keepdims=True)
        dmod_ref[index, :, D : 2 * D] = jnp.sum(dz[cut], 0, keepdims=True)
        dmod_ref[index, :, 2 * D :] = jnp.sum(dz[cut] * normed[cut], 0, keepdims=True)

    shards, taken = 2 * near_ref.shape[0], near_ref.shape[1]

    @pl.when(step == pl.num_programs(0) - 1)
    def _():
        for place_of in range(shards):
            order[place_of] = tail_ref[place_of * taken : (place_of + 1) * taken, :]
        for entry in range(shards):
            (far_ref if entry % 2 else near_ref)[entry // 2] = order[spot_ref[0] ^ entry]


def tail_rows(shards):
    return -(-(OUT + 2) // shards)


def feed(spot, t, noisy, pos, wpatch, o, gate, mod, bias, head, hbias, velocity, pieces, shards, count_all, images=2):
    batch = o.shape[0]
    kept1 = (shards, FF // shards, D)
    kept2 = (shards, (D + FF) // shards, D)
    half = (shards // 2, tail_rows(shards), D)
    tokens = batch * SEQ
    return pl.pallas_call(
        partial(feed_kernel, images=images, count_all=count_all),
        grid=(batch // images,),
        in_specs=[
            pl.BlockSpec(memory_space=pltpu.SMEM),
            pl.BlockSpec(memory_space=pltpu.SMEM),
            rows(images, SEQ, PATCH),
            whole((SEQ, D)),
            whole((PATCH, D)),
            rows(images, SEQ, D),
            rows(images, 1, 3 * D),
            rows(images, 1, 5 * D),
            whole((BIASES, D)),
            whole((D, OUT)),
            whole((1, OUT)),
            rows(images, SEQ, OUT),
        ]
        + [ANYWHERE] * len(pieces),
        out_specs=[
            rows(images, SEQ, D),
            rows(images, SEQ, D),
            rows(images, SEQ, D),
            rows(images * SEQ, FF),
            rows(images * SEQ, FF),
            rows(images, SEQ, D),
            rows(images, SEQ, D),
            rows(images, 1, 3 * D),
            fixed(half),
            fixed(half),
            fixed((1, D)),
            ANYWHERE,
            ANYWHERE,
        ],
        out_shape=[
            shape_of((batch, SEQ, D), F32),
            shape_of((batch, SEQ, D), BF),
            shape_of((batch, SEQ, D), BF),
            shape_of((tokens, FF), BF),
            shape_of((tokens, FF), BF),
            shape_of((batch, SEQ, D), BF),
            shape_of((batch, SEQ, D), F32),
            shape_of((batch, 1, 3 * D), F32),
            shape_of(half, F32),
            shape_of(half, F32),
            shape_of((1, D), F32),
            shape_of(kept1, BF),
            shape_of(kept2, BF),
        ],
        scratch_shapes=[
            pltpu.VMEM((shards, kept1[1] + kept2[1], D), BF),
            pltpu.VMEM((shards * half[1], D), F32),
            pltpu.VMEM((shards,) + half[1:], F32),
            pltpu.SemaphoreType.DMA,
            pltpu.SemaphoreType.DMA((2,)),
        ],
        compiler_params=pltpu.CompilerParams(vmem_limit_bytes=VMEM_LIMIT),
        name="feed",
        cost_estimate=cost(52),
    )(spot, t, noisy, pos, wpatch, o, gate, mod, bias, head, hbias, velocity, *pieces)


def feed_back_kernel(
    m_ref, df_ref, g_ref, slope_ref, w1_ref, w2_ref, wup_ref, wdown_ref, bup_ref, dm_ref, mt, dft, *, tile
):
    step = pl.program_id(0)

    @pl.when(step == 0)
    def _():
        mt[...] = m_ref[...].T
        dft[...] = df_ref[...].T
        dm_ref[...] = jnp.zeros_like(dm_ref)

    tokens = m_ref.shape[0]
    w1 = w1_ref[...].reshape(D, D)
    w2 = w2_ref[...]
    du_parts = []
    for i in range(tokens // tile):
        cut = slice(i * tile, (i + 1) * tile)
        du = (dot_nt(df_ref[cut, :], w2) * slope_ref[cut, :].astype(F32)).astype(BF)
        du_parts.append(du)
        dm_ref[cut, :] += dot_nt(du, w1)
    du = jnp.concatenate(du_parts, 0)
    bup_ref[...] = jnp.sum(du.astype(F32), 0, keepdims=True)
    wup_ref[...] = dot(mt[...], du).astype(BF).reshape(wup_ref.shape)
    wdown_ref[...] = dot(dft[...], g_ref[...]).T.astype(BF)


def feed_back(m, df, g, slope, w1, wout, first, last, tile=512):
    chunk = D
    shards = w1.shape[0]
    rows_of = D // shards
    tokens = m.shape[0]
    steps = (last - first) // chunk
    base = first // chunk
    return pl.pallas_call(
        partial(feed_back_kernel, tile=tile),
        grid=(steps,),
        in_specs=[
            whole((tokens, D)),
            whole((tokens, D)),
            pl.BlockSpec((tokens, chunk), lambda step: (0, step + base)),
            pl.BlockSpec((tokens, chunk), lambda step: (0, step + base)),
            pl.BlockSpec((shards, rows_of, D), lambda step: (0, step + base, 0)),
            pl.BlockSpec((chunk, D), lambda step: (step + base + D // chunk, 0)),
        ],
        out_specs=[
            pl.BlockSpec((shards, rows_of, D), lambda step: (0, step, 0)),
            pl.BlockSpec((chunk, D), lambda step: (step + base + D // chunk, 0)),
            pl.BlockSpec((1, chunk), lambda step: (0, step)),
            pl.BlockSpec((tokens, D), lambda step: (0, 0), pipeline_mode=pl.Buffered(1)),
        ],
        out_shape=[
            shape_of((shards, steps * rows_of, D), BF),
            shape_of((D + FF, D), BF),
            shape_of((1, last - first), F32),
            shape_of((tokens, D), F32),
        ],
        scratch_shapes=[pltpu.VMEM((D, tokens), BF), pltpu.VMEM((D, tokens), BF)],
        compiler_params=pltpu.CompilerParams(vmem_limit_bytes=VMEM_LIMIT),
        name="feed_back",
        cost_estimate=cost(51),
    )(m, df, g, slope, w1, wout)


def middle_back_kernel(
    mid_ref, dm_ref, ds_ref, y_ref, o_ref, gate_ref, mod_ref, bias_ref, wproj_ref, gout_ref,
    dmid_ref, do_ref, dmod_ref, wproj_out_ref, bproj_ref, total, *, images
):
    step = pl.program_id(0)

    @pl.when(step == 0)
    def _():
        total[...] = jnp.zeros_like(total)
        bproj_ref[...] = jnp.zeros_like(bproj_ref)

    tokens = images * SEQ
    dy_parts = []
    for index in range(images):
        normed, inverse = norm_parts(mid_ref[index])
        dm = dm_ref[index]
        dmid = ds_ref[index] + norm_back(
            dm * (1.0 + (mod_ref[index, :, D : 2 * D] + bias_ref[B_ADA + 4 : B_ADA + 5, :])), normed, inverse
        )
        dmid_ref[index] = dmid
        dmod_ref[index, :, :D] = jnp.sum(dmid * y_ref[index].astype(F32), 0, keepdims=True)
        dmod_ref[index, :, D : 2 * D] = jnp.sum(dm, 0, keepdims=True)
        dmod_ref[index, :, 2 * D :] = jnp.sum(dm * normed, 0, keepdims=True)
        gate = gate_ref[index, :, 2 * D :] + bias_ref[B_ADA + 2 : B_ADA + 3, :]
        dy_parts.append((dmid * gate).astype(BF))
    dy = jnp.concatenate(dy_parts, 0)
    bproj_ref[...] += jnp.sum(dy.astype(F32), 0, keepdims=True)
    do_ref[...] = dot_nt(dy, wproj_ref[...]).astype(BF).reshape(images, SEQ, D)
    total[...] += dot_tn(o_ref[...].reshape(tokens, D), dy)

    @pl.when(step == pl.num_programs(0) - 1)
    def _():
        wproj_out_ref[...] = total[...].astype(BF)


def middle_back(mid, dm, ds, y, o, gate, mod, bias, wout, gout, images=2):
    batch = mid.shape[0]
    return pl.pallas_call(
        partial(middle_back_kernel, images=images),
        grid=(batch // images,),
        in_specs=[
            rows(images, SEQ, D),
            rows(images, SEQ, D),
            rows(images, SEQ, D),
            rows(images, SEQ, D),
            rows(images, SEQ, D),
            rows(images, 1, 3 * D),
            rows(images, 1, 5 * D),
            whole((BIASES, D)),
            whole((D, D)),
            pl.BlockSpec(memory_space=pl.ANY),
        ],
        out_specs=[
            rows(images, SEQ, D),
            rows(images, SEQ, D),
            rows(images, 1, 3 * D),
            fixed((D, D)),
            fixed((1, D)),
        ],
        out_shape=[
            shape_of((batch, SEQ, D), F32),
            shape_of((batch, SEQ, D), BF),
            shape_of((batch, 1, 3 * D), F32),
            shape_of((D + FF, D), BF),
            shape_of((1, D), F32),
        ],
        input_output_aliases={9: 3},
        scratch_shapes=[pltpu.VMEM((D, D), F32)],
        compiler_params=pltpu.CompilerParams(vmem_limit_bytes=VMEM_LIMIT),
        name="middle_back",
        cost_estimate=cost(18),
    )(mid, dm, ds, y, o, gate, mod, bias, wout, gout)


def attend_back_kernel(qkv_ref, do_ref, a_ref, dqkv_ref, wqkv_ref, bqkv_ref, total, *, images):
    step = pl.program_id(0)

    @pl.when(step == 0)
    def _():
        total[...] = jnp.zeros_like(total)
        bqkv_ref[...] = jnp.zeros_like(bqkv_ref)

    masks = head_masks()
    tokens = images * SEQ

    def image(index, carry):
        for pair in range(PAIRS):
            base = pair * PAIR
            queries = qkv_ref[index, :, base : base + PAIR] * jnp.asarray(HDIM**-0.5, BF)
            keys = qkv_ref[index, :, D + base : D + base + PAIR]
            values = qkv_ref[index, :, 2 * D + base : 2 * D + base + PAIR]
            grads = do_ref[index, :, base : base + PAIR]
            zeros = jnp.zeros_like(queries)
            dq, dk, dv = 0.0, 0.0, 0.0
            for mask in masks:
                part_q = jnp.where(mask, queries, zeros)
                part_g = jnp.where(mask, grads, zeros)
                part_k = jnp.where(mask, keys * jnp.asarray(HDIM**-0.5, BF), zeros)
                scores = dot_nt(keys, part_q)
                power = jnp.exp(scores - jnp.max(scores, 0, keepdims=True))
                prob = power * (1.0 / jnp.sum(power, 0, keepdims=True))
                dprob = dot_nt(values, part_g)
                delta = jnp.sum(prob * dprob, 0, keepdims=True)
                dscore = (prob * (dprob - delta)).astype(BF)
                dv = dv + dot(prob.astype(BF), part_g)
                dk = dk + dot(dscore, part_q)
                dq = dq + dot_tn(dscore, part_k)
            dqkv_ref[index, :, base : base + PAIR] = dq.astype(BF)
            dqkv_ref[index, :, D + base : D + base + PAIR] = dk.astype(BF)
            dqkv_ref[index, :, 2 * D + base : 2 * D + base + PAIR] = dv.astype(BF)
        return carry

    lax.fori_loop(0, images, image, 0)
    dqkv = dqkv_ref[...].reshape(tokens, 3 * D)
    total[...] += dot_tn(a_ref[...].reshape(tokens, D), dqkv)
    bqkv_ref[...] += jnp.sum(dqkv.astype(F32), 0, keepdims=True)

    @pl.when(step == pl.num_programs(0) - 1)
    def _():
        for part in range(3):
            width = wqkv_ref.shape[1] // 3
            wqkv_ref[:, part * width : (part + 1) * width, :] = (
                total[:, part * D : (part + 1) * D].astype(BF).reshape(wqkv_ref.shape[0], width, D)
            )


def attend_back(qkv, do, a, shards, images=2):
    batch = qkv.shape[0]
    return pl.pallas_call(
        partial(attend_back_kernel, images=images),
        grid=(batch // images,),
        in_specs=[rows(images, SEQ, 3 * D), rows(images, SEQ, D), rows(images, SEQ, D)],
        out_specs=[rows(images, SEQ, 3 * D), fixed((shards, 3 * D // shards, D)), fixed((1, 3 * D))],
        out_shape=[
            shape_of((batch, SEQ, 3 * D), BF),
            shape_of((shards, 3 * D // shards, D), BF),
            shape_of((1, 3 * D), F32),
        ],
        scratch_shapes=[pltpu.VMEM((D, 3 * D), F32)],
        compiler_params=pltpu.CompilerParams(vmem_limit_bytes=VMEM_LIMIT),
        name="attend_back",
        cost_estimate=cost(45),
    )(qkv, do, a)


def stream_back_kernel(
    spot_ref, dqkv_ref, dmid_ref, noisy_ref, pos_ref, wpatch_ref, mod_ref, bias_ref, wqkv_ref,
    dmod_ref, near_ref, far_ref, bpatch_ref, wpatch_out_ref, order, *, images
):
    step = pl.program_id(0)

    @pl.when(step == 0)
    def _():
        wpatch_out_ref[...] = jnp.zeros_like(wpatch_out_ref)
        bpatch_ref[...] = jnp.zeros_like(bpatch_ref)

    tokens = images * SEQ
    dqkv = dqkv_ref[...].reshape(tokens, 3 * D)
    da = sum(dot_nt(dqkv[:, part * D : (part + 1) * D], part_of(wqkv_ref, part, 3)) for part in range(3))
    for index in range(images):
        noisy = noisy_ref[index]
        stream = dot(noisy, wpatch_ref[...]) + (pos_ref[...] + bias_ref[B_PATCH : B_PATCH + 1, :])
        scale = 1.0 + (mod_ref[index, :, D : 2 * D] + bias_ref[B_ADA + 1 : B_ADA + 2, :])
        normed, inverse = norm_parts(stream)
        part = da[index * SEQ : (index + 1) * SEQ]
        dmod_ref[index, :, :D] = jnp.sum(part, 0, keepdims=True)
        dmod_ref[index, :, D:] = jnp.sum(part * normed, 0, keepdims=True)
        dstream = dmid_ref[index] + norm_back(part * scale, normed, inverse)
        embedded = dstream.astype(BF)
        bpatch_ref[...] += jnp.sum(embedded.astype(F32), 0, keepdims=True)
        wpatch_out_ref[...] += dot_tn(noisy, embedded)

    width = near_ref.shape[2]
    shards = D // width

    @pl.when(step == pl.num_programs(0) - 1)
    def _():
        for place_of in range(shards):
            order[place_of] = wpatch_out_ref[:, place_of * width : (place_of + 1) * width]
        for entry in range(shards):
            (far_ref if entry % 2 else near_ref)[entry // 2] = order[spot_ref[0] ^ entry]


def stream_back(spot, dqkv, dmid, noisy, pos, wpatch, mod, bias, wqkv, images=2):
    batch = dqkv.shape[0]
    half = (wqkv.shape[0] // 2, PATCH, D // wqkv.shape[0])
    return pl.pallas_call(
        partial(stream_back_kernel, images=images),
        grid=(batch // images,),
        in_specs=[
            pl.BlockSpec(memory_space=pltpu.SMEM),
            rows(images, SEQ, 3 * D),
            rows(images, SEQ, D),
            rows(images, SEQ, PATCH),
            whole((SEQ, D)),
            whole((PATCH, D)),
            rows(images, 1, 3 * D),
            whole((BIASES, D)),
            whole(wqkv.shape),
        ],
        out_specs=[rows(images, 1, 2 * D), fixed(half), fixed(half), fixed((1, D))],
        out_shape=[
            shape_of((batch, 1, 2 * D), F32),
            shape_of(half, F32),
            shape_of(half, F32),
            shape_of((1, D), F32),
        ],
        scratch_shapes=[pltpu.VMEM((PATCH, D), F32), pltpu.VMEM((2 * half[0],) + half[1:], F32)],
        compiler_params=pltpu.CompilerParams(vmem_limit_bytes=VMEM_LIMIT),
        name="stream_back",
        cost_estimate=cost(19),
    )(spot, dqkv, dmid, noisy, pos, wpatch, mod, bias, wqkv)


MARKS = 4
PATCH_ROW = TFREQ
BIAS_ROW = TFREQ + PATCH
MESSAGE = 304


def condition_kernel(spot_ref, near_ref, other_ref, times_ref, embed_ref, table_ref, *rest, team):
    me = spot_ref[0]
    width = embed_ref.shape[1]
    shards = D // width
    messages = [(other_ref if entry % 2 else near_ref).at[entry // 2] for entry in range(shards)]
    if team:
        in_ref, final_ref, time_pre_ref, condition_ref, marks_ref, wpatch_ref, bias_ref = rest[:7]
        near1_ref, far1_ref, near2_ref, far2_ref, table, bias_rows, order = rest[7:]
        batch = near1_ref.shape[1]
        marks = jnp.concatenate(
            [message[:batch, width : width + MARKS].astype(F32) for message in messages], 0
        )
        marks_ref[...] = marks
    else:
        groups_marks, (marks_ref, features_ref, time_act_ref, act_ref, table, bias_rows, order) = rest[:-7], rest[-7:]
        team_count = groups_marks[0].shape[0]
        for entry, part in enumerate(groups_marks):
            start = pl.multiple_of((spot_ref[1] ^ entry) * team_count, team_count)
            marks_ref[pl.ds(start, team_count), :] = part[...]
        marks = marks_ref[...]
    count = marks.shape[0]
    marks = marks.astype(jnp.int32)
    index = marks[:, 0:1] * 32 + marks[:, 1:2]
    label = marks[:, 2:3] * 32 + marks[:, 3:4]

    for entry in range(shards):
        bias_rows[me ^ entry] = messages[entry][BIAS_ROW : BIAS_ROW + BIASES, :width].astype(F32)
        if team:
            order[me ^ entry] = messages[entry][PATCH_ROW : PATCH_ROW + PATCH, :width]

    def bias_row(row):
        return bias_rows[lax.div(row, BIASES), pl.ds(lax.rem(row, BIASES), 1), :]

    entry = lax.broadcasted_iota(jnp.int32, (count, times_ref.shape[1]), 1)
    moment = jnp.sum(jnp.where(entry == index, times_ref[...], 0.0), 1, keepdims=True)
    half = TFREQ // 2
    frequency = lax.broadcasted_iota(jnp.int32, (1, half), 1).astype(F32)
    angles = moment * jnp.exp(-math.log(10000.0) * frequency / half)
    features = jnp.concatenate([jnp.cos(angles), jnp.sin(angles)], 1).astype(BF)
    table[...] = jnp.zeros_like(table)
    table[:NCLASS, :] = table_ref[...].astype(BF)
    entry = lax.broadcasted_iota(jnp.int32, (count, table.shape[0]), 1)
    onehot = (entry == label).astype(F32).astype(BF)
    condition = dot(onehot, table[...]) + bias_row(B_CLASS * shards + me)
    for entry in range(shards):
        place_of = me ^ entry
        time_pre = dot(features, messages[entry][:TFREQ, :width])
        time_pre = time_pre + bias_row(B_TIME * shards + place_of)
        time_act = (time_pre * (1.0 / (1.0 + jnp.exp(-time_pre)))).astype(BF)
        start = pl.multiple_of(TFREQ + PATCH + place_of * width, 16)
        condition = condition + dot(time_act, embed_ref[pl.ds(start, width), :])
        if team:
            if entry == 0:
                time_pre_ref[...] = time_pre
        else:
            time_act_ref[place_of] = time_act
    act = (condition * (1.0 / (1.0 + jnp.exp(-condition)))).astype(BF)
    if not team:
        features_ref[...] = features
        act_ref[...] = act
        return
    condition_ref[...] = condition
    for place_of in range(shards):
        wpatch_ref[:, place_of * width : (place_of + 1) * width] = order[place_of]
    for row in range(BIASES):
        for column in range(shards):
            holder, inner = divmod(row * shards + column, BIASES)
            bias_ref[row : row + 1, column * width : (column + 1) * width] = bias_rows[
                holder, inner : inner + 1, :
            ]
    part = jnp.concatenate([dot(act, in_ref[0].astype(BF)), dot(act, final_ref[...].astype(BF))], 1)
    first = near1_ref.shape[2]
    for pair in range(shards // 2):
        row = 2 * pair * batch
        near1_ref[pair] = part[row : row + batch, :first]
        far1_ref[pair] = part[row + batch : row + 2 * batch, :first]
        near2_ref[pair] = part[row : row + batch, first:]
        far2_ref[pair] = part[row + batch : row + 2 * batch, first:]


def condition_call(operands, in_specs, out_shape, width, team):
    shards = D // width
    return pl.pallas_call(
        partial(condition_kernel, team=team),
        grid=(1,),
        in_specs=[pl.BlockSpec(memory_space=pltpu.SMEM)] + in_specs,
        out_specs=[whole(out.shape) for out in out_shape],
        out_shape=out_shape,
        scratch_shapes=[
            pltpu.VMEM((1024, width), BF),
            pltpu.VMEM((shards, BIASES, width), F32),
            pltpu.VMEM((shards, PATCH, width), BF),
        ],
        compiler_params=pltpu.CompilerParams(vmem_limit_bytes=VMEM_LIMIT),
        name="condition",
        cost_estimate=cost(6),
    )(*operands)


def condition_of_team(spot, near, other, times, embed, table, in_mats, final, batch):
    width = embed.shape[1]
    shards = D // width
    count = shards * batch
    operands = [spot, near, other, times, embed, table, in_mats, final]
    in_specs = [whole(part.shape) for part in operands[1:6]]
    in_specs += [pl.BlockSpec((1, width, 6 * D), lambda step: (0, 0, 0)), whole(final.shape)]
    half = (shards // 2, batch)
    out_shape = [
        shape_of((count, width), F32),
        shape_of((count, width), F32),
        shape_of((count, MARKS), F32),
        shape_of((PATCH, D), BF),
        shape_of((BIASES, D), F32),
        shape_of(half + (3 * D,), F32),
        shape_of(half + (3 * D,), F32),
        shape_of(half + (5 * D,), F32),
        shape_of(half + (5 * D,), F32),
    ]
    return condition_call(operands, in_specs, out_shape, width, True)


def condition_of_all(spot, near, other, times, embed, table, marks):
    width = embed.shape[1]
    count = len(marks) * marks[0].shape[0]
    operands = [spot, near, other, times, embed, table] + marks
    out_shape = [
        shape_of((count, MARKS), F32),
        shape_of((count, TFREQ), BF),
        shape_of((D // width, count, width), BF),
        shape_of((count, width), BF),
    ]
    return condition_call(operands, [whole(part.shape) for part in operands[1:]], out_shape, width, False)


def condition_back_kernel(
    spot_ref, near_ref, other_ref, team_ref, condition_ref, in_ref, final_ref, embed_ref,
    late_ref, grad_ref, near_act_ref, far_act_ref
):
    me = spot_ref[0]
    pairs, width = near_ref.shape[0], embed_ref.shape[1]
    late = jnp.concatenate([ref[pair] for pair in range(pairs) for ref in (near_ref, other_ref)], 0)
    late_ref[...] = late
    early = team_ref[...]
    grad = dot_nt(late, in_ref[0, :, : 5 * D].astype(BF))
    grad = grad + dot_nt(early[:, :D], in_ref[0, :, 5 * D :].astype(BF))
    grad = grad + dot_nt(early[:, D:], final_ref[...].astype(BF))
    condition = condition_ref[...]
    turn = 1.0 / (1.0 + jnp.exp(-condition))
    grad = (grad * (turn * (1.0 + condition * (1.0 - turn)))).astype(BF)
    grad_ref[...] = grad
    for entry in range(2 * pairs):
        start = pl.multiple_of(TFREQ + PATCH + (me ^ entry) * width, 16)
        part = dot_nt(grad, embed_ref[pl.ds(start, width), :])
        (far_act_ref if entry % 2 else near_act_ref)[entry // 2] = part


def condition_back(spot, near, other, team, condition, in_mats, final, embed):
    width = embed.shape[1]
    count = condition.shape[0]
    operands = [spot, near, other, team, condition, in_mats, final, embed]
    in_specs = [pl.BlockSpec(memory_space=pltpu.SMEM)] + [whole(part.shape) for part in operands[1:5]]
    in_specs += [pl.BlockSpec((1, width, 6 * D), lambda step: (0, 0, 0)), whole(final.shape), whole(embed.shape)]
    half = (near.shape[0], count, width)
    out_shape = [
        shape_of((count, 5 * D), BF),
        shape_of((count, width), BF),
        shape_of(half, F32),
        shape_of(half, F32),
    ]
    return pl.pallas_call(
        condition_back_kernel,
        grid=(1,),
        in_specs=in_specs,
        out_specs=[whole(out.shape) for out in out_shape],
        out_shape=out_shape,
        compiler_params=pltpu.CompilerParams(vmem_limit_bytes=VMEM_LIMIT),
        name="condition_back",
        cost_estimate=cost(4),
    )(*operands)


BIAS_PARTS = (B_PATCH, B_QUERY, B_VALUE, B_PROJ, B_UP, B_UP + 1, B_UP + 2, B_UP + 3, B_DOWN)


def condition_grads_kernel(spot_ref, marks_ref, features_ref, time_act_ref, act_ref, *refs, groups):
    early, late, last = refs[:groups], refs[groups : 2 * groups], refs[2 * groups : 3 * groups]
    gada_ref, gembed_ref, gtable_ref, bias_ref, message_ref, squares_ref = refs[3 * groups : 3 * groups + 6]
    early_all, late_all, grads_all = refs[3 * groups + 6 :]
    group = spot_ref[1]
    team = late[0].shape[0]
    width = act_ref.shape[1]
    shards = D // width
    for entry in range(groups):
        here = pl.ds(pl.multiple_of((group ^ entry) * team, team), team)
        early_all[here, :] = early[entry][...]
        late_all[here, :] = late[entry][...]
        grads_all[here, :width] = last[entry][:team, :].astype(BF)
        grads_all[here, width:] = last[entry][team : 2 * team, :].astype(BF)
    rest = [ref[2 * team :, :] for ref in last]
    while len(rest) > 1:
        rest = [rest[i] + rest[i + 1] for i in range(0, len(rest), 2)]
    rest = rest[0]
    act = act_ref[...]
    grad_time = grads_all[:, :width]
    grad_condition = grads_all[:, width:]
    gada_ref[:, : 5 * D] = dot_tn(act, late_all[...])
    gada_ref[:, 5 * D :] = dot_tn(act, early_all[...])
    marks = marks_ref[...].astype(jnp.int32)
    label = marks[:, 2:3] * 32 + marks[:, 3:4]
    entry = lax.broadcasted_iota(jnp.int32, (marks.shape[0], 1024), 1)
    onehot = (entry == label).astype(F32).astype(BF)
    gtable_ref[...] = dot_tn(grad_condition, onehot)[:, :NCLASS]
    early_rows = PATCH + TFREQ
    gembed_ref[:, :PATCH] = rest[:PATCH, :].T
    gembed_ref[:, PATCH:early_rows] = dot_tn(grad_time, features_ref[...])
    for entry in range(shards):
        start = early_rows + entry * width
        gembed_ref[:, start : start + width] = dot_tn(grad_condition, time_act_ref[entry])
    late_sum = jnp.sum(late_all[...].astype(F32), 0, keepdims=True)
    early_sum = jnp.sum(early_all[...].astype(F32), 0, keepdims=True)
    bias_ref[B_TIME : B_ADA, :] = jnp.zeros((2, D), F32)
    for part in range(5):
        bias_ref[B_ADA + part : B_ADA + part + 1, :] = late_sum[:, part * D : (part + 1) * D]
    for part in range(3):
        row = B_FINAL + part - 1 if part else B_ADA + 5
        bias_ref[row : row + 1, :] = early_sum[:, part * D : (part + 1) * D]
    for part, row in enumerate(BIAS_PARTS):
        for column in range(shards):
            first = PATCH + part * shards + column
            bias_ref[row : row + 1, column * width : (column + 1) * width] = rest[first : first + 1, :]
    btime = jnp.sum(grads_all[...].astype(F32), 0, keepdims=True)
    message_ref[0:1, :] = btime[:, :width]
    message_ref[1:2, :] = btime[:, width:]
    tail = rest[PATCH + len(BIAS_PARTS) * shards :, :]
    message_ref[2:, :] = tail
    taken = tail.shape[0] // shards
    row = lax.broadcasted_iota(jnp.int32, tail.shape, 0) // shards + spot_ref[0] * taken
    head = jnp.where(row <= OUT, tail, 0.0)

    def square(part):
        return jnp.sum(jnp.sum(part * part, 0, keepdims=True), 1, keepdims=True)

    squares_ref[...] = square(gada_ref[...]) + square(gembed_ref[...]) + square(gtable_ref[...]) + square(btime) + square(head)


def condition_grads(spot, marks, features, time_act, act, early, late, last):
    groups = len(early)
    count, width = act.shape
    operands = [spot, marks, features, time_act, act] + early + late + last
    shards = D // width
    out_shape = [
        shape_of((width, 8 * D), F32),
        shape_of((width, PATCH + TFREQ + D), F32),
        shape_of((width, NCLASS), F32),
        shape_of((BIASES, D), F32),
        shape_of((2 + tail_rows(shards) * shards, width), F32),
        shape_of((1, 1), F32),
    ]
    return pl.pallas_call(
        partial(condition_grads_kernel, groups=groups),
        grid=(1,),
        in_specs=[pl.BlockSpec(memory_space=pltpu.SMEM)] + [whole(part.shape) for part in operands[1:]],
        out_specs=[whole(out.shape) for out in out_shape],
        out_shape=out_shape,
        scratch_shapes=[
            pltpu.VMEM((count, 3 * D), BF),
            pltpu.VMEM((count, 5 * D), BF),
            pltpu.VMEM((count, 2 * width), BF),
        ],
        compiler_params=pltpu.CompilerParams(vmem_limit_bytes=VMEM_LIMIT),
        name="condition_grads",
        cost_estimate=cost(6),
    )(*operands)


def swap(array_in, axis, hop):
    count = lax.axis_size(axis)
    return lax.ppermute(array_in, axis, [(place_of, place_of ^ hop) for place_of in range(count)])


def spread(array_in, axis):
    count = lax.axis_size(axis)
    if axis == "shard":
        near = jnp.stack([array_in] + [swap(array_in, axis, hop) for hop in range(2, count, 2)])
        return jnp.stack([near, swap(near, axis, 1)], 1).reshape((count,) + array_in.shape)
    return jnp.stack([array_in] + [swap(array_in, axis, hop) for hop in range(1, count)])


def total_of(parts):
    while len(parts) > 1:
        parts = [parts[i] + parts[i + 1] for i in range(0, len(parts), 2)]
    return parts[0]


def exchange_sum(near):
    return total_of([near[0]] + [swap(near[hop], "shard", 2 * hop) for hop in range(1, near.shape[0])])


def from_groups(array_in, tuned):
    count = lax.axis_size("grp")
    if tuned:
        return [array_in] + [swap(array_in, "grp", hop) for hop in range(1, count)]
    parts = jnp.broadcast_to(array_in[None], (count,) + array_in.shape)
    parts = ordered(lax.all_to_all(parts, "grp", 0, 0, tiled=True), "grp")
    return [parts[i] for i in range(count)]


def ordered(array_in, axis):
    count = lax.axis_size(axis)
    place_of = lax.axis_index(axis)
    bit = 1
    while bit < count:
        pairs = array_in.reshape((count // (2 * bit), 2, bit) + array_in.shape[1:])
        array_in = jnp.where(place_of & bit != 0, pairs[:, ::-1], pairs).reshape(array_in.shape)
        bit *= 2
    return array_in


def sum_spread(array_in, axis):
    parts = spread(array_in, axis)
    return total_of([parts[i] for i in range(parts.shape[0])])


def tie(arrays, after):
    return lax.optimization_barrier((arrays, after))[0]


def rows_near(own):
    rows_all = own.shape[0]
    quarter = -(-rows_all // 64) * 16
    group = lax.axis_index("grp")
    start = jnp.where(group == 3, rows_all - quarter, group * quarter)
    part = lax.dynamic_slice_in_dim(own, start, quarter, 0)
    return [swap(part, "shard", hop) for hop in (2, 4, 6)]


def rows_far(near):
    near = jnp.stack(near)
    return [near] + [swap(near, "grp", hop) for hop in (1, 2, 3)]


def rows_all(own, parts):
    return [own] + parts + [swap(own, "shard", 1), swap(jnp.concatenate(parts), "shard", 1)]


def quarter_start(rows_all, quarter, group):
    return jnp.where(group == 3, rows_all - quarter, group * quarter)


def cores_summed(grads):
    pairs = grads.reshape((4, 2) + grads.shape[1:])
    core = lax.axis_index("shard") % 2
    theirs = lax.dynamic_index_in_dim(pairs, 1 - core, 1, keepdims=False)
    mine = lax.dynamic_index_in_dim(pairs, core, 1, keepdims=False)
    return lower(mine.astype(F32) + swap(theirs, "shard", 1).astype(F32))


def groups_traded(grads):
    group = lax.axis_index("grp")
    rows_all = grads.shape[1]
    quarter = -(-rows_all // 64) * 16
    parts = []
    for hop in range(4):
        start = quarter_start(rows_all, quarter, group ^ hop)
        part = lax.dynamic_slice_in_dim(grads, start, quarter, 1)
        parts.append(swap(part, "grp", hop) if hop else part)
    return parts


def shards_traded(parts):
    total = total_of([part.astype(F32) for part in parts])
    low = lower(total)
    chip = lax.axis_index("shard") // 2
    own = lax.dynamic_index_in_dim(total, chip, 0, keepdims=False)
    return [own] + [
        swap(lax.dynamic_index_in_dim(low, chip ^ hop, 0, keepdims=False), "shard", 2 * hop) for hop in (1, 2, 3)
    ]


def shards_summed(parts):
    return lower(total_of([part.astype(F32) for part in parts]))


def quarters_of_both(first, second, first_rows, second_rows):
    taken = first.shape[0]
    both = jnp.concatenate([first, second])
    parts = ordered(jnp.stack([both] + [swap(both, "grp", hop) for hop in (1, 2, 3)]), "grp")
    joined = []
    for part, rows_all in ((parts[:, :taken], first_rows), (parts[:, taken:], second_rows)):
        quarter = part.shape[1]
        joined.append(jnp.concatenate([part[0], part[1], part[2], part[3, 4 * quarter - rows_all :]]).astype(F32))
    return joined


def quarters_traded(part):
    return [quarter[0] for quarter in groups_traded(part[None])]


def matmul(formula, left, right):
    return jnp.einsum(formula, left, right, preferred_element_type=F32)


def lower(array_in):
    return array_in.astype(BF)


def summed(array_in, axes):
    return jnp.sum(array_in.astype(F32), axes)


def position_table():
    quarter = D // 4
    angular = jnp.exp(-math.log(10000.0) * jnp.arange(quarter, dtype=F32) / quarter)
    position = jnp.arange(GRID * GRID, dtype=jnp.int32)
    column = (position % GRID).astype(F32)[:, None] * angular
    row_pos = (position // GRID).astype(F32)[:, None] * angular
    return jnp.concatenate(
        [jnp.sin(column), jnp.cos(column), jnp.sin(row_pos), jnp.cos(row_pos)], 1
    )


def pick_times(time_index, times):
    matches = time_index[:, None] == jnp.arange(times.shape[0], dtype=jnp.int32)[None, :]
    return jnp.sum(jnp.where(matches, times[None, :], 0.0), 1)


def condition_grads_plain(spot, marks, features, time_act, act, early, late, last):
    team, width = late[0].shape[0], act.shape[1]
    shards = D // width
    early, late, last_all = [
        ordered(jnp.stack(parts), "grp").reshape(-1, parts[0].shape[1])
        for parts in (early, late, [part[: 2 * team] for part in last])
    ]
    last_all = lower(last_all).reshape(-1, 2, team, width)
    grad_time, grad_condition = last_all[:, 0].reshape(-1, width), last_all[:, 1].reshape(-1, width)
    rest = total_of([part[2 * team :] for part in last])
    gada = jnp.concatenate([matmul("bd,be->de", act, late), matmul("bd,be->de", act, early)], 1)
    labels = (marks[:, 2:3] * 32.0 + marks[:, 3:4]).astype(jnp.int32)
    onehot = lower((labels == jnp.arange(NCLASS, dtype=jnp.int32)[None, :]).astype(F32))
    gtable = matmul("bd,bn->dn", grad_condition, onehot)
    gembed = jnp.concatenate(
        [
            rest[:PATCH].T,
            matmul("bd,bf->df", grad_time, features),
            matmul("be,sbd->esd", grad_condition, time_act).reshape(width, D),
        ],
        1,
    )
    bias = jnp.zeros((BIASES, D), F32)
    bias = bias.at[B_ADA : B_ADA + 5].set(summed(late, 0).reshape(5, D))
    early_sum = summed(early, 0).reshape(3, D)
    bias = bias.at[B_ADA + 5].set(early_sum[0]).at[B_FINAL:].set(early_sum[1:])
    parts = rest[PATCH : PATCH + len(BIAS_PARTS) * shards].reshape(len(BIAS_PARTS), D)
    for part, row in enumerate(BIAS_PARTS):
        bias = bias.at[row].set(parts[part])
    btime = jnp.stack([summed(grad_time, 0), summed(grad_condition, 0)])
    tail = rest[PATCH + len(BIAS_PARTS) * shards :]
    taken = tail.shape[0] // shards
    row = jnp.arange(tail.shape[0], dtype=jnp.int32)[:, None] // shards + spot[0] * taken
    head = jnp.where(row <= OUT, tail, 0.0)
    squares = sum(jnp.sum(part * part) for part in (gada, gembed, gtable, btime, head))
    return gada, gembed, gtable, bias, jnp.concatenate([btime, tail]), squares.reshape(1, 1)


def adamw(weight, moment_one, moment_two, gradient, factor):
    gradient = gradient * factor
    moment_one = BETA_ONE * moment_one + (1.0 - BETA_ONE) * gradient
    moment_two = BETA_TWO * moment_two + (1.0 - BETA_TWO) * gradient * gradient
    fix_one = 1.0 - BETA_ONE**STEP
    fix_two = 1.0 - BETA_TWO**STEP
    update = (
        moment_one / fix_one / (jnp.sqrt(moment_two / fix_two) + EPS_ADAM) + WEIGHT_DECAY * weight
    )
    return (weight - LEARN_RATE * update, moment_one, moment_two)


def per_device(
    latents, noise, velocity, labels, time_index, times,
    in_mats, out_mats, embed_mats, class_table, final_ada, head_mat, bias_vec,
    in_mats_first, out_mats_first, embed_first, table_first, final_first, head_first, bias_first,
    in_mats_second, out_mats_second, embed_second, table_second, final_second, head_second, bias_second,
):
    shards = lax.axis_size("shard")
    groups = lax.axis_size("grp")
    me = lax.axis_index("shard")
    mine = lax.axis_index("grp")
    batch = latents.shape[0]
    width = embed_mats.shape[1]
    team = shards * batch
    tuned = groups == 4 and shards == 8

    embed_low = lower(embed_mats)
    marks = jnp.stack([time_index // 32, time_index % 32, labels // 32, labels % 32], 1).astype(BF)
    marks = jnp.pad(marks, ((0, TFREQ - batch), (0, 128 - width - MARKS)))
    message = jnp.concatenate(
        [embed_low[PATCH : PATCH + TFREQ], embed_low[:PATCH], lower(bias_vec).reshape(BIASES, width)]
    )
    message = jnp.pad(message, ((0, MESSAGE - message.shape[0]), (0, 128 - width)))
    message = message + jnp.pad(marks, ((0, MESSAGE - TFREQ), (width, 0)))
    arrived = [swap(message, "shard", hop) for hop in range(2, shards, 2)]
    near_message = jnp.stack([message] + arrived)
    other_message = swap(near_message, "shard", 1)
    in_mats_early, out_mats_early = tie((in_mats, out_mats), message)

    def rows_of(first, count):
        part = lower(in_mats_early[0, :, first : first + count * D])
        return part.reshape(width, count, D).transpose(1, 0, 2).reshape(count * width, D)

    own_qkv = rows_of(6 * D, 3)
    own_feed = jnp.concatenate([rows_of(9 * D, FF // D), lower(out_mats_early[0])])
    spot = jnp.stack([me, mine]).astype(jnp.int32)
    if tuned:
        near_qkv = rows_near(own_qkv)
        own_feed = tie(own_feed, near_message)
        near_feed = rows_near(own_feed)
        far_qkv = rows_far(tie(near_qkv, near_message))
    else:
        qkv_pieces, feed_pieces = [[lax.all_gather(own, "shard")] for own in (own_qkv, own_feed)]
    times_row = jnp.pad(times, (0, -times.shape[0] % 128))[None]
    time_pre, condition, marks_team, wpatch, biases, near_attn, far_attn, near_rest, far_rest = condition_of_team(
        spot, near_message, other_message, times_row, embed_low, class_table, in_mats, final_ada, batch
    )
    near_attn = near_attn + swap(far_attn, "shard", 1)
    mod_attn = exchange_sum(near_attn)[:, None, :]
    latents, noise, velocity, head_mat_late = tie((latents, noise, velocity, head_mat), near_attn)
    if tuned:
        qkv_pieces = rows_all(own_qkv, tie(far_qkv, near_attn))
        far_feed = rows_far(tie(near_feed, near_attn))
    moment = pick_times(time_index, times)
    noisy = lower((1.0 - moment)[:, None, None] * latents + moment[:, None, None] * noise)
    pos = position_table()
    a, qkv, o, wqkv = attend(spot, noisy, pos, wpatch, mod_attn, biases, qkv_pieces, shards)
    if tuned:
        feed_pieces = rows_all(*tie((own_feed, far_feed), o))
    near_rest, far_rest = tie((near_rest, far_rest), o)
    mod_rest = exchange_sum(near_rest + swap(far_rest, "shard", 1))[:, None, :]
    marks_team = tie(marks_team, o)
    marks_all = from_groups(marks_team, tuned)
    marks_all, features, time_act, cond_act_all = condition_of_all(
        spot, near_message, other_message, times_row, embed_low, class_table, marks_all
    )
    mod_rest = tie(mod_rest, features)
    count_all = float(groups * shards * batch * SEQ * OUT)
    head_low = lower(head_mat_late)
    mid, y, m, g, slope, df, ds, dmod_feed, near_tail, far_tail, bdown, wup, wout = feed(
        spot, moment, noisy, pos, wpatch, o, mod_attn, mod_rest, biases, head_low[:D],
        head_low[D:].astype(F32), velocity, feed_pieces, shards, count_all,
    )
    wout = wout.reshape(D + FF, D)
    tokens = batch * SEQ
    early = lower(dmod_feed[:, 0])
    early_far = [swap(early, "shard", hop) for hop in range(2, shards, 2)]
    gup, gout, bup, dm = feed_back(
        m.reshape(tokens, D), df.reshape(tokens, D), g, slope, wup, wout, 0, FF
    )
    gup = lax.psum_scatter(gup, "shard", scatter_dimension=0)
    early_near = jnp.stack([early] + tie(early_far, dm))
    early_other = swap(early_near, "shard", 1)
    dmid, do, dmod_mid, gout, bproj = middle_back(
        mid, dm.reshape(batch, SEQ, D), ds, y, o, mod_attn, mod_rest, biases, wout, gout
    )

    early_near, early_other = tie((early_near, early_other), dmid)
    early = jnp.stack([early_near, early_other], 1).reshape(team, 3 * D)
    grads_early = from_groups(early, tuned)
    gout = gout.reshape(shards, (D + FF) // shards, D)
    if tuned:
        gout = cores_summed(gout)
        do = tie(do, gout)
        gout_parts = groups_traded(gout)
    else:
        gout = lax.psum_scatter(gout, "shard", scatter_dimension=0)
    dqkv, gqkv, bqkv = attend_back(qkv, do, a, shards)
    gqkv = lax.psum_scatter(gqkv, "shard", scatter_dimension=0)
    if tuned:
        gout_parts, grads_early = tie((gout_parts, grads_early), dqkv)
        gout_parts = shards_traded(gout_parts)
        dmid, gup, bqkv = tie((dmid, gup, bqkv), gout_parts[0])
        gup_parts = quarters_traded(gup)
    dmod_attn, near_patch, far_patch, bpatch = stream_back(
        spot, dqkv, dmid, noisy, pos, wpatch, mod_attn, biases, wqkv
    )
    late = lower(jnp.concatenate([dmod_attn[:, 0], dmod_mid[:, 0]], 1))
    if tuned:
        gup_parts, gout_parts = tie((gup_parts, gout_parts), late)
        gup, gout = shards_summed(gup_parts), shards_summed(gout_parts)
        late = tie(late, (gup, gout))

    near_late = jnp.stack([late] + [swap(late, "shard", hop) for hop in range(2, shards, 2)])
    other_late = swap(near_late, "shard", 1)
    late, grad_condition, near_act, far_act = condition_back(
        spot, near_late, other_late, early, condition, in_mats, final_ada, embed_low
    )
    bias_part = jnp.concatenate([bpatch, bqkv[:, :D], bqkv[:, 2 * D :], bproj, bup, bdown], 1)
    bias_part = jnp.broadcast_to(bias_part.reshape(1, -1, width), (shards // 2, len(BIAS_PARTS) * shards, width))

    def by_width(part):
        return part.reshape(part.shape[0], -1, width)

    far_act = jnp.concatenate([far_act, far_patch, bias_part, by_width(far_tail)], 1)
    near_act = jnp.concatenate([near_act, near_patch, bias_part, by_width(near_tail)], 1)
    act_part = exchange_sum(near_act + swap(far_act, "shard", 1))
    unused, time_pull = jax.vjp(jax.nn.silu, time_pre)
    grad_time = lower(time_pull(act_part[:team])[0])
    last = jnp.concatenate([grad_time.astype(F32), grad_condition.astype(F32), act_part[team:]])
    grads_last = from_groups(last, tuned)
    grads_late = from_groups(late, tuned)
    gqkv = from_groups(gqkv, tuned)
    if tuned:
        gfeed = quarters_of_both(gup, gout, FF // shards, (D + FF) // shards)
    else:
        gfeed = [
            total_of([part.astype(F32) for part in from_groups(grads, tuned)]) for grads in (gup, gout)
        ]
    grads_of = condition_grads if tuned else condition_grads_plain
    gada, gembed, gtable, bias_grad, message, squares = grads_of(
        spot, marks_all, features, time_act, cond_act_all, grads_early, grads_late, grads_last
    )
    gup, gout = gfeed
    gqkv = total_of([part.astype(F32) for part in gqkv])
    share = bias_vec.shape[0]
    bias_grad = lax.dynamic_slice_in_dim(bias_grad.reshape(-1), me * share, share, 0)
    squares = squares + sum(jnp.sum(part * part) for part in (gup, gqkv, gout, bias_grad))
    message = jnp.concatenate([message, jnp.broadcast_to(squares, (6, width))])
    final = spread(message, "shard")
    grad_norm = jnp.sqrt(total_of([final[i, -1, 0] for i in range(shards)]))
    factor = CLIP_NORM / jnp.maximum(grad_norm, CLIP_NORM)
    final = ordered(final, "shard")
    btime = jnp.concatenate([final[:, 0].reshape(-1), final[:, 1].reshape(-1)])
    tail = final[:, 2:-6].reshape(-1, D)
    head_grad = jnp.concatenate([tail[:OUT].T, tail[OUT : OUT + 1, :OUT]])
    loss_sum = tail[OUT + 1, 0]
    btime = jnp.concatenate([jnp.zeros((D,), F32), btime, jnp.zeros((12 * D + FF,), F32)])
    bias_grad = bias_grad + lax.dynamic_slice_in_dim(btime, me * share, share, 0)
    in_grad = jnp.concatenate(
        [gada[:, : 6 * D]]
        + [gqkv[part * width : (part + 1) * width] for part in range(3)]
        + [gup[part * width : (part + 1) * width] for part in range(FF // D)],
        1,
    )
    weights = (in_mats, out_mats, embed_mats, class_table, final_ada, head_mat, bias_vec)
    firsts = (in_mats_first, out_mats_first, embed_first, table_first, final_first, head_first, bias_first)
    seconds = (
        in_mats_second, out_mats_second, embed_second, table_second, final_second, head_second, bias_second
    )
    grads = (in_grad[None], gout[None], gembed.T, gtable.T, gada[:, 6 * D :], head_grad, bias_grad)
    stepped = [
        adamw(weight, moment_one, moment_two, gradient, factor)
        for weight, moment_one, moment_two, gradient in zip(weights, firsts, seconds, grads)
    ]
    return tuple(part[0] for part in stepped) + tuple(part[1] for part in stepped) + tuple(
        part[2] for part in stepped
    ) + (loss_sum, grad_norm)


def solution(mesh):
    images = P(("grp", "shard"))
    placed = (
        P(None, "shard", None),
        P(None, "shard", None),
        P(None, "shard"),
        P(None, "shard"),
        P("shard", None),
        P(),
        P("shard"),
    )
    return jax.shard_map(
        per_device,
        mesh=mesh,
        in_specs=(images,) * 5 + (P(),) + placed * 3,
        out_specs=placed * 3 + (P(), P()),
        check_vma=False,
    )
```

```python
import math
from functools import partial
import numpy as np
import jax
import jax.numpy as jnp
from jax import lax
from jax.sharding import PartitionSpec as P
from jax.experimental import pallas as pl
from jax.experimental.pallas import tpu as pltpu

D = 768
HEADS = 12
HDIM = 64
FF = 3072
PATCH = 16
SEQ = 256
OUT = 32
GRID = 16
STEP = 10
BETA_ONE = 0.9
BETA_TWO = 0.999
LEARN_RATE = 0.05
WEIGHT_DECAY = 0.05
EPS_ADAM = 1e-08
CLIP_NORM = 0.01
TFREQ = 256
NCLASS = 1001
EPS_NORM = 1e-06
BF = jnp.bfloat16
F32 = jnp.float32
VMEM_LIMIT = 60 * 1024 * 1024
COST = 3 * 10**8
PAIR = 2 * HDIM
PAIRS = HEADS // 2
BIASES = 19
B_PATCH, B_TIME, B_CLASS, B_ADA, B_QUERY, B_VALUE, B_PROJ, B_UP, B_DOWN, B_FINAL = 0, 1, 2, 3, 9, 10, 11, 12, 16, 17


def dot(left, right):
    return jnp.dot(left, right, preferred_element_type=F32)


def dot_nt(left, right):
    return lax.dot_general(left, right, (((1,), (1,)), ((), ())), preferred_element_type=F32)


def dot_tn(left, right):
    return lax.dot_general(left, right, (((0,), (0,)), ((), ())), preferred_element_type=F32)


def whole(shape):
    zeros = (0,) * len(shape)
    return pl.BlockSpec(shape, lambda step: zeros, pipeline_mode=pl.Buffered(1))


def fixed(shape):
    zeros = (0,) * len(shape)
    return pl.BlockSpec(shape, lambda step: zeros)


def rows(count, *rest):
    zeros = (0,) * len(rest)
    return pl.BlockSpec((count,) + rest, lambda step: (step,) + zeros)


def shape_of(shape, dtype):
    return jax.ShapeDtypeStruct(shape, dtype)


def norm_parts(array_in):
    centre = array_in - jnp.mean(array_in, -1, keepdims=True)
    inverse = lax.rsqrt(jnp.mean(centre * centre, -1, keepdims=True) + EPS_NORM)
    return centre * inverse, inverse


def norm_back(grad_normed, normed, inverse):
    first = jnp.mean(grad_normed, -1, keepdims=True)
    second = jnp.mean(grad_normed * normed, -1, keepdims=True)
    return inverse * (grad_normed - first - normed * second)


def cost(microseconds):
    return pl.CostEstimate(flops=microseconds * COST, bytes_accessed=0, transcendentals=0)


def head_masks():
    lane = lax.broadcasted_iota(jnp.int32, (1, PAIR), 1)
    return (lane < HDIM, lane >= HDIM)


def weight_copies(spot_ref, pieces, target, sem):
    if len(pieces) == 1:
        return [pltpu.make_async_copy(pieces[0], target, sem)]
    own, near, pair, other = pieces
    shard = spot_ref[0]
    quarter = near.shape[2]
    rest = target.shape[1] - 3 * quarter
    made = [
        pltpu.make_async_copy(own, target.at[shard], sem),
        pltpu.make_async_copy(pair, target.at[shard ^ 1], sem),
    ]
    for block in range(4):
        count = rest if block == 3 else quarter
        rows_here = slice(block * quarter, block * quarter + count)
        for core, part in enumerate((near, other)):
            for hop in range(3):
                source = part.at[block, hop, quarter - count :] if count < quarter else part.at[block, hop]
                slot = shard ^ (2 * hop + 2 + core)
                made.append(pltpu.make_async_copy(source, target.at[slot, rows_here], sem))
    return made


def run_copies(made, start):
    for copy in made:
        copy.start() if start else copy.wait()


def part_of(weights, part, count):
    width = weights.shape[1] // count
    return weights[:, part * width : (part + 1) * width, :].reshape(D, D)


def attend_kernel(
    spot_ref, noisy_ref, pos_ref, wpatch_ref, mod_ref, bias_ref, *refs, images
):
    pieces, (a_ref, qkv_ref, o_ref, kept_ref, wqkv_ref, sem, out_sem) = refs[:-7], refs[-7:]
    step = pl.program_id(0)
    made = weight_copies(spot_ref, pieces, wqkv_ref, sem)
    keep = pltpu.make_async_copy(wqkv_ref, kept_ref, out_sem)

    @pl.when(step == 0)
    def _():
        run_copies(made, True)
        run_copies(made, False)
        keep.start()

    @pl.when(step == pl.num_programs(0) - 1)
    def _():
        keep.wait()

    masks = head_masks()

    def bias(row):
        return bias_ref[row : row + 1, :]

    def image(index, carry):
        stream = dot(noisy_ref[index], wpatch_ref[...]) + (pos_ref[...] + bias(B_PATCH))
        normed, unused = norm_parts(stream)
        scale = 1.0 + (mod_ref[index, :, D : 2 * D] + bias(B_ADA + 1))
        a = (normed * scale + (mod_ref[index, :, :D] + bias(B_ADA))).astype(BF)
        a_ref[index] = a
        for part in range(3):
            cut = slice(part * D, (part + 1) * D)
            product = dot(a, part_of(wqkv_ref, part, 3))
            if part != 1:
                product = product + bias(B_QUERY if part == 0 else B_VALUE)
            qkv_ref[index, :, cut] = product.astype(BF)
        for pair in range(PAIRS):
            base = pair * PAIR
            queries = qkv_ref[index, :, base : base + PAIR]
            keys = qkv_ref[index, :, D + base : D + base + PAIR]
            values = qkv_ref[index, :, 2 * D + base : 2 * D + base + PAIR]
            mixed = []
            for mask in masks:
                part = jnp.where(mask, queries * jnp.asarray(HDIM**-0.5, BF), jnp.zeros_like(queries))
                scores = dot_nt(part, keys)
                power = jnp.exp(scores - jnp.max(scores, -1, keepdims=True))
                total = jnp.sum(power, -1, keepdims=True)
                prob = (power * (1.0 / total)).astype(BF)
                mixed.append(dot(prob, values))
            o_ref[index, :, base : base + PAIR] = jnp.where(masks[0], mixed[0], mixed[1]).astype(BF)
        return carry

    lax.fori_loop(0, images, image, 0)


ANYWHERE = pl.BlockSpec(memory_space=pl.ANY)


def attend(spot, noisy, pos, wpatch, mod, bias, pieces, shards, images=2):
    batch = noisy.shape[0]
    kept = (shards, 3 * D // shards, D)
    return pl.pallas_call(
        partial(attend_kernel, images=images),
        grid=(batch // images,),
        in_specs=[
            pl.BlockSpec(memory_space=pltpu.SMEM),
            rows(images, SEQ, PATCH),
            whole((SEQ, D)),
            whole((PATCH, D)),
            rows(images, 1, 8 * D),
            whole((BIASES, D)),
        ]
        + [ANYWHERE] * len(pieces),
        out_specs=[rows(images, SEQ, D), rows(images, SEQ, 3 * D), rows(images, SEQ, D), ANYWHERE],
        out_shape=[
            shape_of((batch, SEQ, D), BF),
            shape_of((batch, SEQ, 3 * D), BF),
            shape_of((batch, SEQ, D), BF),
            shape_of(kept, BF),
        ],
        scratch_shapes=[pltpu.VMEM(kept, BF), pltpu.SemaphoreType.DMA, pltpu.SemaphoreType.DMA],
        compiler_params=pltpu.CompilerParams(vmem_limit_bytes=VMEM_LIMIT),
        name="attend",
        cost_estimate=cost(32),
    )(spot, noisy, pos, wpatch, mod, bias, *pieces)


GELU_A = math.sqrt(2.0 / math.pi)
GELU_B = 0.044715


def gelu_both(u):
    square = u * u
    turn = jnp.tanh(u * (GELU_A + (GELU_A * GELU_B) * square))
    half = 0.5 + 0.5 * turn
    slope = half + (0.5 * u) * (1.0 - turn * turn) * (GELU_A + (3.0 * GELU_A * GELU_B) * square)
    return u * half, slope


def feed_kernel(
    spot_ref, t_ref, noisy_ref, pos_ref, wpatch_ref, o_ref, mod_ref, bias_ref,
    head_ref, hbias_ref, vel_ref, *refs, images, count_all
):
    pieces, refs = refs[:-18], refs[-18:]
    mid_ref, y_ref, m_ref, g_ref, slope_ref, df_ref, ds_ref, dmod_ref, near_ref, far_ref, bdown_ref = refs[:11]
    kept1_ref, kept2_ref, weights_ref, tail_ref, order, sem, out_sem = refs[11:]
    step = pl.program_id(0)
    made = weight_copies(spot_ref, pieces, weights_ref, sem)
    up_width, out_width = kept1_ref.shape[1], kept2_ref.shape[1]
    keeps = [
        pltpu.make_async_copy(weights_ref.at[:, :up_width], kept1_ref, out_sem.at[0]),
        pltpu.make_async_copy(weights_ref.at[:, up_width:], kept2_ref, out_sem.at[1]),
    ]

    @pl.when(step == 0)
    def _():
        run_copies(made, True)
        run_copies(made, False)
        for keep in keeps:
            keep.start()

    @pl.when(step == pl.num_programs(0) - 1)
    def _():
        for keep in keeps:
            keep.wait()

    @pl.when(step == 0)
    def _():
        tail_ref[...] = jnp.zeros_like(tail_ref)
        bdown_ref[...] = jnp.zeros_like(bdown_ref)

    tokens = images * SEQ

    def bias(row):
        return bias_ref[row : row + 1, :]

    def spread(part):
        parts = []
        for index in range(images):
            row = mod_ref[index, :, (part + 2) * D : (part + 3) * D]
            row = row + bias(B_ADA + 2 + part if part < 4 else B_FINAL + part - 4)
            parts.append(jnp.broadcast_to(row, (SEQ, D)))
        return jnp.concatenate(parts, 0)

    def up_part(part):
        rows_of = up_width * D // FF
        return weights_ref[:, part * rows_of : (part + 1) * rows_of, :].reshape(D, D)

    def out_rows(part):
        first, taken = part * D, []
        while first < (part + 1) * D:
            place_of, row = first // out_width, first % out_width
            count = min(out_width - row, (part + 1) * D - first)
            taken.append(weights_ref[place_of, up_width + row : up_width + row + count, :])
            first += count
        return jnp.concatenate(taken, 0)

    position = jnp.concatenate([pos_ref[...] + bias(B_PATCH)] * images, 0)
    stream = dot(noisy_ref[...].reshape(tokens, PATCH), wpatch_ref[...]) + position
    y = dot(o_ref[...].reshape(tokens, D), out_rows(0)) + bias(B_PROJ)
    y_ref[...] = y.astype(BF).reshape(images, SEQ, D)
    mid = stream + spread(0) * y
    mid_ref[...] = mid.reshape(images, SEQ, D)
    normed, unused = norm_parts(mid)
    m = (normed * (1.0 + spread(2)) + spread(1)).astype(BF)
    m_ref[...] = m.reshape(images, SEQ, D)
    feed = jnp.broadcast_to(bias(B_DOWN), (tokens, D))
    for j in range(FF // D):
        cut = slice(j * D, (j + 1) * D)
        g, slope = gelu_both(dot(m, up_part(j)) + bias(B_UP + j))
        g = g.astype(BF)
        g_ref[:, cut] = g
        slope_ref[:, cut] = slope.astype(BF)
        feed = feed + dot(g, out_rows(j + 1))
    gate = spread(3)
    stream = mid + gate * feed
    normed, inverse = norm_parts(stream)
    scale = 1.0 + spread(5)
    z = (normed * scale + spread(4)).astype(BF)
    predicted = dot(z, head_ref[...]) + hbias_ref[...]
    t = jnp.concatenate(
        [jnp.full((SEQ, 1), t_ref[step * images + index], F32) for index in range(images)], 0
    )
    residual = predicted - vel_ref[...].reshape(tokens, OUT)
    weighted = t * residual
    loss = jnp.sum(jnp.sum(weighted * residual, 0, keepdims=True), 1, keepdims=True)
    tail_ref[OUT + 1 : OUT + 2, :] += jnp.broadcast_to(loss, (1, D))
    grad_pred = (2.0 * weighted / count_all).astype(BF)
    tail_ref[OUT : OUT + 1, :OUT] += jnp.sum(grad_pred.astype(F32), 0, keepdims=True)
    tail_ref[:OUT, :] += dot_tn(grad_pred, z)
    dz = dot_nt(grad_pred, head_ref[...])
    ds = norm_back(dz * scale, normed, inverse)
    ds_ref[...] = ds.reshape(images, SEQ, D)
    df = (ds * gate).astype(BF)
    df_ref[...] = df.reshape(images, SEQ, D)
    bdown_ref[...] += jnp.sum(df.astype(F32), 0, keepdims=True)
    for index in range(images):
        cut = slice(index * SEQ, (index + 1) * SEQ)
        dmod_ref[index, :, :D] = jnp.sum(ds[cut] * feed[cut], 0, keepdims=True)
        dmod_ref[index, :, D : 2 * D] = jnp.sum(dz[cut], 0, keepdims=True)
        dmod_ref[index, :, 2 * D :] = jnp.sum(dz[cut] * normed[cut], 0, keepdims=True)

    shards, taken = 2 * near_ref.shape[0], near_ref.shape[1]

    @pl.when(step == pl.num_programs(0) - 1)
    def _():
        for place_of in range(shards):
            order[place_of] = tail_ref[place_of * taken : (place_of + 1) * taken, :]
        for entry in range(shards):
            (far_ref if entry % 2 else near_ref)[entry // 2] = order[spot_ref[0] ^ entry]


def tail_rows(shards):
    return -(-(OUT + 2) // shards)


def feed(spot, t, noisy, pos, wpatch, o, mod, bias, head, hbias, velocity, pieces, shards, count_all, images=2):
    batch = o.shape[0]
    kept1 = (shards, FF // shards, D)
    kept2 = (shards, (D + FF) // shards, D)
    half = (shards // 2, tail_rows(shards), D)
    tokens = batch * SEQ
    return pl.pallas_call(
        partial(feed_kernel, images=images, count_all=count_all),
        grid=(batch // images,),
        in_specs=[
            pl.BlockSpec(memory_space=pltpu.SMEM),
            pl.BlockSpec(memory_space=pltpu.SMEM),
            rows(images, SEQ, PATCH),
            whole((SEQ, D)),
            whole((PATCH, D)),
            rows(images, SEQ, D),
            rows(images, 1, 8 * D),
            whole((BIASES, D)),
            whole((D, OUT)),
            whole((1, OUT)),
            rows(images, SEQ, OUT),
        ]
        + [ANYWHERE] * len(pieces),
        out_specs=[
            rows(images, SEQ, D),
            rows(images, SEQ, D),
            rows(images, SEQ, D),
            rows(images * SEQ, FF),
            rows(images * SEQ, FF),
            rows(images, SEQ, D),
            rows(images, SEQ, D),
            rows(images, 1, 3 * D),
            fixed(half),
            fixed(half),
            fixed((1, D)),
            ANYWHERE,
            ANYWHERE,
        ],
        out_shape=[
            shape_of((batch, SEQ, D), F32),
            shape_of((batch, SEQ, D), BF),
            shape_of((batch, SEQ, D), BF),
            shape_of((tokens, FF), BF),
            shape_of((tokens, FF), BF),
            shape_of((batch, SEQ, D), BF),
            shape_of((batch, SEQ, D), F32),
            shape_of((batch, 1, 3 * D), F32),
            shape_of(half, F32),
            shape_of(half, F32),
            shape_of((1, D), F32),
            shape_of(kept1, BF),
            shape_of(kept2, BF),
        ],
        scratch_shapes=[
            pltpu.VMEM((shards, kept1[1] + kept2[1], D), BF),
            pltpu.VMEM((shards * half[1], D), F32),
            pltpu.VMEM((shards,) + half[1:], F32),
            pltpu.SemaphoreType.DMA,
            pltpu.SemaphoreType.DMA((2,)),
        ],
        compiler_params=pltpu.CompilerParams(vmem_limit_bytes=VMEM_LIMIT),
        name="feed",
        cost_estimate=cost(52),
    )(spot, t, noisy, pos, wpatch, o, mod, bias, head, hbias, velocity, *pieces)


def feed_back_kernel(
    m_ref, df_ref, g_ref, slope_ref, w1_ref, w2_ref, wup_ref, wdown_ref, bup_ref, dm_ref, mt, dft, *, tile
):
    step = pl.program_id(0)

    @pl.when(step == 0)
    def _():
        mt[...] = m_ref[...].T
        dft[...] = df_ref[...].T
        dm_ref[...] = jnp.zeros_like(dm_ref)

    tokens = m_ref.shape[0]
    w1 = w1_ref[...].reshape(D, D)
    w2 = w2_ref[...]
    du_parts = []
    for i in range(tokens // tile):
        cut = slice(i * tile, (i + 1) * tile)
        du = (dot_nt(df_ref[cut, :], w2) * slope_ref[cut, :].astype(F32)).astype(BF)
        du_parts.append(du)
        dm_ref[cut, :] += dot_nt(du, w1)
    du = jnp.concatenate(du_parts, 0)
    bup_ref[...] = jnp.sum(du.astype(F32), 0, keepdims=True)
    wup_ref[...] = dot(mt[...], du).astype(BF).reshape(wup_ref.shape)
    wdown_ref[...] = dot(dft[...], g_ref[...]).T.astype(BF)


def feed_back(m, df, g, slope, w1, wout, first, last, tile=512):
    chunk = D
    shards = w1.shape[0]
    rows_of = D // shards
    tokens = m.shape[0]
    steps = (last - first) // chunk
    base = first // chunk
    return pl.pallas_call(
        partial(feed_back_kernel, tile=tile),
        grid=(steps,),
        in_specs=[
            whole((tokens, D)),
            whole((tokens, D)),
            pl.BlockSpec((tokens, chunk), lambda step: (0, step + base)),
            pl.BlockSpec((tokens, chunk), lambda step: (0, step + base)),
            pl.BlockSpec((shards, rows_of, D), lambda step: (0, step + base, 0)),
            pl.BlockSpec((chunk, D), lambda step: (step + base + D // chunk, 0)),
        ],
        out_specs=[
            pl.BlockSpec((shards, rows_of, D), lambda step: (0, step, 0)),
            pl.BlockSpec((chunk, D), lambda step: (step + base + D // chunk, 0)),
            pl.BlockSpec((1, chunk), lambda step: (0, step)),
            pl.BlockSpec((tokens, D), lambda step: (0, 0), pipeline_mode=pl.Buffered(1)),
        ],
        out_shape=[
            shape_of((shards, steps * rows_of, D), BF),
            shape_of((D + FF, D), BF),
            shape_of((1, last - first), F32),
            shape_of((tokens, D), F32),
        ],
        scratch_shapes=[pltpu.VMEM((D, tokens), BF), pltpu.VMEM((D, tokens), BF)],
        compiler_params=pltpu.CompilerParams(vmem_limit_bytes=VMEM_LIMIT),
        name="feed_back",
        cost_estimate=cost(51),
    )(m, df, g, slope, w1, wout)


def middle_back_kernel(
    mid_ref, dm_ref, ds_ref, y_ref, o_ref, mod_ref, bias_ref, wproj_ref, gout_ref,
    dmid_ref, do_ref, dmod_ref, wproj_out_ref, bproj_ref, total, *, images
):
    step = pl.program_id(0)

    @pl.when(step == 0)
    def _():
        total[...] = jnp.zeros_like(total)
        bproj_ref[...] = jnp.zeros_like(bproj_ref)

    tokens = images * SEQ
    dy_parts = []
    for index in range(images):
        normed, inverse = norm_parts(mid_ref[index])
        dm = dm_ref[index]
        dmid = ds_ref[index] + norm_back(
            dm * (1.0 + (mod_ref[index, :, 4 * D : 5 * D] + bias_ref[B_ADA + 4 : B_ADA + 5, :])), normed, inverse
        )
        dmid_ref[index] = dmid
        dmod_ref[index, :, :D] = jnp.sum(dmid * y_ref[index].astype(F32), 0, keepdims=True)
        dmod_ref[index, :, D : 2 * D] = jnp.sum(dm, 0, keepdims=True)
        dmod_ref[index, :, 2 * D :] = jnp.sum(dm * normed, 0, keepdims=True)
        gate = mod_ref[index, :, 2 * D : 3 * D] + bias_ref[B_ADA + 2 : B_ADA + 3, :]
        dy_parts.append((dmid * gate).astype(BF))
    dy = jnp.concatenate(dy_parts, 0)
    bproj_ref[...] += jnp.sum(dy.astype(F32), 0, keepdims=True)
    do_ref[...] = dot_nt(dy, wproj_ref[...]).astype(BF).reshape(images, SEQ, D)
    total[...] += dot_tn(o_ref[...].reshape(tokens, D), dy)

    @pl.when(step == pl.num_programs(0) - 1)
    def _():
        wproj_out_ref[...] = total[...].astype(BF)


def middle_back(mid, dm, ds, y, o, mod, bias, wout, gout, images=2):
    batch = mid.shape[0]
    return pl.pallas_call(
        partial(middle_back_kernel, images=images),
        grid=(batch // images,),
        in_specs=[
            rows(images, SEQ, D),
            rows(images, SEQ, D),
            rows(images, SEQ, D),
            rows(images, SEQ, D),
            rows(images, SEQ, D),
            rows(images, 1, 8 * D),
            whole((BIASES, D)),
            whole((D, D)),
            pl.BlockSpec(memory_space=pl.ANY),
        ],
        out_specs=[
            rows(images, SEQ, D),
            rows(images, SEQ, D),
            rows(images, 1, 3 * D),
            fixed((D, D)),
            fixed((1, D)),
        ],
        out_shape=[
            shape_of((batch, SEQ, D), F32),
            shape_of((batch, SEQ, D), BF),
            shape_of((batch, 1, 3 * D), F32),
            shape_of((D + FF, D), BF),
            shape_of((1, D), F32),
        ],
        input_output_aliases={8: 3},
        scratch_shapes=[pltpu.VMEM((D, D), F32)],
        compiler_params=pltpu.CompilerParams(vmem_limit_bytes=VMEM_LIMIT),
        name="middle_back",
        cost_estimate=cost(18),
    )(mid, dm, ds, y, o, mod, bias, wout, gout)


def attend_back_kernel(qkv_ref, do_ref, a_ref, dqkv_ref, wqkv_ref, bqkv_ref, total, *, images):
    step = pl.program_id(0)

    @pl.when(step == 0)
    def _():
        total[...] = jnp.zeros_like(total)
        bqkv_ref[...] = jnp.zeros_like(bqkv_ref)

    masks = head_masks()
    tokens = images * SEQ

    def image(index, carry):
        for pair in range(PAIRS):
            base = pair * PAIR
            queries = qkv_ref[index, :, base : base + PAIR] * jnp.asarray(HDIM**-0.5, BF)
            keys = qkv_ref[index, :, D + base : D + base + PAIR]
            values = qkv_ref[index, :, 2 * D + base : 2 * D + base + PAIR]
            grads = do_ref[index, :, base : base + PAIR]
            zeros = jnp.zeros_like(queries)
            dq, dk, dv = 0.0, 0.0, 0.0
            for mask in masks:
                part_q = jnp.where(mask, queries, zeros)
                part_g = jnp.where(mask, grads, zeros)
                part_k = jnp.where(mask, keys * jnp.asarray(HDIM**-0.5, BF), zeros)
                scores = dot_nt(keys, part_q)
                power = jnp.exp(scores - jnp.max(scores, 0, keepdims=True))
                prob = power * (1.0 / jnp.sum(power, 0, keepdims=True))
                dprob = dot_nt(values, part_g)
                delta = jnp.sum(prob * dprob, 0, keepdims=True)
                dscore = (prob * (dprob - delta)).astype(BF)
                dv = dv + dot(prob.astype(BF), part_g)
                dk = dk + dot(dscore, part_q)
                dq = dq + dot_tn(dscore, part_k)
            dqkv_ref[index, :, base : base + PAIR] = dq.astype(BF)
            dqkv_ref[index, :, D + base : D + base + PAIR] = dk.astype(BF)
            dqkv_ref[index, :, 2 * D + base : 2 * D + base + PAIR] = dv.astype(BF)
        return carry

    lax.fori_loop(0, images, image, 0)
    dqkv = dqkv_ref[...].reshape(tokens, 3 * D)
    total[...] += dot_tn(a_ref[...].reshape(tokens, D), dqkv)
    bqkv_ref[...] += jnp.sum(dqkv.astype(F32), 0, keepdims=True)

    @pl.when(step == pl.num_programs(0) - 1)
    def _():
        for part in range(3):
            width = wqkv_ref.shape[1] // 3
            wqkv_ref[:, part * width : (part + 1) * width, :] = (
                total[:, part * D : (part + 1) * D].astype(BF).reshape(wqkv_ref.shape[0], width, D)
            )


def attend_back(qkv, do, a, shards, images=2):
    batch = qkv.shape[0]
    return pl.pallas_call(
        partial(attend_back_kernel, images=images),
        grid=(batch // images,),
        in_specs=[rows(images, SEQ, 3 * D), rows(images, SEQ, D), rows(images, SEQ, D)],
        out_specs=[rows(images, SEQ, 3 * D), fixed((shards, 3 * D // shards, D)), fixed((1, 3 * D))],
        out_shape=[
            shape_of((batch, SEQ, 3 * D), BF),
            shape_of((shards, 3 * D // shards, D), BF),
            shape_of((1, 3 * D), F32),
        ],
        scratch_shapes=[pltpu.VMEM((D, 3 * D), F32)],
        compiler_params=pltpu.CompilerParams(vmem_limit_bytes=VMEM_LIMIT),
        name="attend_back",
        cost_estimate=cost(45),
    )(qkv, do, a)


def stream_back_kernel(
    spot_ref, dqkv_ref, dmid_ref, noisy_ref, pos_ref, wpatch_ref, mod_ref, bias_ref, wqkv_ref,
    dmod_ref, near_ref, far_ref, bpatch_ref, wpatch_out_ref, order, *, images
):
    step = pl.program_id(0)

    @pl.when(step == 0)
    def _():
        wpatch_out_ref[...] = jnp.zeros_like(wpatch_out_ref)
        bpatch_ref[...] = jnp.zeros_like(bpatch_ref)

    tokens = images * SEQ
    dqkv = dqkv_ref[...].reshape(tokens, 3 * D)
    da = sum(dot_nt(dqkv[:, part * D : (part + 1) * D], part_of(wqkv_ref, part, 3)) for part in range(3))
    for index in range(images):
        noisy = noisy_ref[index]
        stream = dot(noisy, wpatch_ref[...]) + (pos_ref[...] + bias_ref[B_PATCH : B_PATCH + 1, :])
        scale = 1.0 + (mod_ref[index, :, D : 2 * D] + bias_ref[B_ADA + 1 : B_ADA + 2, :])
        normed, inverse = norm_parts(stream)
        part = da[index * SEQ : (index + 1) * SEQ]
        dmod_ref[index, :, :D] = jnp.sum(part, 0, keepdims=True)
        dmod_ref[index, :, D:] = jnp.sum(part * normed, 0, keepdims=True)
        dstream = dmid_ref[index] + norm_back(part * scale, normed, inverse)
        embedded = dstream.astype(BF)
        bpatch_ref[...] += jnp.sum(embedded.astype(F32), 0, keepdims=True)
        wpatch_out_ref[...] += dot_tn(noisy, embedded)

    width = near_ref.shape[2]
    shards = D // width

    @pl.when(step == pl.num_programs(0) - 1)
    def _():
        for place_of in range(shards):
            order[place_of] = wpatch_out_ref[:, place_of * width : (place_of + 1) * width]
        for entry in range(shards):
            (far_ref if entry % 2 else near_ref)[entry // 2] = order[spot_ref[0] ^ entry]


def stream_back(spot, dqkv, dmid, noisy, pos, wpatch, mod, bias, wqkv, images=2):
    batch = dqkv.shape[0]
    half = (wqkv.shape[0] // 2, PATCH, D // wqkv.shape[0])
    return pl.pallas_call(
        partial(stream_back_kernel, images=images),
        grid=(batch // images,),
        in_specs=[
            pl.BlockSpec(memory_space=pltpu.SMEM),
            rows(images, SEQ, 3 * D),
            rows(images, SEQ, D),
            rows(images, SEQ, PATCH),
            whole((SEQ, D)),
            whole((PATCH, D)),
            rows(images, 1, 8 * D),
            whole((BIASES, D)),
            whole(wqkv.shape),
        ],
        out_specs=[rows(images, 1, 2 * D), fixed(half), fixed(half), fixed((1, D))],
        out_shape=[
            shape_of((batch, 1, 2 * D), F32),
            shape_of(half, F32),
            shape_of(half, F32),
            shape_of((1, D), F32),
        ],
        scratch_shapes=[pltpu.VMEM((PATCH, D), F32), pltpu.VMEM((2 * half[0],) + half[1:], F32)],
        compiler_params=pltpu.CompilerParams(vmem_limit_bytes=VMEM_LIMIT),
        name="stream_back",
        cost_estimate=cost(19),
    )(spot, dqkv, dmid, noisy, pos, wpatch, mod, bias, wqkv)


MARKS = 4
PATCH_ROW = TFREQ
BIAS_ROW = TFREQ + PATCH
MESSAGE = 304


def condition_kernel(spot_ref, near_ref, other_ref, times_ref, embed_ref, table_ref, *rest, team):
    me = spot_ref[0]
    width = embed_ref.shape[1]
    shards = D // width
    messages = [(other_ref if entry % 2 else near_ref).at[entry // 2] for entry in range(shards)]
    if team:
        in_ref, final_ref, time_pre_ref, condition_ref, marks_ref, wpatch_ref, bias_ref = rest[:7]
        near_mod_ref, far_mod_ref, table, bias_rows, order = rest[7:]
        batch = near_mod_ref.shape[1]
        marks = jnp.concatenate(
            [message[:batch, width : width + MARKS].astype(F32) for message in messages], 0
        )
        marks_ref[...] = marks
    else:
        groups_marks, (marks_ref, features_ref, time_act_ref, act_ref, table, bias_rows, order) = rest[:-7], rest[-7:]
        team_count = groups_marks[0].shape[0]
        for entry, part in enumerate(groups_marks):
            start = pl.multiple_of((spot_ref[1] ^ entry) * team_count, team_count)
            marks_ref[pl.ds(start, team_count), :] = part[...]
        marks = marks_ref[...]
    count = marks.shape[0]
    marks = marks.astype(jnp.int32)
    index = marks[:, 0:1] * 32 + marks[:, 1:2]
    label = marks[:, 2:3] * 32 + marks[:, 3:4]

    for entry in range(shards):
        bias_rows[me ^ entry] = messages[entry][BIAS_ROW : BIAS_ROW + BIASES, :width].astype(F32)
        if team:
            order[me ^ entry] = messages[entry][PATCH_ROW : PATCH_ROW + PATCH, :width]

    def bias_row(row):
        return bias_rows[lax.div(row, BIASES), pl.ds(lax.rem(row, BIASES), 1), :]

    entry = lax.broadcasted_iota(jnp.int32, (count, times_ref.shape[1]), 1)
    moment = jnp.sum(jnp.where(entry == index, times_ref[...], 0.0), 1, keepdims=True)
    half = TFREQ // 2
    frequency = lax.broadcasted_iota(jnp.int32, (1, half), 1).astype(F32)
    angles = moment * jnp.exp(-math.log(10000.0) * frequency / half)
    features = jnp.concatenate([jnp.cos(angles), jnp.sin(angles)], 1).astype(BF)
    table[...] = jnp.zeros_like(table)
    table[:, :NCLASS] = table_ref[...].astype(BF)
    entry = lax.broadcasted_iota(jnp.int32, (count, table.shape[1]), 1)
    onehot = (entry == label).astype(F32).astype(BF)
    condition = dot_nt(onehot, table[...]) + bias_row(B_CLASS * shards + me)
    for entry in range(shards):
        place_of = me ^ entry
        time_pre = dot(features, messages[entry][:TFREQ, :width])
        time_pre = time_pre + bias_row(B_TIME * shards + place_of)
        time_act = (time_pre * (1.0 / (1.0 + jnp.exp(-time_pre)))).astype(BF)
        start = pl.multiple_of(TFREQ + PATCH + place_of * width, 16)
        condition = condition + dot(time_act, embed_ref[pl.ds(start, width), :])
        if team:
            if entry == 0:
                for block in range(shards):
                    time_pre_ref[me ^ block] = time_pre[block * batch : (block + 1) * batch, :]
        else:
            time_act_ref[place_of] = time_act
    act = (condition * (1.0 / (1.0 + jnp.exp(-condition)))).astype(BF)
    if not team:
        features_ref[...] = features
        act_ref[...] = act
        return
    condition_ref[...] = condition
    for place_of in range(shards):
        wpatch_ref[:, place_of * width : (place_of + 1) * width] = order[place_of]
    for row in range(BIASES):
        for column in range(shards):
            holder, inner = divmod(row * shards + column, BIASES)
            bias_ref[row : row + 1, column * width : (column + 1) * width] = bias_rows[
                holder, inner : inner + 1, :
            ]
    part = jnp.concatenate([dot(act, in_ref[0].astype(BF)), dot(act, final_ref[...].astype(BF))], 1)
    for pair in range(shards // 2):
        row = 2 * pair * batch
        near_mod_ref[pair] = part[row : row + batch, :]
        far_mod_ref[pair] = part[row + batch : row + 2 * batch, :]


def condition_call(operands, in_specs, out_shape, width, team):
    shards = D // width
    return pl.pallas_call(
        partial(condition_kernel, team=team),
        grid=(1,),
        in_specs=[pl.BlockSpec(memory_space=pltpu.SMEM)] + in_specs,
        out_specs=[whole(out.shape) for out in out_shape],
        out_shape=out_shape,
        scratch_shapes=[
            pltpu.VMEM((width, 1024), BF),
            pltpu.VMEM((shards, BIASES, width), F32),
            pltpu.VMEM((shards, PATCH, width), BF),
        ],
        compiler_params=pltpu.CompilerParams(vmem_limit_bytes=VMEM_LIMIT),
        name="condition",
        cost_estimate=cost(6),
    )(*operands)


def condition_of_team(spot, near, other, times, embed, table, in_mats, final, batch):
    width = embed.shape[1]
    shards = D // width
    count = shards * batch
    operands = [spot, near, other, times, embed, table, in_mats, final]
    in_specs = [whole(part.shape) for part in operands[1:6]]
    in_specs += [pl.BlockSpec((1, width, 6 * D), lambda step: (0, 0, 0)), whole(final.shape)]
    half = (shards // 2, batch)
    out_shape = [
        shape_of((shards, batch, width), F32),
        shape_of((count, width), F32),
        shape_of((count, MARKS), F32),
        shape_of((PATCH, D), BF),
        shape_of((BIASES, D), F32),
        shape_of(half + (8 * D,), F32),
        shape_of(half + (8 * D,), F32),
    ]
    return condition_call(operands, in_specs, out_shape, width, True)


def condition_of_all(spot, near, other, times, embed, table, marks):
    width = embed.shape[1]
    count = len(marks) * marks[0].shape[0]
    operands = [spot, near, other, times, embed, table] + marks
    out_shape = [
        shape_of((count, MARKS), F32),
        shape_of((count, TFREQ), BF),
        shape_of((D // width, count, width), BF),
        shape_of((count, width), BF),
    ]
    return condition_call(operands, [whole(part.shape) for part in operands[1:]], out_shape, width, False)


def condition_back_kernel(
    spot_ref, near_ref, other_ref, early_near_ref, early_other_ref, condition_ref, in_ref, final_ref, embed_ref,
    late_ref, grad_ref, near_act_ref, far_act_ref, order
):
    me = spot_ref[0]
    pairs, width = near_ref.shape[0], embed_ref.shape[1]
    late = jnp.concatenate([ref[pair] for pair in range(pairs) for ref in (near_ref, other_ref)], 0)
    late_ref[...] = late
    early = [ref[pair, 0] for pair in range(pairs) for ref in (early_near_ref, early_other_ref)]
    early = jnp.concatenate(early, 0)
    grad = dot_nt(late, in_ref[0, :, : 5 * D].astype(BF))
    grad = grad + dot_nt(early[:, :D], in_ref[0, :, 5 * D :].astype(BF))
    grad = grad + dot_nt(early[:, D:], final_ref[...].astype(BF))
    condition = condition_ref[...]
    turn = 1.0 / (1.0 + jnp.exp(-condition))
    grad = grad * (turn * (1.0 + condition * (1.0 - turn)))
    batch = order.shape[1]
    for block in range(2 * pairs):
        order[me ^ block] = grad[block * batch : (block + 1) * batch, :]
    grad = order[...].reshape(grad.shape).astype(BF)
    grad_ref[...] = grad
    for entry in range(2 * pairs):
        start = pl.multiple_of(TFREQ + PATCH + (me ^ entry) * width, 16)
        part = dot_nt(grad, embed_ref[pl.ds(start, width), :])
        (far_act_ref if entry % 2 else near_act_ref)[entry // 2] = part


def condition_back(spot, near, other, early_near, early_other, condition, in_mats, final, embed):
    width = embed.shape[1]
    count = condition.shape[0]
    operands = [spot, near, other, early_near, early_other, condition, in_mats, final, embed]
    in_specs = [pl.BlockSpec(memory_space=pltpu.SMEM)] + [whole(part.shape) for part in operands[1:6]]
    in_specs += [pl.BlockSpec((1, width, 6 * D), lambda step: (0, 0, 0)), whole(final.shape), whole(embed.shape)]
    half = (near.shape[0], count, width)
    out_shape = [
        shape_of((count, 5 * D), BF),
        shape_of((count, width), BF),
        shape_of(half, F32),
        shape_of(half, F32),
    ]
    return pl.pallas_call(
        condition_back_kernel,
        grid=(1,),
        in_specs=in_specs,
        out_specs=[whole(out.shape) for out in out_shape],
        out_shape=out_shape,
        scratch_shapes=[pltpu.VMEM((2 * half[0], near.shape[1], width), F32)],
        compiler_params=pltpu.CompilerParams(vmem_limit_bytes=VMEM_LIMIT),
        name="condition_back",
        cost_estimate=cost(4),
    )(*operands)


BIAS_PARTS = (B_PATCH, B_QUERY, B_VALUE, B_PROJ, B_UP, B_UP + 1, B_UP + 2, B_UP + 3, B_DOWN)


def condition_grads_kernel(spot_ref, marks_ref, features_ref, time_act_ref, act_ref, early_near_ref, early_other_ref, *refs, groups):
    late, last, refs = refs[:groups], refs[groups : 2 * groups], refs[2 * groups :]
    gada_ref, gembed_ref, gtable_ref, bias_ref, message_ref, squares_ref = refs[:6]
    early_all, late_all, grads_all = refs[6:]
    me, group = spot_ref[0], spot_ref[1]
    team = late[0].shape[0]
    width = act_ref.shape[1]
    shards = D // width
    for entry in range(groups):
        here = pl.ds(pl.multiple_of((group ^ entry) * team, team), team)
        early = [ref[pair, entry] for pair in range(shards // 2) for ref in (early_near_ref, early_other_ref)]
        early_all[here, :] = jnp.concatenate(early, 0)
        late_all[here, :] = late[entry][...]
        for part in range(2):
            blocks = []
            for block in range(shards):
                start = pl.multiple_of(part * team + (me ^ block) * (team // shards), 8)
                blocks.append(last[entry][pl.ds(start, team // shards), :])
            grads_all[here, part * width : (part + 1) * width] = jnp.concatenate(blocks, 0).astype(BF)
    rest = [ref[2 * team :, :] for ref in last]
    while len(rest) > 1:
        rest = [rest[i] + rest[i + 1] for i in range(0, len(rest), 2)]
    rest = rest[0]
    act = act_ref[...]
    grad_time = grads_all[:, :width]
    grad_condition = grads_all[:, width:]
    gada_ref[:, : 5 * D] = dot_tn(act, late_all[...])
    gada_ref[:, 5 * D :] = dot_tn(act, early_all[...])
    marks = marks_ref[...].astype(jnp.int32)
    label = marks[:, 2:3] * 32 + marks[:, 3:4]
    entry = lax.broadcasted_iota(jnp.int32, (marks.shape[0], 1024), 1)
    onehot = (entry == label).astype(F32).astype(BF)
    gtable_ref[...] = dot_tn(grad_condition, onehot)[:, :NCLASS]
    early_rows = PATCH + TFREQ
    gembed_ref[:, :PATCH] = rest[:PATCH, :].T
    gembed_ref[:, PATCH:early_rows] = dot_tn(grad_time, features_ref[...])
    for entry in range(shards):
        start = early_rows + entry * width
        gembed_ref[:, start : start + width] = dot_tn(grad_condition, time_act_ref[entry])
    late_sum = jnp.sum(late_all[...].astype(F32), 0, keepdims=True)
    early_sum = jnp.sum(early_all[...].astype(F32), 0, keepdims=True)
    bias_ref[B_TIME : B_ADA, :] = jnp.zeros((2, D), F32)
    for part in range(5):
        bias_ref[B_ADA + part : B_ADA + part + 1, :] = late_sum[:, part * D : (part + 1) * D]
    for part in range(3):
        row = B_FINAL + part - 1 if part else B_ADA + 5
        bias_ref[row : row + 1, :] = early_sum[:, part * D : (part + 1) * D]
    for part, row in enumerate(BIAS_PARTS):
        for column in range(shards):
            first = PATCH + part * shards + column
            bias_ref[row : row + 1, column * width : (column + 1) * width] = rest[first : first + 1, :]
    btime = jnp.sum(grads_all[...].astype(F32), 0, keepdims=True)
    message_ref[0:1, :] = btime[:, :width]
    message_ref[1:2, :] = btime[:, width:]
    tail = rest[PATCH + len(BIAS_PARTS) * shards :, :]
    message_ref[2:, :] = tail
    taken = tail.shape[0] // shards
    row = lax.broadcasted_iota(jnp.int32, tail.shape, 0) // shards + spot_ref[0] * taken
    head = jnp.where(row <= OUT, tail, 0.0)

    def square(part):
        return jnp.sum(jnp.sum(part * part, 0, keepdims=True), 1, keepdims=True)

    squares_ref[...] = square(gada_ref[...]) + square(gembed_ref[...]) + square(gtable_ref[...]) + square(btime) + square(head)


def condition_grads(spot, marks, features, time_act, act, early_near, early_other, late, last):
    groups = len(late)
    count, width = act.shape
    operands = [spot, marks, features, time_act, act, early_near, early_other] + late + last
    shards = D // width
    out_shape = [
        shape_of((width, 8 * D), F32),
        shape_of((width, PATCH + TFREQ + D), F32),
        shape_of((width, NCLASS), F32),
        shape_of((BIASES, D), F32),
        shape_of((2 + tail_rows(shards) * shards, width), F32),
        shape_of((1, 1), F32),
    ]
    return pl.pallas_call(
        partial(condition_grads_kernel, groups=groups),
        grid=(1,),
        in_specs=[pl.BlockSpec(memory_space=pltpu.SMEM)] + [whole(part.shape) for part in operands[1:]],
        out_specs=[whole(out.shape) for out in out_shape],
        out_shape=out_shape,
        scratch_shapes=[
            pltpu.VMEM((count, 3 * D), BF),
            pltpu.VMEM((count, 5 * D), BF),
            pltpu.VMEM((count, 2 * width), BF),
        ],
        compiler_params=pltpu.CompilerParams(vmem_limit_bytes=VMEM_LIMIT),
        name="condition_grads",
        cost_estimate=cost(6),
    )(*operands)


def swap(array_in, axis, hop):
    count = lax.axis_size(axis)
    return lax.ppermute(array_in, axis, [(place_of, place_of ^ hop) for place_of in range(count)])


def spread(array_in, axis):
    count = lax.axis_size(axis)
    if axis == "shard":
        near = jnp.stack([array_in] + [swap(array_in, axis, hop) for hop in range(2, count, 2)])
        return jnp.stack([near, swap(near, axis, 1)], 1).reshape((count,) + array_in.shape)
    return jnp.stack([array_in] + [swap(array_in, axis, hop) for hop in range(1, count)])


def total_of(parts):
    while len(parts) > 1:
        parts = [parts[i] + parts[i + 1] for i in range(0, len(parts), 2)]
    return parts[0]


def exchange_sum(near):
    return total_of([near[0]] + [swap(near[hop], "shard", 2 * hop) for hop in range(1, near.shape[0])])


def from_groups(array_in, tuned, first=1):
    count = lax.axis_size("grp")
    if tuned:
        pair = jnp.stack([array_in, swap(array_in, "grp", first)])
        far = swap(pair, "grp", 3 - first)
        parts = [pair[0], pair[1], far[0], far[1]]
        return parts if first == 1 else [parts[0], parts[2], parts[1], parts[3]]
    parts = jnp.broadcast_to(array_in[None], (count,) + array_in.shape)
    parts = ordered(lax.all_to_all(parts, "grp", 0, 0, tiled=True), "grp")
    return [parts[i] for i in range(count)]


def ordered(array_in, axis):
    count = lax.axis_size(axis)
    place_of = lax.axis_index(axis)
    bit = 1
    while bit < count:
        pairs = array_in.reshape((count // (2 * bit), 2, bit) + array_in.shape[1:])
        array_in = jnp.where(place_of & bit != 0, pairs[:, ::-1], pairs).reshape(array_in.shape)
        bit *= 2
    return array_in


def sum_spread(array_in, axis):
    parts = spread(array_in, axis)
    return total_of([parts[i] for i in range(parts.shape[0])])


def tie(arrays, after):
    return lax.optimization_barrier((arrays, after))[0]


def rows_near(own):
    rows_all = own.shape[0]
    quarter = -(-rows_all // 64) * 16
    group = lax.axis_index("grp")
    start = jnp.where(group == 3, rows_all - quarter, group * quarter)
    part = lax.dynamic_slice_in_dim(own, start, quarter, 0)
    return [swap(part, "shard", hop) for hop in (2, 4, 6)]


def rows_far(near):
    return lax.all_gather(jnp.stack(near), "grp")


def rows_all(own, far):
    return [own, far, swap(own, "shard", 1), swap(far, "shard", 1)]


def quarter_start(rows_all, quarter, group):
    return jnp.where(group == 3, rows_all - quarter, group * quarter)


def cores_summed(grads):
    pairs = grads.reshape((4, 2) + grads.shape[1:])
    core = lax.axis_index("shard") % 2
    theirs = lax.dynamic_index_in_dim(pairs, 1 - core, 1, keepdims=False)
    mine = lax.dynamic_index_in_dim(pairs, core, 1, keepdims=False)
    return lower(mine.astype(F32) + swap(theirs, "shard", 1).astype(F32))


def groups_traded(grads):
    group = lax.axis_index("grp")
    rows_all = grads.shape[1]
    quarter = -(-rows_all // 64) * 16
    parts = []
    for hop in range(4):
        start = quarter_start(rows_all, quarter, group ^ hop)
        part = lax.dynamic_slice_in_dim(grads, start, quarter, 1)
        parts.append(swap(part, "grp", hop) if hop else part)
    return parts


def shards_traded(parts):
    return chips_traded(total_of([part.astype(F32) for part in parts]))


def chips_traded(total):
    low = lower(total)
    chip = lax.axis_index("shard") // 2
    own = lax.dynamic_index_in_dim(total, chip, 0, keepdims=False)
    return [own] + [
        swap(lax.dynamic_index_in_dim(low, chip ^ hop, 0, keepdims=False), "shard", 2 * hop) for hop in (1, 2, 3)
    ]


def shards_summed(parts):
    return lower(total_of([part.astype(F32) for part in parts]))


def quarters_joined(parts, *sizes):
    joined, first = [], 0
    for quarter, count in sizes:
        part = parts[:, first : first + quarter]
        first += quarter
        skipped = 4 * quarter - count // 8
        joined.append(jnp.concatenate([part[0], part[1], part[2], part[3, skipped:]]).astype(F32))
    return joined


def halves_added(part, bit):
    axis = part.ndim - 2
    half = part.shape[axis] // 2
    side = (lax.axis_index("grp") // bit) % 2
    ours = lax.dynamic_slice_in_dim(part, side * half, half, axis)
    theirs = lax.dynamic_slice_in_dim(part, (1 - side) * half, half, axis)
    return [ours, swap(theirs, "grp", bit)]


def matmul(formula, left, right):
    return jnp.einsum(formula, left, right, preferred_element_type=F32)


def lower(array_in):
    return array_in.astype(BF)


def summed(array_in, axes):
    return jnp.sum(array_in.astype(F32), axes)


def position_table():
    quarter = D // 4
    angular = np.exp(-math.log(10000.0) * np.arange(quarter) / quarter)
    position = np.arange(GRID * GRID)
    column = (position % GRID)[:, None] * angular
    row_pos = (position // GRID)[:, None] * angular
    table = np.concatenate([np.sin(column), np.cos(column), np.sin(row_pos), np.cos(row_pos)], 1)
    return jnp.asarray(table.astype(np.float32))


def pick_times(time_index, times):
    matches = time_index[:, None] == jnp.arange(times.shape[0], dtype=jnp.int32)[None, :]
    return jnp.sum(jnp.where(matches, times[None, :], 0.0), 1)


def condition_grads_plain(spot, marks, features, time_act, act, early_near, early_other, late, last):
    team, width = late[0].shape[0], act.shape[1]
    shards = D // width

    def in_exchange(part):
        part = part.reshape(2, shards, team // shards, width).transpose(1, 0, 2, 3)
        return ordered(part, "shard").transpose(1, 0, 2, 3).reshape(2 * team, width)

    early = jnp.stack([early_near, early_other], 1).transpose(2, 0, 1, 3, 4)
    early = early.reshape(len(late), team, 3 * D)
    early, late, last_all = [
        ordered(jnp.stack(parts), "grp").reshape(-1, parts[0].shape[1])
        for parts in (list(early), late, [in_exchange(part[: 2 * team]) for part in last])
    ]
    last_all = lower(last_all).reshape(-1, 2, team, width)
    grad_time, grad_condition = last_all[:, 0].reshape(-1, width), last_all[:, 1].reshape(-1, width)
    rest = total_of([part[2 * team :] for part in last])
    gada = jnp.concatenate([matmul("bd,be->de", act, late), matmul("bd,be->de", act, early)], 1)
    labels = (marks[:, 2:3] * 32.0 + marks[:, 3:4]).astype(jnp.int32)
    onehot = lower((labels == jnp.arange(NCLASS, dtype=jnp.int32)[None, :]).astype(F32))
    gtable = matmul("bd,bn->dn", grad_condition, onehot)
    gembed = jnp.concatenate(
        [
            rest[:PATCH].T,
            matmul("bd,bf->df", grad_time, features),
            matmul("be,sbd->esd", grad_condition, time_act).reshape(width, D),
        ],
        1,
    )
    bias = jnp.zeros((BIASES, D), F32)
    bias = bias.at[B_ADA : B_ADA + 5].set(summed(late, 0).reshape(5, D))
    early_sum = summed(early, 0).reshape(3, D)
    bias = bias.at[B_ADA + 5].set(early_sum[0]).at[B_FINAL:].set(early_sum[1:])
    parts = rest[PATCH : PATCH + len(BIAS_PARTS) * shards].reshape(len(BIAS_PARTS), D)
    for part, row in enumerate(BIAS_PARTS):
        bias = bias.at[row].set(parts[part])
    btime = jnp.stack([summed(grad_time, 0), summed(grad_condition, 0)])
    tail = rest[PATCH + len(BIAS_PARTS) * shards :]
    taken = tail.shape[0] // shards
    row = jnp.arange(tail.shape[0], dtype=jnp.int32)[:, None] // shards + spot[0] * taken
    head = jnp.where(row <= OUT, tail, 0.0)
    squares = sum(jnp.sum(part * part) for part in (gada, gembed, gtable, btime, head))
    return gada, gembed, gtable, bias, jnp.concatenate([btime, tail]), squares.reshape(1, 1)


def adamw(weight, moment_one, moment_two, gradient, factor):
    gradient = gradient * factor
    moment_one = BETA_ONE * moment_one + (1.0 - BETA_ONE) * gradient
    moment_two = BETA_TWO * moment_two + (1.0 - BETA_TWO) * gradient * gradient
    fix_one = 1.0 - BETA_ONE**STEP
    fix_two = 1.0 - BETA_TWO**STEP
    update = (
        moment_one / fix_one / (jnp.sqrt(moment_two / fix_two) + EPS_ADAM) + WEIGHT_DECAY * weight
    )
    return (weight - LEARN_RATE * update, moment_one, moment_two)


def per_device(
    latents, noise, velocity, labels, time_index, times,
    in_mats, out_mats, embed_mats, class_table, final_ada, head_mat, bias_vec,
    in_mats_first, out_mats_first, embed_first, table_first, final_first, head_first, bias_first,
    in_mats_second, out_mats_second, embed_second, table_second, final_second, head_second, bias_second,
):
    shards = lax.axis_size("shard")
    groups = lax.axis_size("grp")
    me = lax.axis_index("shard")
    mine = lax.axis_index("grp")
    batch = latents.shape[0]
    width = embed_mats.shape[1]
    team = shards * batch
    tuned = groups == 4 and shards == 8

    embed_low = lower(embed_mats)
    marks = jnp.stack([time_index // 32, time_index % 32, labels // 32, labels % 32], 1).astype(BF)
    marks = jnp.pad(marks, ((0, TFREQ - batch), (0, 128 - width - MARKS)))
    message = jnp.concatenate(
        [embed_low[PATCH : PATCH + TFREQ], embed_low[:PATCH], lower(bias_vec).reshape(BIASES, width)]
    )
    message = jnp.pad(message, ((0, MESSAGE - message.shape[0]), (0, 128 - width)))
    message = message + jnp.pad(marks, ((0, MESSAGE - TFREQ), (width, 0)))
    arrived = [swap(message, "shard", hop) for hop in range(2, shards, 2)]
    near_message = jnp.stack([message] + arrived)
    other_message = swap(near_message, "shard", 1)
    in_mats_early, out_mats_early = tie((in_mats, out_mats), message)

    def rows_of(first, count):
        return [lower(in_mats_early[0, :, first + part * D : first + (part + 1) * D]) for part in range(count)]

    own_qkv = jnp.concatenate(rows_of(6 * D, 3))
    own_feed = jnp.concatenate(rows_of(9 * D, FF // D) + [lower(out_mats_early[0])])
    spot = jnp.stack([me, mine]).astype(jnp.int32)
    if tuned:
        near_qkv = rows_near(own_qkv)
        near_feed = rows_near(own_feed)
    else:
        qkv_pieces, feed_pieces = [[lax.all_gather(own, "shard")] for own in (own_qkv, own_feed)]
    times_row = jnp.pad(times, (0, -times.shape[0] % 128))[None]
    time_pre, condition, marks_team, wpatch, biases, near_mod, far_mod = condition_of_team(
        spot, near_message, other_message, times_row, embed_low, class_table.T, in_mats, final_ada, batch
    )
    if tuned:
        far_qkv = rows_far(tie(near_qkv, time_pre))
        far_feed = rows_far(tie(near_feed, far_qkv))
    near_mod = near_mod + swap(far_mod, "shard", 1)
    mods = lower(near_mod)
    mods = [near_mod[0]] + [swap(mods[hop], "shard", 2 * hop) for hop in range(1, shards // 2)]
    mod = total_of([part.astype(F32) for part in mods])[:, None, :]
    latents, noise, velocity, head_mat_late, marks_team = tie(
        (latents, noise, velocity, head_mat, marks_team), near_mod
    )
    if tuned:
        far_qkv = tie(far_qkv, near_mod)
        qkv_pieces = rows_all(own_qkv, far_qkv)
    marks_all = from_groups(marks_team, tuned)
    moment = pick_times(time_index, times)
    noisy = lower((1.0 - moment)[:, None, None] * latents + moment[:, None, None] * noise)
    pos = position_table()
    a, qkv, o, wqkv = attend(spot, noisy, pos, wpatch, mod, biases, qkv_pieces, shards)
    if tuned:
        o, far_feed, marks_all = lax.optimization_barrier((o, far_feed, marks_all))
        feed_pieces = rows_all(tie(own_feed, o), far_feed)
    marks_all, features, time_act, cond_act_all = condition_of_all(
        spot, near_message, other_message, times_row, embed_low, class_table.T, marks_all
    )
    mod = tie(mod, features)
    count_all = float(groups * shards * batch * SEQ * OUT)
    head_low = lower(head_mat_late)
    mid, y, m, g, slope, df, ds, dmod_feed, near_tail, far_tail, bdown, wup, wout = feed(
        spot, moment, noisy, pos, wpatch, o, mod, biases, head_low[:D],
        head_low[D:].astype(F32), velocity, feed_pieces, shards, count_all,
    )
    wout = wout.reshape(D + FF, D)
    tokens = batch * SEQ
    early = lower(dmod_feed[:, 0])
    early = [early] + [swap(early, "grp", hop) for hop in range(1, groups)] if tuned else from_groups(early, tuned)
    gup, gout, bup, dm = feed_back(
        m.reshape(tokens, D), df.reshape(tokens, D), g, slope, wup, wout, 0, FF
    )
    gup, gout, bup, dm, early = lax.optimization_barrier((gup, gout, bup, dm, early))
    gup = lax.psum_scatter(gup, "shard", scatter_dimension=0)
    early = jnp.stack(early)
    early_far = [swap(early, "shard", hop) for hop in range(2, shards, 2)]
    dmid, do, dmod_mid, gout, bproj = middle_back(
        mid, dm.reshape(batch, SEQ, D), tie(ds, early), y, o, mod, biases, wout, gout
    )

    dmid, do, dmod_mid, gout, bproj, early, early_far = lax.optimization_barrier(
        (dmid, do, dmod_mid, gout, bproj, early, early_far)
    )

    gout = gout.reshape(shards, (D + FF) // shards, D)
    if tuned:
        gout = cores_summed(gout)
        early_near = jnp.stack([early] + early_far)
        near_tail, far_tail = [part.reshape(shards // 2, -1, width) for part in tie((near_tail, far_tail), dmid)]
        do = tie(do, (gout, early_near, near_tail, far_tail))
        gout_parts = groups_traded(gout)
    else:
        near_tail, far_tail = [part.reshape(shards // 2, -1, width) for part in (near_tail, far_tail)]
        early_near = jnp.stack([early] + early_far)
        gout = lax.psum_scatter(gout, "shard", scatter_dimension=0)
    early_other = swap(early_near, "shard", 1)
    dqkv, gqkv, bqkv = attend_back(qkv, do, a, shards)
    if tuned:
        dqkv, gqkv, bqkv, gout_parts, early_other = lax.optimization_barrier(
            (dqkv, gqkv, bqkv, gout_parts, early_other)
        )
    if tuned:
        gqkv = halves_added(cores_summed(gqkv), 2)
        gout_parts = shards_traded(gout_parts)
        dmid, dmod_mid, gup, bqkv, bproj, bup, bdown = tie(
            (dmid, dmod_mid, gup, bqkv, bproj, bup, bdown), gout_parts[0]
        )
        gup = halves_added(gup, 2)
    else:
        gqkv = lax.psum_scatter(gqkv, "shard", scatter_dimension=0)
    dmod_attn, near_patch, far_patch, bpatch = stream_back(
        spot, dqkv, dmid, noisy, pos, wpatch, mod, biases, wqkv
    )
    if tuned:
        dmod_attn, near_patch, far_patch, bpatch, gup, gout_parts, gqkv = lax.optimization_barrier(
            (dmod_attn, near_patch, far_patch, bpatch, gup, gout_parts, gqkv)
        )
        gup, gout = shards_summed(gup), shards_summed(gout_parts)
        gqkv = halves_added(shards_summed(gqkv), 1)
    late = lower(jnp.concatenate([dmod_attn[:, 0], dmod_mid[:, 0]], 1))

    near_late = jnp.stack([late] + [swap(late, "shard", hop) for hop in range(2, shards, 2)])
    other_late = swap(near_late, "shard", 1)
    if tuned:
        gup, other_late, gqkv = tie((gup, other_late, gqkv), gout)
        gqkv = shards_traded(gqkv)
    late, grad_condition, near_act, far_act = condition_back(
        spot, near_late, other_late, early_near, early_other, condition, in_mats, final_ada, embed_low
    )
    bias_part = jnp.concatenate([bpatch, bqkv[:, :D], bqkv[:, 2 * D :], bproj, bup, bdown], 1)
    bias_part = jnp.broadcast_to(bias_part.reshape(1, -1, width), (shards // 2, len(BIAS_PARTS) * shards, width))

    far_act = jnp.concatenate([far_act, far_patch, bias_part, far_tail], 1)
    near_act = jnp.concatenate([near_act, near_patch, bias_part, near_tail], 1)
    near_act = near_act + swap(far_act, "shard", 1)
    acts = [near_act[0]] + [swap(near_act[hop], "shard", 2 * hop) for hop in range(1, near_act.shape[0])]

    def last_of(acts):
        act_part = total_of(acts)
        unused, time_pull = jax.vjp(jax.nn.silu, time_pre)
        grad_time = lower(time_pull(act_part[:team].reshape(time_pre.shape))[0]).reshape(team, width)
        return jnp.concatenate([grad_time.astype(F32), grad_condition.astype(F32), act_part[team:]])

    if tuned:
        gup, late_x, late_y = halves_added(gup, 1), swap(late, "grp", 1), swap(late, "grp", 2)
        acts, gup, late_x, late_y, gqkv = lax.optimization_barrier((acts, gup, late_x, late_y, gqkv))
        last = last_of(acts)
        both = jnp.concatenate([shards_summed(gup), gout, shards_summed(gqkv)])
        last_x, late_xy, both_y = swap(last, "grp", 1), swap(late_x, "grp", 2), swap(both, "grp", 2)
        last_x, late_xy, both_y = lax.optimization_barrier((last_x, late_xy, both_y))
        pair = jnp.stack([last, last_x])
        both = jnp.stack([both, both_y])
        last_far, both_far = swap(pair, "grp", 2), swap(both, "grp", 1)
        grads_last = [last, last_x, last_far[0], last_far[1]]
        grads_late = [late, late_x, late_y, late_xy]
        both = ordered(jnp.stack([both[0], both_far[0], both[1], both_far[1]]), "grp")
        gup, gout, gqkv = quarters_joined(both, (gup[0].shape[0], FF), (gout.shape[0], D + FF), (gqkv[0].shape[0], 3 * D))
        gfeed = [gup, gout]
    else:
        grads_last = from_groups(last_of(acts), tuned)
        grads_late = from_groups(late, tuned)
        gup, gout, gqkv = [
            total_of([part.astype(F32) for part in from_groups(grads, tuned)]) for grads in (gup, gout, gqkv)
        ]
        gfeed = [gup, gout]
    grads_of = condition_grads if tuned else condition_grads_plain
    gada, gembed, gtable, bias_grad, message, squares = grads_of(
        spot, marks_all, features, time_act, cond_act_all, early_near, early_other, grads_late, grads_last
    )
    gup, gout = gfeed
    share = bias_vec.shape[0]
    bias_grad = lax.dynamic_slice_in_dim(bias_grad.reshape(-1), me * share, share, 0)
    squares = squares + sum(jnp.sum(part * part) for part in (gup, gqkv, gout, bias_grad))
    message = jnp.concatenate([message, jnp.broadcast_to(squares, (6, width))])
    final = spread(message, "shard")
    grad_norm = jnp.sqrt(total_of([final[i, -1, 0] for i in range(shards)]))
    factor = CLIP_NORM / jnp.maximum(grad_norm, CLIP_NORM)
    final = ordered(final, "shard")
    btime = jnp.concatenate([final[:, 0].reshape(-1), final[:, 1].reshape(-1)])
    tail = final[:, 2:-6].reshape(-1, D)
    head_grad = jnp.concatenate([tail[:OUT].T, tail[OUT : OUT + 1, :OUT]])
    loss_sum = tail[OUT + 1, 0]
    btime = jnp.concatenate([jnp.zeros((D,), F32), btime, jnp.zeros((12 * D + FF,), F32)])
    bias_grad = bias_grad + lax.dynamic_slice_in_dim(btime, me * share, share, 0)
    in_grad = jnp.concatenate(
        [gada[:, : 6 * D]]
        + [gqkv[part * width : (part + 1) * width] for part in range(3)]
        + [gup[part * width : (part + 1) * width] for part in range(FF // D)],
        1,
    )
    weights = (in_mats, out_mats, embed_mats, class_table, final_ada, head_mat, bias_vec)
    firsts = (in_mats_first, out_mats_first, embed_first, table_first, final_first, head_first, bias_first)
    seconds = (
        in_mats_second, out_mats_second, embed_second, table_second, final_second, head_second, bias_second
    )
    grads = (in_grad[None], gout[None], gembed.T, gtable.T, gada[:, 6 * D :], head_grad, bias_grad)
    stepped = [
        adamw(weight, moment_one, moment_two, gradient, factor)
        for weight, moment_one, moment_two, gradient in zip(weights, firsts, seconds, grads)
    ]
    return tuple(part[0] for part in stepped) + tuple(part[1] for part in stepped) + tuple(
        part[2] for part in stepped
    ) + (loss_sum, grad_norm)


def solution(mesh):
    images = P(("grp", "shard"))
    placed = (
        P(None, "shard", None),
        P(None, "shard", None),
        P(None, "shard"),
        P(None, "shard"),
        P("shard", None),
        P(),
        P("shard"),
    )
    return jax.shard_map(
        per_device,
        mesh=mesh,
        in_specs=(images,) * 5 + (P(),) + placed * 3,
        out_specs=placed * 3 + (P(), P()),
        check_vma=False,
    )
```

```python
import math
from functools import partial
import numpy as np
import jax
import jax.numpy as jnp
from jax import lax
from jax.sharding import PartitionSpec as P
from jax.experimental import pallas as pl
from jax.experimental.pallas import tpu as pltpu

D = 768
HEADS = 12
HDIM = 64
FF = 3072
PATCH = 16
SEQ = 256
OUT = 32
GRID = 16
STEP = 10
BETA_ONE = 0.9
BETA_TWO = 0.999
LEARN_RATE = 0.05
WEIGHT_DECAY = 0.05
EPS_ADAM = 1e-08
CLIP_NORM = 0.01
TFREQ = 256
NCLASS = 1001
EPS_NORM = 1e-06
BF = jnp.bfloat16
F32 = jnp.float32
VMEM_LIMIT = 60 * 1024 * 1024
COST = 3 * 10**8
PAIR = 2 * HDIM
PAIRS = HEADS // 2
BIASES = 19
B_PATCH, B_TIME, B_CLASS, B_ADA, B_QUERY, B_VALUE, B_PROJ, B_UP, B_DOWN, B_FINAL = 0, 1, 2, 3, 9, 10, 11, 12, 16, 17


def dot(left, right):
    return jnp.dot(left, right, preferred_element_type=F32)


def dot_nt(left, right):
    return lax.dot_general(left, right, (((1,), (1,)), ((), ())), preferred_element_type=F32)


def dot_tn(left, right):
    return lax.dot_general(left, right, (((0,), (0,)), ((), ())), preferred_element_type=F32)


def whole(shape):
    zeros = (0,) * len(shape)
    return pl.BlockSpec(shape, lambda step: zeros, pipeline_mode=pl.Buffered(1))


def fixed(shape):
    zeros = (0,) * len(shape)
    return pl.BlockSpec(shape, lambda step: zeros)


def rows(count, *rest):
    zeros = (0,) * len(rest)
    return pl.BlockSpec((count,) + rest, lambda step: (step,) + zeros)


def shape_of(shape, dtype):
    return jax.ShapeDtypeStruct(shape, dtype)


def norm_parts(array_in):
    centre = array_in - jnp.mean(array_in, -1, keepdims=True)
    inverse = lax.rsqrt(jnp.mean(centre * centre, -1, keepdims=True) + EPS_NORM)
    return centre * inverse, inverse


def norm_back(grad_normed, normed, inverse):
    first = jnp.mean(grad_normed, -1, keepdims=True)
    second = jnp.mean(grad_normed * normed, -1, keepdims=True)
    return inverse * (grad_normed - first - normed * second)


def cost(microseconds):
    return pl.CostEstimate(flops=microseconds * COST, bytes_accessed=0, transcendentals=0)


def head_masks():
    lane = lax.broadcasted_iota(jnp.int32, (1, PAIR), 1)
    return (lane < HDIM, lane >= HDIM)


def both_heads(part, masks):
    return jnp.concatenate([jnp.where(mask, part, jnp.zeros_like(part)) for mask in masks], 0)


def weight_copies(spot_ref, pieces, target, sem):
    if len(pieces) == 1:
        return [pltpu.make_async_copy(pieces[0], target, sem)]
    own, near, pair, other, *direct = pieces
    shard = spot_ref[0]
    quarter = near.shape[2]
    traded = target.shape[1] - (direct[0].shape[1] if direct else 0)
    rest = traded - 3 * quarter
    made = [
        pltpu.make_async_copy(own, target.at[shard], sem),
        pltpu.make_async_copy(pair, target.at[shard ^ 1], sem),
    ]
    for block in range(4):
        count = rest if block == 3 else quarter
        rows_here = slice(block * quarter, block * quarter + count)
        for core, part in enumerate((near, other)):
            for hop in range(3):
                source = part.at[block, hop, quarter - count :] if count < quarter else part.at[block, hop]
                slot = shard ^ (2 * hop + 2 + core)
                made.append(pltpu.make_async_copy(source, target.at[slot, rows_here], sem))
    for core, part in enumerate(direct):
        for hop in range(3):
            slot = shard ^ (2 * hop + 2 + core)
            made.append(pltpu.make_async_copy(part.at[hop], target.at[slot, traded:], sem))
    return made


def run_copies(made, start):
    for copy in made:
        copy.start() if start else copy.wait()


def part_of(weights, part, count):
    width = weights.shape[1] // count
    return weights[:, part * width : (part + 1) * width, :].reshape(D, D)


def attend_kernel(
    spot_ref, noisy_ref, pos_ref, wpatch_ref, mod_ref, bias_ref, *refs, images
):
    pieces, (a_ref, qkv_ref, o_ref, kept_ref, wqkv_ref, sem, out_sem) = refs[:-7], refs[-7:]
    step = pl.program_id(0)
    made = weight_copies(spot_ref, pieces, wqkv_ref, sem)
    keep = pltpu.make_async_copy(wqkv_ref, kept_ref, out_sem)

    @pl.when(step == 0)
    def _():
        run_copies(made, True)
        run_copies(made, False)
        keep.start()

    @pl.when(step == pl.num_programs(0) - 1)
    def _():
        keep.wait()

    masks = head_masks()

    def bias(row):
        return bias_ref[row : row + 1, :]

    def image(index, carry):
        stream = dot(noisy_ref[index], wpatch_ref[...]) + (pos_ref[...] + bias(B_PATCH))
        normed, unused = norm_parts(stream)
        scale = 1.0 + (mod_ref[index, :, D : 2 * D] + bias(B_ADA + 1))
        a = (normed * scale + (mod_ref[index, :, :D] + bias(B_ADA))).astype(BF)
        a_ref[index] = a
        for part in range(3):
            cut = slice(part * D, (part + 1) * D)
            product = dot(a, part_of(wqkv_ref, part, 3))
            if part != 1:
                product = product + bias(B_QUERY if part == 0 else B_VALUE)
            qkv_ref[index, :, cut] = product.astype(BF)
        for pair in range(PAIRS):
            base = pair * PAIR
            queries = qkv_ref[index, :, base : base + PAIR]
            keys = qkv_ref[index, :, D + base : D + base + PAIR]
            values = qkv_ref[index, :, 2 * D + base : 2 * D + base + PAIR]
            scores = dot_nt(both_heads(queries * jnp.asarray(HDIM**-0.5, BF), masks), keys)
            power = jnp.exp(scores - jnp.max(scores, -1, keepdims=True))
            total = jnp.sum(power, -1, keepdims=True)
            mixed = dot((power * (1.0 / total)).astype(BF), values)
            o_ref[index, :, base : base + PAIR] = jnp.where(masks[0], mixed[:SEQ], mixed[SEQ:]).astype(BF)
        return carry

    lax.fori_loop(0, images, image, 0)


ANYWHERE = pl.BlockSpec(memory_space=pl.ANY)


def attend(spot, noisy, pos, wpatch, mod, bias, pieces, shards, images=2):
    batch = noisy.shape[0]
    kept = (shards, 3 * D // shards, D)
    return pl.pallas_call(
        partial(attend_kernel, images=images),
        grid=(batch // images,),
        in_specs=[
            pl.BlockSpec(memory_space=pltpu.SMEM),
            rows(images, SEQ, PATCH),
            whole((SEQ, D)),
            whole((PATCH, D)),
            rows(images, 1, 8 * D),
            whole((BIASES, D)),
        ]
        + [ANYWHERE] * len(pieces),
        out_specs=[rows(images, SEQ, D), rows(images, SEQ, 3 * D), rows(images, SEQ, D), ANYWHERE],
        out_shape=[
            shape_of((batch, SEQ, D), BF),
            shape_of((batch, SEQ, 3 * D), BF),
            shape_of((batch, SEQ, D), BF),
            shape_of(kept, BF),
        ],
        scratch_shapes=[pltpu.VMEM(kept, BF), pltpu.SemaphoreType.DMA, pltpu.SemaphoreType.DMA],
        compiler_params=pltpu.CompilerParams(vmem_limit_bytes=VMEM_LIMIT),
        name="attend",
        cost_estimate=cost(32),
    )(spot, noisy, pos, wpatch, mod, bias, *pieces)


GELU_A = math.sqrt(2.0 / math.pi)
GELU_B = 0.044715


def gelu_both(u):
    square = u * u
    turn = jnp.tanh(u * (GELU_A + (GELU_A * GELU_B) * square))
    half = 0.5 + 0.5 * turn
    value = u * half
    slope = half + (value * (1.0 - half)) * (2.0 * GELU_A + (6.0 * GELU_A * GELU_B) * square)
    return value, slope


def feed_kernel(
    spot_ref, t_ref, noisy_ref, pos_ref, wpatch_ref, o_ref, mod_ref, bias_ref,
    head_ref, hbias_ref, vel_ref, *refs, images, count_all
):
    pieces, refs = refs[:-18], refs[-18:]
    mid_ref, y_ref, m_ref, g_ref, slope_ref, df_ref, ds_ref, dmod_ref, near_ref, far_ref, bdown_ref = refs[:11]
    kept1_ref, kept2_ref, weights_ref, tail_ref, order, sem, out_sem = refs[11:]
    step = pl.program_id(0)
    made = weight_copies(spot_ref, pieces, weights_ref, sem)
    up_width, out_width = kept1_ref.shape[1], kept2_ref.shape[1]
    keeps = [
        pltpu.make_async_copy(weights_ref.at[:, :up_width], kept1_ref, out_sem.at[0]),
        pltpu.make_async_copy(weights_ref.at[:, up_width:], kept2_ref, out_sem.at[1]),
    ]

    @pl.when(step == 0)
    def _():
        run_copies(made, True)
        run_copies(made, False)
        for keep in keeps:
            keep.start()

    @pl.when(step == pl.num_programs(0) - 1)
    def _():
        for keep in keeps:
            keep.wait()

    @pl.when(step == 0)
    def _():
        tail_ref[...] = jnp.zeros_like(tail_ref)
        bdown_ref[...] = jnp.zeros_like(bdown_ref)

    tokens = images * SEQ

    def bias(row):
        return bias_ref[row : row + 1, :]

    def spread(part):
        parts = []
        for index in range(images):
            row = mod_ref[index, :, (part + 2) * D : (part + 3) * D]
            row = row + bias(B_ADA + 2 + part if part < 4 else B_FINAL + part - 4)
            parts.append(jnp.broadcast_to(row, (SEQ, D)))
        return jnp.concatenate(parts, 0)

    def up_part(part):
        rows_of = up_width * D // FF
        return weights_ref[:, part * rows_of : (part + 1) * rows_of, :].reshape(D, D)

    def out_rows(part):
        first, taken = part * D, []
        while first < (part + 1) * D:
            place_of, row = first // out_width, first % out_width
            count = min(out_width - row, (part + 1) * D - first)
            taken.append(weights_ref[place_of, up_width + row : up_width + row + count, :])
            first += count
        return jnp.concatenate(taken, 0)

    position = jnp.concatenate([pos_ref[...] + bias(B_PATCH)] * images, 0)
    stream = dot(noisy_ref[...].reshape(tokens, PATCH), wpatch_ref[...]) + position
    y = dot(o_ref[...].reshape(tokens, D), out_rows(0)) + bias(B_PROJ)
    y_ref[...] = y.astype(BF).reshape(images, SEQ, D)
    mid = stream + spread(0) * y
    mid_ref[...] = mid.reshape(images, SEQ, D)
    normed, unused = norm_parts(mid)
    m = (normed * (1.0 + spread(2)) + spread(1)).astype(BF)
    m_ref[...] = m.reshape(images, SEQ, D)
    feed = jnp.broadcast_to(bias(B_DOWN), (tokens, D))
    for j in range(FF // D):
        cut = slice(j * D, (j + 1) * D)
        g, slope = gelu_both(dot(m, up_part(j)) + bias(B_UP + j))
        g = g.astype(BF)
        g_ref[:, cut] = g
        slope_ref[:, cut] = slope.astype(BF)
        feed = feed + dot(g, out_rows(j + 1))
    gate = spread(3)
    stream = mid + gate * feed
    normed, inverse = norm_parts(stream)
    scale = 1.0 + spread(5)
    z = (normed * scale + spread(4)).astype(BF)
    predicted = dot(z, head_ref[...]) + hbias_ref[...]
    t = jnp.concatenate(
        [jnp.full((SEQ, 1), t_ref[step * images + index], F32) for index in range(images)], 0
    )
    residual = predicted - vel_ref[...].reshape(tokens, OUT)
    weighted = t * residual
    loss = jnp.sum(jnp.sum(weighted * residual, 0, keepdims=True), 1, keepdims=True)
    tail_ref[OUT + 1 : OUT + 2, :] += jnp.broadcast_to(loss, (1, D))
    grad_pred = (2.0 * weighted / count_all).astype(BF)
    tail_ref[OUT : OUT + 1, :OUT] += jnp.sum(grad_pred.astype(F32), 0, keepdims=True)
    tail_ref[:OUT, :] += dot_tn(grad_pred, z)
    dz = dot_nt(grad_pred, head_ref[...])
    ds = norm_back(dz * scale, normed, inverse)
    ds_ref[...] = ds.reshape(images, SEQ, D)
    df = (ds * gate).astype(BF)
    df_ref[...] = df.reshape(images, SEQ, D)
    bdown_ref[...] += jnp.sum(df.astype(F32), 0, keepdims=True)
    for index in range(images):
        cut = slice(index * SEQ, (index + 1) * SEQ)
        dmod_ref[index, :, :D] = jnp.sum(ds[cut] * feed[cut], 0, keepdims=True)
        dmod_ref[index, :, D : 2 * D] = jnp.sum(dz[cut], 0, keepdims=True)
        dmod_ref[index, :, 2 * D :] = jnp.sum(dz[cut] * normed[cut], 0, keepdims=True)

    shards, taken = 2 * near_ref.shape[0], near_ref.shape[1]

    @pl.when(step == pl.num_programs(0) - 1)
    def _():
        for place_of in range(shards):
            order[place_of] = tail_ref[place_of * taken : (place_of + 1) * taken, :]
        for entry in range(shards):
            (far_ref if entry % 2 else near_ref)[entry // 2] = order[spot_ref[0] ^ entry]


def tail_rows(shards):
    return -(-(OUT + 2) // shards)


def feed(spot, t, noisy, pos, wpatch, o, mod, bias, head, hbias, velocity, pieces, shards, count_all, images=2):
    batch = o.shape[0]
    kept1 = (shards, FF // shards, D)
    kept2 = (shards, (D + FF) // shards, D)
    half = (shards // 2, tail_rows(shards), D)
    tokens = batch * SEQ
    return pl.pallas_call(
        partial(feed_kernel, images=images, count_all=count_all),
        grid=(batch // images,),
        in_specs=[
            pl.BlockSpec(memory_space=pltpu.SMEM),
            pl.BlockSpec(memory_space=pltpu.SMEM),
            rows(images, SEQ, PATCH),
            whole((SEQ, D)),
            whole((PATCH, D)),
            rows(images, SEQ, D),
            rows(images, 1, 8 * D),
            whole((BIASES, D)),
            whole((D, OUT)),
            whole((1, OUT)),
            rows(images, SEQ, OUT),
        ]
        + [ANYWHERE] * len(pieces),
        out_specs=[
            rows(images, SEQ, D),
            rows(images, SEQ, D),
            rows(images, SEQ, D),
            rows(images * SEQ, FF),
            rows(images * SEQ, FF),
            rows(images, SEQ, D),
            rows(images, SEQ, D),
            rows(images, 1, 3 * D),
            fixed(half),
            fixed(half),
            fixed((1, D)),
            ANYWHERE,
            ANYWHERE,
        ],
        out_shape=[
            shape_of((batch, SEQ, D), F32),
            shape_of((batch, SEQ, D), BF),
            shape_of((batch, SEQ, D), BF),
            shape_of((tokens, FF), BF),
            shape_of((tokens, FF), BF),
            shape_of((batch, SEQ, D), BF),
            shape_of((batch, SEQ, D), F32),
            shape_of((batch, 1, 3 * D), F32),
            shape_of(half, F32),
            shape_of(half, F32),
            shape_of((1, D), F32),
            shape_of(kept1, BF),
            shape_of(kept2, BF),
        ],
        scratch_shapes=[
            pltpu.VMEM((shards, kept1[1] + kept2[1], D), BF),
            pltpu.VMEM((shards * half[1], D), F32),
            pltpu.VMEM((shards,) + half[1:], F32),
            pltpu.SemaphoreType.DMA,
            pltpu.SemaphoreType.DMA((2,)),
        ],
        compiler_params=pltpu.CompilerParams(vmem_limit_bytes=VMEM_LIMIT),
        name="feed",
        cost_estimate=cost(52),
    )(spot, t, noisy, pos, wpatch, o, mod, bias, head, hbias, velocity, *pieces)


def feed_back_kernel(
    m_ref, df_ref, g_ref, slope_ref, w1_ref, w2_ref, wup_ref, wdown_ref, bup_ref, dm_ref, mt, dft, *, tile
):
    step = pl.program_id(0)

    @pl.when(step == 0)
    def _():
        mt[...] = m_ref[...].T
        dft[...] = df_ref[...].T
        dm_ref[...] = jnp.zeros_like(dm_ref)

    tokens = m_ref.shape[0]
    w1 = w1_ref[...].reshape(D, D)
    w2 = w2_ref[...]
    du_parts = []
    for i in range(tokens // tile):
        cut = slice(i * tile, (i + 1) * tile)
        du = (dot_nt(df_ref[cut, :], w2) * slope_ref[cut, :].astype(F32)).astype(BF)
        du_parts.append(du)
        dm_ref[cut, :] += dot_nt(du, w1)
    du = jnp.concatenate(du_parts, 0)
    bup_ref[...] = jnp.sum(du.astype(F32), 0, keepdims=True)
    wup_ref[...] = dot(mt[...], du).astype(BF).reshape(wup_ref.shape)
    wdown_ref[...] = dot(dft[...], g_ref[...]).T.astype(BF)


def feed_back(m, df, g, slope, w1, wout, first, last, tile=512):
    chunk = D
    shards = w1.shape[0]
    rows_of = D // shards
    tokens = m.shape[0]
    steps = (last - first) // chunk
    base = first // chunk
    return pl.pallas_call(
        partial(feed_back_kernel, tile=tile),
        grid=(steps,),
        in_specs=[
            whole((tokens, D)),
            whole((tokens, D)),
            pl.BlockSpec((tokens, chunk), lambda step: (0, step + base)),
            pl.BlockSpec((tokens, chunk), lambda step: (0, step + base)),
            pl.BlockSpec((shards, rows_of, D), lambda step: (0, step + base, 0)),
            pl.BlockSpec((chunk, D), lambda step: (step + base + D // chunk, 0)),
        ],
        out_specs=[
            pl.BlockSpec((shards, rows_of, D), lambda step: (0, step, 0)),
            pl.BlockSpec((chunk, D), lambda step: (step + base + D // chunk, 0)),
            pl.BlockSpec((1, chunk), lambda step: (0, step)),
            pl.BlockSpec((tokens, D), lambda step: (0, 0), pipeline_mode=pl.Buffered(1)),
        ],
        out_shape=[
            shape_of((shards, steps * rows_of, D), BF),
            shape_of((D + FF, D), BF),
            shape_of((1, last - first), F32),
            shape_of((tokens, D), F32),
        ],
        scratch_shapes=[pltpu.VMEM((D, tokens), BF), pltpu.VMEM((D, tokens), BF)],
        compiler_params=pltpu.CompilerParams(vmem_limit_bytes=VMEM_LIMIT),
        name="feed_back",
        cost_estimate=cost(51),
    )(m, df, g, slope, w1, wout)


def middle_back_kernel(
    mid_ref, dm_ref, ds_ref, y_ref, o_ref, mod_ref, bias_ref, wproj_ref, gout_ref,
    dmid_ref, do_ref, dmod_ref, wproj_out_ref, bproj_ref, total, *, images
):
    step = pl.program_id(0)

    @pl.when(step == 0)
    def _():
        total[...] = jnp.zeros_like(total)
        bproj_ref[...] = jnp.zeros_like(bproj_ref)

    tokens = images * SEQ
    dy_parts = []
    for index in range(images):
        normed, inverse = norm_parts(mid_ref[index])
        dm = dm_ref[index]
        dmid = ds_ref[index] + norm_back(
            dm * (1.0 + (mod_ref[index, :, 4 * D : 5 * D] + bias_ref[B_ADA + 4 : B_ADA + 5, :])), normed, inverse
        )
        dmid_ref[index] = dmid
        dmod_ref[index, :, :D] = jnp.sum(dmid * y_ref[index].astype(F32), 0, keepdims=True)
        dmod_ref[index, :, D : 2 * D] = jnp.sum(dm, 0, keepdims=True)
        dmod_ref[index, :, 2 * D :] = jnp.sum(dm * normed, 0, keepdims=True)
        gate = mod_ref[index, :, 2 * D : 3 * D] + bias_ref[B_ADA + 2 : B_ADA + 3, :]
        dy_parts.append((dmid * gate).astype(BF))
    dy = jnp.concatenate(dy_parts, 0)
    bproj_ref[...] += jnp.sum(dy.astype(F32), 0, keepdims=True)
    do_ref[...] = dot_nt(dy, wproj_ref[...]).astype(BF).reshape(images, SEQ, D)
    total[...] += dot_tn(o_ref[...].reshape(tokens, D), dy)

    @pl.when(step == pl.num_programs(0) - 1)
    def _():
        wproj_out_ref[...] = total[...].astype(BF)


def middle_back(mid, dm, ds, y, o, mod, bias, wout, gout, images=2):
    batch = mid.shape[0]
    return pl.pallas_call(
        partial(middle_back_kernel, images=images),
        grid=(batch // images,),
        in_specs=[
            rows(images, SEQ, D),
            rows(images, SEQ, D),
            rows(images, SEQ, D),
            rows(images, SEQ, D),
            rows(images, SEQ, D),
            rows(images, 1, 8 * D),
            whole((BIASES, D)),
            whole((D, D)),
            pl.BlockSpec(memory_space=pl.ANY),
        ],
        out_specs=[
            rows(images, SEQ, D),
            rows(images, SEQ, D),
            rows(images, 1, 3 * D),
            fixed((D, D)),
            fixed((1, D)),
        ],
        out_shape=[
            shape_of((batch, SEQ, D), F32),
            shape_of((batch, SEQ, D), BF),
            shape_of((batch, 1, 3 * D), F32),
            shape_of((D + FF, D), BF),
            shape_of((1, D), F32),
        ],
        input_output_aliases={8: 3},
        scratch_shapes=[pltpu.VMEM((D, D), F32)],
        compiler_params=pltpu.CompilerParams(vmem_limit_bytes=VMEM_LIMIT),
        name="middle_back",
        cost_estimate=cost(18),
    )(mid, dm, ds, y, o, mod, bias, wout, gout)


def attend_back_kernel(qkv_ref, do_ref, a_ref, dqkv_ref, wqkv_ref, bqkv_ref, total, *, images):
    step = pl.program_id(0)

    @pl.when(step == 0)
    def _():
        total[...] = jnp.zeros_like(total)
        bqkv_ref[...] = jnp.zeros_like(bqkv_ref)

    masks = head_masks()
    tokens = images * SEQ

    def image(index, carry):
        for pair in range(PAIRS):
            base = pair * PAIR
            scale = jnp.asarray(HDIM**-0.5, BF)
            queries = both_heads(qkv_ref[index, :, base : base + PAIR] * scale, masks)
            keys = qkv_ref[index, :, D + base : D + base + PAIR]
            values = qkv_ref[index, :, 2 * D + base : 2 * D + base + PAIR]
            grads = both_heads(do_ref[index, :, base : base + PAIR], masks)
            scores = dot_nt(keys, queries)
            power = jnp.exp(scores - jnp.max(scores, 0, keepdims=True))
            prob = power * (1.0 / jnp.sum(power, 0, keepdims=True))
            dprob = dot_nt(values, grads)
            delta = jnp.sum(prob * dprob, 0, keepdims=True)
            dscore = (prob * (dprob - delta)).astype(BF)
            dv = dot(prob.astype(BF), grads)
            dk = dot(dscore, queries)
            dq = dot_tn(dscore, keys * scale)
            dq = jnp.where(masks[0], dq[:SEQ], dq[SEQ:])
            dqkv_ref[index, :, base : base + PAIR] = dq.astype(BF)
            dqkv_ref[index, :, D + base : D + base + PAIR] = dk.astype(BF)
            dqkv_ref[index, :, 2 * D + base : 2 * D + base + PAIR] = dv.astype(BF)
        return carry

    lax.fori_loop(0, images, image, 0)
    dqkv = dqkv_ref[...].reshape(tokens, 3 * D)
    total[...] += dot_tn(a_ref[...].reshape(tokens, D), dqkv)
    bqkv_ref[...] += jnp.sum(dqkv.astype(F32), 0, keepdims=True)

    @pl.when(step == pl.num_programs(0) - 1)
    def _():
        for part in range(3):
            width = wqkv_ref.shape[1] // 3
            wqkv_ref[:, part * width : (part + 1) * width, :] = (
                total[:, part * D : (part + 1) * D].astype(BF).reshape(wqkv_ref.shape[0], width, D)
            )


def attend_back(qkv, do, a, shards, images=2):
    batch = qkv.shape[0]
    return pl.pallas_call(
        partial(attend_back_kernel, images=images),
        grid=(batch // images,),
        in_specs=[rows(images, SEQ, 3 * D), rows(images, SEQ, D), rows(images, SEQ, D)],
        out_specs=[rows(images, SEQ, 3 * D), fixed((shards, 3 * D // shards, D)), fixed((1, 3 * D))],
        out_shape=[
            shape_of((batch, SEQ, 3 * D), BF),
            shape_of((shards, 3 * D // shards, D), BF),
            shape_of((1, 3 * D), F32),
        ],
        scratch_shapes=[pltpu.VMEM((D, 3 * D), F32)],
        compiler_params=pltpu.CompilerParams(vmem_limit_bytes=VMEM_LIMIT),
        name="attend_back",
        cost_estimate=cost(45),
    )(qkv, do, a)


def stream_back_kernel(
    spot_ref, dqkv_ref, dmid_ref, noisy_ref, pos_ref, wpatch_ref, mod_ref, bias_ref, wqkv_ref,
    dmod_ref, near_ref, far_ref, bpatch_ref, wpatch_out_ref, order, *, images
):
    step = pl.program_id(0)

    @pl.when(step == 0)
    def _():
        wpatch_out_ref[...] = jnp.zeros_like(wpatch_out_ref)
        bpatch_ref[...] = jnp.zeros_like(bpatch_ref)

    tokens = images * SEQ
    dqkv = dqkv_ref[...].reshape(tokens, 3 * D)
    da = sum(dot_nt(dqkv[:, part * D : (part + 1) * D], part_of(wqkv_ref, part, 3)) for part in range(3))
    for index in range(images):
        noisy = noisy_ref[index]
        stream = dot(noisy, wpatch_ref[...]) + (pos_ref[...] + bias_ref[B_PATCH : B_PATCH + 1, :])
        scale = 1.0 + (mod_ref[index, :, D : 2 * D] + bias_ref[B_ADA + 1 : B_ADA + 2, :])
        normed, inverse = norm_parts(stream)
        part = da[index * SEQ : (index + 1) * SEQ]
        dmod_ref[index, :, :D] = jnp.sum(part, 0, keepdims=True)
        dmod_ref[index, :, D:] = jnp.sum(part * normed, 0, keepdims=True)
        dstream = dmid_ref[index] + norm_back(part * scale, normed, inverse)
        embedded = dstream.astype(BF)
        bpatch_ref[...] += jnp.sum(embedded.astype(F32), 0, keepdims=True)
        wpatch_out_ref[...] += dot_tn(noisy, embedded)

    width = near_ref.shape[2]
    shards = D // width

    @pl.when(step == pl.num_programs(0) - 1)
    def _():
        for place_of in range(shards):
            order[place_of] = wpatch_out_ref[:, place_of * width : (place_of + 1) * width]
        for entry in range(shards):
            (far_ref if entry % 2 else near_ref)[entry // 2] = order[spot_ref[0] ^ entry]


def stream_back(spot, dqkv, dmid, noisy, pos, wpatch, mod, bias, wqkv, images=2):
    batch = dqkv.shape[0]
    half = (wqkv.shape[0] // 2, PATCH, D // wqkv.shape[0])
    return pl.pallas_call(
        partial(stream_back_kernel, images=images),
        grid=(batch // images,),
        in_specs=[
            pl.BlockSpec(memory_space=pltpu.SMEM),
            rows(images, SEQ, 3 * D),
            rows(images, SEQ, D),
            rows(images, SEQ, PATCH),
            whole((SEQ, D)),
            whole((PATCH, D)),
            rows(images, 1, 8 * D),
            whole((BIASES, D)),
            whole(wqkv.shape),
        ],
        out_specs=[rows(images, 1, 2 * D), fixed(half), fixed(half), fixed((1, D))],
        out_shape=[
            shape_of((batch, 1, 2 * D), F32),
            shape_of(half, F32),
            shape_of(half, F32),
            shape_of((1, D), F32),
        ],
        scratch_shapes=[pltpu.VMEM((PATCH, D), F32), pltpu.VMEM((2 * half[0],) + half[1:], F32)],
        compiler_params=pltpu.CompilerParams(vmem_limit_bytes=VMEM_LIMIT),
        name="stream_back",
        cost_estimate=cost(19),
    )(spot, dqkv, dmid, noisy, pos, wpatch, mod, bias, wqkv)


MARKS = 4
PATCH_ROW = TFREQ
BIAS_ROW = TFREQ + PATCH
MESSAGE = 304


def condition_kernel(spot_ref, near_ref, other_ref, times_ref, embed_ref, table_ref, *rest, team):
    me = spot_ref[0]
    width = embed_ref.shape[1]
    shards = D // width
    messages = [(other_ref if entry % 2 else near_ref).at[entry // 2] for entry in range(shards)]
    if team:
        in_ref, final_ref, time_pre_ref, condition_ref, marks_ref, wpatch_ref, bias_ref = rest[:7]
        near_mod_ref, far_mod_ref, table, bias_rows, order = rest[7:]
        batch = near_mod_ref.shape[1]
        marks = jnp.concatenate(
            [message[:batch, width : width + MARKS].astype(F32) for message in messages], 0
        )
        marks_ref[...] = marks
    else:
        groups_marks, (marks_ref, features_ref, time_act_ref, act_ref, table, bias_rows, order) = rest[:-7], rest[-7:]
        team_count = groups_marks[0].shape[0]
        for entry, part in enumerate(groups_marks):
            start = pl.multiple_of((spot_ref[1] ^ entry) * team_count, team_count)
            marks_ref[pl.ds(start, team_count), :] = part[...]
        marks = marks_ref[...]
    count = marks.shape[0]
    marks = marks.astype(jnp.int32)
    index = marks[:, 0:1] * 32 + marks[:, 1:2]
    label = marks[:, 2:3] * 32 + marks[:, 3:4]

    for entry in range(shards):
        bias_rows[me ^ entry] = messages[entry][BIAS_ROW : BIAS_ROW + BIASES, :width].astype(F32)
        if team:
            order[me ^ entry] = messages[entry][PATCH_ROW : PATCH_ROW + PATCH, :width]

    def bias_row(row):
        return bias_rows[lax.div(row, BIASES), pl.ds(lax.rem(row, BIASES), 1), :]

    entry = lax.broadcasted_iota(jnp.int32, (count, times_ref.shape[1]), 1)
    moment = jnp.sum(jnp.where(entry == index, times_ref[...], 0.0), 1, keepdims=True)
    half = TFREQ // 2
    frequency = lax.broadcasted_iota(jnp.int32, (1, half), 1).astype(F32)
    angles = moment * jnp.exp(-math.log(10000.0) * frequency / half)
    features = jnp.concatenate([jnp.cos(angles), jnp.sin(angles)], 1).astype(BF)
    table[...] = jnp.zeros_like(table)
    table[:, :NCLASS] = table_ref[...].astype(BF)
    entry = lax.broadcasted_iota(jnp.int32, (count, table.shape[1]), 1)
    onehot = (entry == label).astype(F32).astype(BF)
    condition = dot_nt(onehot, table[...]) + bias_row(B_CLASS * shards + me)
    for entry in range(shards):
        place_of = me ^ entry
        time_pre = dot(features, messages[entry][:TFREQ, :width])
        time_pre = time_pre + bias_row(B_TIME * shards + place_of)
        time_act = (time_pre * (1.0 / (1.0 + jnp.exp(-time_pre)))).astype(BF)
        start = pl.multiple_of(TFREQ + PATCH + place_of * width, 16)
        condition = condition + dot(time_act, embed_ref[pl.ds(start, width), :])
        if team:
            if entry == 0:
                for block in range(shards):
                    time_pre_ref[me ^ block] = time_pre[block * batch : (block + 1) * batch, :]
        else:
            time_act_ref[place_of] = time_act
    act = (condition * (1.0 / (1.0 + jnp.exp(-condition)))).astype(BF)
    if not team:
        features_ref[...] = features
        act_ref[...] = act
        return
    condition_ref[...] = condition
    for place_of in range(shards):
        wpatch_ref[:, place_of * width : (place_of + 1) * width] = order[place_of]
    for row in range(BIASES):
        for column in range(shards):
            holder, inner = divmod(row * shards + column, BIASES)
            bias_ref[row : row + 1, column * width : (column + 1) * width] = bias_rows[
                holder, inner : inner + 1, :
            ]
    part = jnp.concatenate([dot(act, in_ref[0].astype(BF)), dot(act, final_ref[...].astype(BF))], 1)
    for pair in range(shards // 2):
        row = 2 * pair * batch
        near_mod_ref[pair] = part[row : row + batch, :]
        far_mod_ref[pair] = part[row + batch : row + 2 * batch, :]


def condition_call(operands, in_specs, out_shape, width, team):
    shards = D // width
    return pl.pallas_call(
        partial(condition_kernel, team=team),
        grid=(1,),
        in_specs=[pl.BlockSpec(memory_space=pltpu.SMEM)] + in_specs,
        out_specs=[whole(out.shape) for out in out_shape],
        out_shape=out_shape,
        scratch_shapes=[
            pltpu.VMEM((width, 1024), BF),
            pltpu.VMEM((shards, BIASES, width), F32),
            pltpu.VMEM((shards, PATCH, width), BF),
        ],
        compiler_params=pltpu.CompilerParams(vmem_limit_bytes=VMEM_LIMIT),
        name="condition",
        cost_estimate=cost(6),
    )(*operands)


def condition_of_team(spot, near, other, times, embed, table, in_mats, final, batch):
    width = embed.shape[1]
    shards = D // width
    count = shards * batch
    operands = [spot, near, other, times, embed, table, in_mats, final]
    in_specs = [whole(part.shape) for part in operands[1:6]]
    in_specs += [pl.BlockSpec((1, width, 6 * D), lambda step: (0, 0, 0)), whole(final.shape)]
    half = (shards // 2, batch)
    out_shape = [
        shape_of((shards, batch, width), F32),
        shape_of((count, width), F32),
        shape_of((count, MARKS), F32),
        shape_of((PATCH, D), BF),
        shape_of((BIASES, D), F32),
        shape_of(half + (8 * D,), F32),
        shape_of(half + (8 * D,), F32),
    ]
    return condition_call(operands, in_specs, out_shape, width, True)


def condition_of_all(spot, near, other, times, embed, table, marks):
    width = embed.shape[1]
    count = len(marks) * marks[0].shape[0]
    operands = [spot, near, other, times, embed, table] + marks
    out_shape = [
        shape_of((count, MARKS), F32),
        shape_of((count, TFREQ), BF),
        shape_of((D // width, count, width), BF),
        shape_of((count, width), BF),
    ]
    return condition_call(operands, [whole(part.shape) for part in operands[1:]], out_shape, width, False)


def condition_back_kernel(
    spot_ref, near_ref, other_ref, early_near_ref, early_other_ref, condition_ref, in_ref, final_ref, embed_ref,
    late_ref, grad_ref, near_act_ref, far_act_ref, order
):
    me = spot_ref[0]
    pairs, width = near_ref.shape[0], embed_ref.shape[1]
    late = jnp.concatenate([ref[pair] for pair in range(pairs) for ref in (near_ref, other_ref)], 0)
    late_ref[...] = late
    early = [ref[pair, 0] for pair in range(pairs) for ref in (early_near_ref, early_other_ref)]
    early = jnp.concatenate(early, 0)
    grad = dot_nt(late, in_ref[0, :, : 5 * D].astype(BF))
    grad = grad + dot_nt(early[:, :D], in_ref[0, :, 5 * D :].astype(BF))
    grad = grad + dot_nt(early[:, D:], final_ref[...].astype(BF))
    condition = condition_ref[...]
    turn = 1.0 / (1.0 + jnp.exp(-condition))
    grad = grad * (turn * (1.0 + condition * (1.0 - turn)))
    batch = order.shape[1]
    for block in range(2 * pairs):
        order[me ^ block] = grad[block * batch : (block + 1) * batch, :]
    grad = order[...].reshape(grad.shape).astype(BF)
    grad_ref[...] = grad
    for entry in range(2 * pairs):
        start = pl.multiple_of(TFREQ + PATCH + (me ^ entry) * width, 16)
        part = dot_nt(grad, embed_ref[pl.ds(start, width), :])
        (far_act_ref if entry % 2 else near_act_ref)[entry // 2] = part


def condition_back(spot, near, other, early_near, early_other, condition, in_mats, final, embed):
    width = embed.shape[1]
    count = condition.shape[0]
    operands = [spot, near, other, early_near, early_other, condition, in_mats, final, embed]
    in_specs = [pl.BlockSpec(memory_space=pltpu.SMEM)] + [whole(part.shape) for part in operands[1:6]]
    in_specs += [pl.BlockSpec((1, width, 6 * D), lambda step: (0, 0, 0)), whole(final.shape), whole(embed.shape)]
    half = (near.shape[0], count, width)
    out_shape = [
        shape_of((count, 5 * D), BF),
        shape_of((count, width), BF),
        shape_of(half, F32),
        shape_of(half, F32),
    ]
    return pl.pallas_call(
        condition_back_kernel,
        grid=(1,),
        in_specs=in_specs,
        out_specs=[whole(out.shape) for out in out_shape],
        out_shape=out_shape,
        scratch_shapes=[pltpu.VMEM((2 * half[0], near.shape[1], width), F32)],
        compiler_params=pltpu.CompilerParams(vmem_limit_bytes=VMEM_LIMIT),
        name="condition_back",
        cost_estimate=cost(4),
    )(*operands)


BIAS_PARTS = (B_PATCH, B_QUERY, B_VALUE, B_PROJ, B_UP, B_UP + 1, B_UP + 2, B_UP + 3, B_DOWN)


def condition_grads_kernel(spot_ref, marks_ref, features_ref, time_act_ref, act_ref, early_near_ref, early_other_ref, *refs, groups):
    late, last, refs = refs[:groups], refs[groups : 2 * groups], refs[2 * groups :]
    gada_ref, gembed_ref, gtable_ref, bias_ref, message_ref, squares_ref = refs[:6]
    early_all, late_all, grads_all = refs[6:]
    me, group = spot_ref[0], spot_ref[1]
    team = late[0].shape[0]
    width = act_ref.shape[1]
    shards = D // width
    for entry in range(groups):
        here = pl.ds(pl.multiple_of((group ^ entry) * team, team), team)
        early = [ref[pair, entry] for pair in range(shards // 2) for ref in (early_near_ref, early_other_ref)]
        early_all[here, :] = jnp.concatenate(early, 0)
        late_all[here, :] = late[entry][...]
        for part in range(2):
            blocks = []
            for block in range(shards):
                start = pl.multiple_of(part * team + (me ^ block) * (team // shards), 8)
                blocks.append(last[entry][pl.ds(start, team // shards), :])
            grads_all[here, part * width : (part + 1) * width] = jnp.concatenate(blocks, 0).astype(BF)
    rest = [ref[2 * team :, :] for ref in last]
    while len(rest) > 1:
        rest = [rest[i] + rest[i + 1] for i in range(0, len(rest), 2)]
    rest = rest[0]
    act = act_ref[...]
    grad_time = grads_all[:, :width]
    grad_condition = grads_all[:, width:]
    gada_ref[:, : 5 * D] = dot_tn(act, late_all[...])
    gada_ref[:, 5 * D :] = dot_tn(act, early_all[...])
    marks = marks_ref[...].astype(jnp.int32)
    label = marks[:, 2:3] * 32 + marks[:, 3:4]
    entry = lax.broadcasted_iota(jnp.int32, (marks.shape[0], 1024), 1)
    onehot = (entry == label).astype(F32).astype(BF)
    gtable_ref[...] = dot_tn(grad_condition, onehot)[:, :NCLASS]
    early_rows = PATCH + TFREQ
    gembed_ref[:, :PATCH] = rest[:PATCH, :].T
    gembed_ref[:, PATCH:early_rows] = dot_tn(grad_time, features_ref[...])
    for entry in range(shards):
        start = early_rows + entry * width
        gembed_ref[:, start : start + width] = dot_tn(grad_condition, time_act_ref[entry])
    late_sum = jnp.sum(late_all[...].astype(F32), 0, keepdims=True)
    early_sum = jnp.sum(early_all[...].astype(F32), 0, keepdims=True)
    bias_ref[B_TIME : B_ADA, :] = jnp.zeros((2, D), F32)
    for part in range(5):
        bias_ref[B_ADA + part : B_ADA + part + 1, :] = late_sum[:, part * D : (part + 1) * D]
    for part in range(3):
        row = B_FINAL + part - 1 if part else B_ADA + 5
        bias_ref[row : row + 1, :] = early_sum[:, part * D : (part + 1) * D]
    for part, row in enumerate(BIAS_PARTS):
        for column in range(shards):
            first = PATCH + part * shards + column
            bias_ref[row : row + 1, column * width : (column + 1) * width] = rest[first : first + 1, :]
    btime = jnp.sum(grads_all[...].astype(F32), 0, keepdims=True)
    message_ref[0:1, :] = btime[:, :width]
    message_ref[1:2, :] = btime[:, width:]
    tail = rest[PATCH + len(BIAS_PARTS) * shards :, :]
    message_ref[2:, :] = tail
    taken = tail.shape[0] // shards
    row = lax.broadcasted_iota(jnp.int32, tail.shape, 0) // shards + spot_ref[0] * taken
    head = jnp.where(row <= OUT, tail, 0.0)

    def square(part):
        return jnp.sum(jnp.sum(part * part, 0, keepdims=True), 1, keepdims=True)

    squares_ref[...] = square(gada_ref[...]) + square(gembed_ref[...]) + square(gtable_ref[...]) + square(btime) + square(head)


def condition_grads(spot, marks, features, time_act, act, early_near, early_other, late, last):
    groups = len(late)
    count, width = act.shape
    operands = [spot, marks, features, time_act, act, early_near, early_other] + late + last
    shards = D // width
    out_shape = [
        shape_of((width, 8 * D), F32),
        shape_of((width, PATCH + TFREQ + D), F32),
        shape_of((width, NCLASS), F32),
        shape_of((BIASES, D), F32),
        shape_of((2 + tail_rows(shards) * shards, width), F32),
        shape_of((1, 1), F32),
    ]
    return pl.pallas_call(
        partial(condition_grads_kernel, groups=groups),
        grid=(1,),
        in_specs=[pl.BlockSpec(memory_space=pltpu.SMEM)] + [whole(part.shape) for part in operands[1:]],
        out_specs=[whole(out.shape) for out in out_shape],
        out_shape=out_shape,
        scratch_shapes=[
            pltpu.VMEM((count, 3 * D), BF),
            pltpu.VMEM((count, 5 * D), BF),
            pltpu.VMEM((count, 2 * width), BF),
        ],
        compiler_params=pltpu.CompilerParams(vmem_limit_bytes=VMEM_LIMIT),
        name="condition_grads",
        cost_estimate=cost(6),
    )(*operands)


def swap(array_in, axis, hop):
    count = lax.axis_size(axis)
    return lax.ppermute(array_in, axis, [(place_of, place_of ^ hop) for place_of in range(count)])


def spread(array_in, axis):
    count = lax.axis_size(axis)
    if axis == "shard":
        near = jnp.stack([array_in] + [swap(array_in, axis, hop) for hop in range(2, count, 2)])
        return jnp.stack([near, swap(near, axis, 1)], 1).reshape((count,) + array_in.shape)
    return jnp.stack([array_in] + [swap(array_in, axis, hop) for hop in range(1, count)])


def total_of(parts):
    while len(parts) > 1:
        parts = [parts[i] + parts[i + 1] for i in range(0, len(parts), 2)]
    return parts[0]


def exchange_sum(near):
    return total_of([near[0]] + [swap(near[hop], "shard", 2 * hop) for hop in range(1, near.shape[0])])


def from_groups(array_in, tuned, first=1):
    count = lax.axis_size("grp")
    if tuned:
        pair = jnp.stack([array_in, swap(array_in, "grp", first)])
        far = swap(pair, "grp", 3 - first)
        parts = [pair[0], pair[1], far[0], far[1]]
        return parts if first == 1 else [parts[0], parts[2], parts[1], parts[3]]
    parts = jnp.broadcast_to(array_in[None], (count,) + array_in.shape)
    parts = ordered(lax.all_to_all(parts, "grp", 0, 0, tiled=True), "grp")
    return [parts[i] for i in range(count)]


def ordered(array_in, axis):
    count = lax.axis_size(axis)
    place_of = lax.axis_index(axis)
    bit = 1
    while bit < count:
        pairs = array_in.reshape((count // (2 * bit), 2, bit) + array_in.shape[1:])
        array_in = jnp.where(place_of & bit != 0, pairs[:, ::-1], pairs).reshape(array_in.shape)
        bit *= 2
    return array_in


def sum_spread(array_in, axis):
    parts = spread(array_in, axis)
    return total_of([parts[i] for i in range(parts.shape[0])])


def tie(arrays, after):
    return lax.optimization_barrier((arrays, after))[0]


DIRECT = 160


def rows_near(own):
    rows_all = own.shape[0]
    quarter = -(-rows_all // 64) * 16
    group = lax.axis_index("grp")
    start = jnp.where(group == 3, rows_all - quarter, group * quarter)
    part = lax.dynamic_slice_in_dim(own, start, quarter, 0)
    return [swap(part, "shard", hop) for hop in (2, 4, 6)]


def rows_far(near):
    return lax.all_gather(jnp.stack(near), "grp")


def rows_all(own, far):
    return [own, far, swap(own, "shard", 1), swap(far, "shard", 1)]


def quarter_start(rows_all, quarter, group):
    return jnp.where(group == 3, rows_all - quarter, group * quarter)


def cores_summed(grads):
    pairs = grads.reshape((4, 2) + grads.shape[1:])
    core = lax.axis_index("shard") % 2
    theirs = lax.dynamic_index_in_dim(pairs, 1 - core, 1, keepdims=False)
    mine = lax.dynamic_index_in_dim(pairs, core, 1, keepdims=False)
    return lower(mine.astype(F32) + swap(theirs, "shard", 1).astype(F32))


def groups_traded(grads):
    group = lax.axis_index("grp")
    rows_all = grads.shape[1]
    quarter = -(-rows_all // 64) * 16
    parts = []
    for hop in range(4):
        start = quarter_start(rows_all, quarter, group ^ hop)
        part = lax.dynamic_slice_in_dim(grads, start, quarter, 1)
        parts.append(swap(part, "grp", hop) if hop else part)
    return parts


def shards_traded(parts):
    return chips_traded(total_of([part.astype(F32) for part in parts]))


def chips_traded(total):
    low = lower(total)
    chip = lax.axis_index("shard") // 2
    own = lax.dynamic_index_in_dim(total, chip, 0, keepdims=False)
    return [own] + [
        swap(lax.dynamic_index_in_dim(low, chip ^ hop, 0, keepdims=False), "shard", 2 * hop) for hop in (1, 2, 3)
    ]


def shards_summed(parts):
    return lower(total_of([part.astype(F32) for part in parts]))


def quarters_joined(parts, *sizes):
    joined, first = [], 0
    for quarter, count in sizes:
        part = parts[:, first : first + quarter]
        first += quarter
        skipped = 4 * quarter - count // 8
        joined.append(jnp.concatenate([part[0], part[1], part[2], part[3, skipped:]]).astype(F32))
    return joined


def halves_added(part, bit):
    axis = part.ndim - 2
    half = part.shape[axis] // 2
    side = (lax.axis_index("grp") // bit) % 2
    ours = lax.dynamic_slice_in_dim(part, side * half, half, axis)
    theirs = lax.dynamic_slice_in_dim(part, (1 - side) * half, half, axis)
    return [ours, swap(theirs, "grp", bit)]


def matmul(formula, left, right):
    return jnp.einsum(formula, left, right, preferred_element_type=F32)


def lower(array_in):
    return array_in.astype(BF)


def summed(array_in, axes):
    return jnp.sum(array_in.astype(F32), axes)


def position_table():
    quarter = D // 4
    angular = np.exp(-math.log(10000.0) * np.arange(quarter) / quarter)
    position = np.arange(GRID * GRID)
    column = (position % GRID)[:, None] * angular
    row_pos = (position // GRID)[:, None] * angular
    table = np.concatenate([np.sin(column), np.cos(column), np.sin(row_pos), np.cos(row_pos)], 1)
    return jnp.asarray(table.astype(np.float32))


def pick_times(time_index, times):
    matches = time_index[:, None] == jnp.arange(times.shape[0], dtype=jnp.int32)[None, :]
    return jnp.sum(jnp.where(matches, times[None, :], 0.0), 1)


def condition_grads_plain(spot, marks, features, time_act, act, early_near, early_other, late, last):
    team, width = late[0].shape[0], act.shape[1]
    shards = D // width

    def in_exchange(part):
        part = part.reshape(2, shards, team // shards, width).transpose(1, 0, 2, 3)
        return ordered(part, "shard").transpose(1, 0, 2, 3).reshape(2 * team, width)

    early = jnp.stack([early_near, early_other], 1).transpose(2, 0, 1, 3, 4)
    early = early.reshape(len(late), team, 3 * D)
    early, late, last_all = [
        ordered(jnp.stack(parts), "grp").reshape(-1, parts[0].shape[1])
        for parts in (list(early), late, [in_exchange(part[: 2 * team]) for part in last])
    ]
    last_all = lower(last_all).reshape(-1, 2, team, width)
    grad_time, grad_condition = last_all[:, 0].reshape(-1, width), last_all[:, 1].reshape(-1, width)
    rest = total_of([part[2 * team :] for part in last])
    gada = jnp.concatenate([matmul("bd,be->de", act, late), matmul("bd,be->de", act, early)], 1)
    labels = (marks[:, 2:3] * 32.0 + marks[:, 3:4]).astype(jnp.int32)
    onehot = lower((labels == jnp.arange(NCLASS, dtype=jnp.int32)[None, :]).astype(F32))
    gtable = matmul("bd,bn->dn", grad_condition, onehot)
    gembed = jnp.concatenate(
        [
            rest[:PATCH].T,
            matmul("bd,bf->df", grad_time, features),
            matmul("be,sbd->esd", grad_condition, time_act).reshape(width, D),
        ],
        1,
    )
    bias = jnp.zeros((BIASES, D), F32)
    bias = bias.at[B_ADA : B_ADA + 5].set(summed(late, 0).reshape(5, D))
    early_sum = summed(early, 0).reshape(3, D)
    bias = bias.at[B_ADA + 5].set(early_sum[0]).at[B_FINAL:].set(early_sum[1:])
    parts = rest[PATCH : PATCH + len(BIAS_PARTS) * shards].reshape(len(BIAS_PARTS), D)
    for part, row in enumerate(BIAS_PARTS):
        bias = bias.at[row].set(parts[part])
    btime = jnp.stack([summed(grad_time, 0), summed(grad_condition, 0)])
    tail = rest[PATCH + len(BIAS_PARTS) * shards :]
    taken = tail.shape[0] // shards
    row = jnp.arange(tail.shape[0], dtype=jnp.int32)[:, None] // shards + spot[0] * taken
    head = jnp.where(row <= OUT, tail, 0.0)
    squares = sum(jnp.sum(part * part) for part in (gada, gembed, gtable, btime, head))
    return gada, gembed, gtable, bias, jnp.concatenate([btime, tail]), squares.reshape(1, 1)


def adamw(weight, moment_one, moment_two, gradient, factor):
    gradient = gradient * factor
    moment_one = BETA_ONE * moment_one + (1.0 - BETA_ONE) * gradient
    moment_two = BETA_TWO * moment_two + (1.0 - BETA_TWO) * gradient * gradient
    fix_one = 1.0 - BETA_ONE**STEP
    fix_two = 1.0 - BETA_TWO**STEP
    update = (
        moment_one / fix_one / (jnp.sqrt(moment_two / fix_two) + EPS_ADAM) + WEIGHT_DECAY * weight
    )
    return (weight - LEARN_RATE * update, moment_one, moment_two)


def per_device(
    latents, noise, velocity, labels, time_index, times,
    in_mats, out_mats, embed_mats, class_table, final_ada, head_mat, bias_vec,
    in_mats_first, out_mats_first, embed_first, table_first, final_first, head_first, bias_first,
    in_mats_second, out_mats_second, embed_second, table_second, final_second, head_second, bias_second,
):
    shards = lax.axis_size("shard")
    groups = lax.axis_size("grp")
    me = lax.axis_index("shard")
    mine = lax.axis_index("grp")
    batch = latents.shape[0]
    width = embed_mats.shape[1]
    team = shards * batch
    tuned = groups == 4 and shards == 8

    embed_low = lower(embed_mats)
    marks = jnp.stack([time_index // 32, time_index % 32, labels // 32, labels % 32], 1).astype(BF)
    marks = jnp.pad(marks, ((0, TFREQ - batch), (0, 128 - width - MARKS)))
    message = jnp.concatenate(
        [embed_low[PATCH : PATCH + TFREQ], embed_low[:PATCH], lower(bias_vec).reshape(BIASES, width)]
    )
    message = jnp.pad(message, ((0, MESSAGE - message.shape[0]), (0, 128 - width)))
    message = message + jnp.pad(marks, ((0, MESSAGE - TFREQ), (width, 0)))
    arrived = [swap(message, "shard", hop) for hop in range(2, shards, 2)]
    near_message = jnp.stack([message] + arrived)
    other_message = swap(near_message, "shard", 1)
    in_mats_early, out_mats_early = tie((in_mats, out_mats), message)

    def rows_of(first, count):
        return [lower(in_mats_early[0, :, first + part * D : first + (part + 1) * D]) for part in range(count)]

    own_qkv = jnp.concatenate(rows_of(6 * D, 3))
    own_feed = jnp.concatenate(rows_of(9 * D, FF // D) + [lower(out_mats_early[0])])
    spot = jnp.stack([me, mine]).astype(jnp.int32)
    if tuned:
        near_qkv = rows_near(own_qkv)
        traded = own_feed.shape[0] - DIRECT
        near_feed = rows_near(own_feed[:traded])
    else:
        qkv_pieces, feed_pieces = [[lax.all_gather(own, "shard")] for own in (own_qkv, own_feed)]
    times_row = jnp.pad(times, (0, -times.shape[0] % 128))[None]
    time_pre, condition, marks_team, wpatch, biases, near_mod, far_mod = condition_of_team(
        spot, near_message, other_message, times_row, embed_low, class_table.T, in_mats, final_ada, batch
    )
    if tuned:
        far_qkv = rows_far(tie(near_qkv, time_pre))
    near_mod = near_mod + swap(far_mod, "shard", 1)
    mods = lower(near_mod)
    mods = [near_mod[0]] + [swap(mods[hop], "shard", 2 * hop) for hop in range(1, shards // 2)]
    mod = total_of([part.astype(F32) for part in mods])[:, None, :]
    if tuned:
        far_feed = rows_far(tie(near_feed, (far_qkv, mod)))
    if tuned:
        direct = [swap(tie(own_feed[traded:], mod), "shard", hop) for hop in (2, 4, 6)]
    latents, noise, velocity, head_mat_late, marks_team = tie(
        (latents, noise, velocity, head_mat, marks_team), near_mod
    )
    if tuned:
        far_qkv = tie(far_qkv, near_mod)
        qkv_pieces = rows_all(own_qkv, far_qkv)
    marks_all = from_groups(marks_team, tuned)
    moment = pick_times(time_index, times)
    noisy = lower((1.0 - moment)[:, None, None] * latents + moment[:, None, None] * noise)
    pos = position_table()
    a, qkv, o, wqkv = attend(spot, noisy, pos, wpatch, mod, biases, qkv_pieces, shards)
    if tuned:
        o, direct, marks_all = lax.optimization_barrier((o, direct, marks_all))
        direct = jnp.stack(direct)
        feed_pieces = rows_all(tie(own_feed, o), tie(far_feed, o)) + [direct, swap(direct, "shard", 1)]
    marks_all, features, time_act, cond_act_all = condition_of_all(
        spot, near_message, other_message, times_row, embed_low, class_table.T, marks_all
    )
    mod = tie(mod, features)
    count_all = float(groups * shards * batch * SEQ * OUT)
    head_low = lower(head_mat_late)
    mid, y, m, g, slope, df, ds, dmod_feed, near_tail, far_tail, bdown, wup, wout = feed(
        spot, moment, noisy, pos, wpatch, o, mod, biases, head_low[:D],
        head_low[D:].astype(F32), velocity, feed_pieces, shards, count_all,
    )
    wout = wout.reshape(D + FF, D)
    tokens = batch * SEQ
    early = lower(dmod_feed[:, 0])
    early = [early] + [swap(early, "grp", hop) for hop in range(1, groups)] if tuned else from_groups(early, tuned)
    gup, gout, bup, dm = feed_back(
        m.reshape(tokens, D), df.reshape(tokens, D), g, slope, wup, wout, 0, FF
    )
    gup, gout, bup, dm, early = lax.optimization_barrier((gup, gout, bup, dm, early))
    gup = lax.psum_scatter(gup, "shard", scatter_dimension=0)
    early = jnp.stack(early)
    early_far = [swap(early, "shard", hop) for hop in range(2, shards, 2)]
    dmid, do, dmod_mid, gout, bproj = middle_back(
        mid, dm.reshape(batch, SEQ, D), tie(ds, early), y, o, mod, biases, wout, gout
    )

    dmid, do, dmod_mid, gout, bproj, early, early_far = lax.optimization_barrier(
        (dmid, do, dmod_mid, gout, bproj, early, early_far)
    )

    gout = gout.reshape(shards, (D + FF) // shards, D)
    if tuned:
        gout = cores_summed(gout)
        early_near = jnp.stack([early] + early_far)
        near_tail, far_tail = [part.reshape(shards // 2, -1, width) for part in tie((near_tail, far_tail), dmid)]
        do = tie(do, (gout, early_near, near_tail, far_tail))
        gout_parts = groups_traded(gout)
    else:
        near_tail, far_tail = [part.reshape(shards // 2, -1, width) for part in (near_tail, far_tail)]
        early_near = jnp.stack([early] + early_far)
        gout = lax.psum_scatter(gout, "shard", scatter_dimension=0)
    early_other = swap(early_near, "shard", 1)
    dqkv, gqkv, bqkv = attend_back(qkv, do, a, shards)
    if tuned:
        dqkv, gqkv, bqkv, gout_parts, early_other = lax.optimization_barrier(
            (dqkv, gqkv, bqkv, gout_parts, early_other)
        )
    if tuned:
        gqkv = halves_added(cores_summed(gqkv), 2)
        gout_parts = shards_traded(gout_parts)
        dmid, dmod_mid, gup, bqkv, bproj, bup, bdown = tie(
            (dmid, dmod_mid, gup, bqkv, bproj, bup, bdown), gout_parts[0]
        )
        gup = halves_added(gup, 2)
    else:
        gqkv = lax.psum_scatter(gqkv, "shard", scatter_dimension=0)
    dmod_attn, near_patch, far_patch, bpatch = stream_back(
        spot, dqkv, dmid, noisy, pos, wpatch, mod, biases, wqkv
    )
    if tuned:
        dmod_attn, near_patch, far_patch, bpatch, gup, gout_parts, gqkv = lax.optimization_barrier(
            (dmod_attn, near_patch, far_patch, bpatch, gup, gout_parts, gqkv)
        )
        gup, gout = shards_summed(gup), shards_summed(gout_parts)
        gqkv, gup = halves_added(shards_summed(gqkv), 1), halves_added(gup, 1)
    late = lower(jnp.concatenate([dmod_attn[:, 0], dmod_mid[:, 0]], 1))

    near_late = jnp.stack([late] + [swap(late, "shard", hop) for hop in range(2, shards, 2)])
    other_late = swap(near_late, "shard", 1)
    if tuned:
        gup, other_late, gqkv = tie((gup, other_late, gqkv), gout)
    late, grad_condition, near_act, far_act = condition_back(
        spot, near_late, other_late, early_near, early_other, condition, in_mats, final_ada, embed_low
    )
    bias_part = jnp.concatenate([bpatch, bqkv[:, :D], bqkv[:, 2 * D :], bproj, bup, bdown], 1)
    bias_part = jnp.broadcast_to(bias_part.reshape(1, -1, width), (shards // 2, len(BIAS_PARTS) * shards, width))

    far_act = jnp.concatenate([far_act, far_patch, bias_part, far_tail], 1)
    near_act = jnp.concatenate([near_act, near_patch, bias_part, near_tail], 1)
    near_act = near_act + swap(far_act, "shard", 1)
    acts = [near_act[0]] + [swap(near_act[hop], "shard", 2 * hop) for hop in range(1, near_act.shape[0])]

    def last_of(acts):
        act_part = total_of(acts)
        unused, time_pull = jax.vjp(jax.nn.silu, time_pre)
        grad_time = lower(time_pull(act_part[:team].reshape(time_pre.shape))[0]).reshape(team, width)
        return jnp.concatenate([grad_time.astype(F32), grad_condition.astype(F32), act_part[team:]])

    if tuned:
        late_x, late_y = swap(late, "grp", 1), swap(late, "grp", 2)
        acts, late_x, late_y, gqkv = lax.optimization_barrier((acts, late_x, late_y, gqkv))
        last = last_of(acts)
        gqkv = shards_traded(gqkv)
        both = jnp.concatenate([shards_summed(gup), gout])
        last_x, late_xy, both_y = swap(last, "grp", 1), swap(late_y, "grp", 1), swap(both, "grp", 2)
        last_x, late_xy, both_y, gqkv = lax.optimization_barrier((last_x, late_xy, both_y, gqkv))
        gqkv = shards_summed(gqkv)
        pair = jnp.stack([last, last_x])
        both = jnp.stack([both, both_y])
        last_far, both_far, gqkv_y = swap(pair, "grp", 2), swap(both, "grp", 1), swap(gqkv, "grp", 2)
        last_far, gqkv_y = lax.optimization_barrier((last_far, gqkv_y))
        grads_last = [last, last_x, last_far[0], last_far[1]]
        grads_late = [late, late_x, late_y, late_xy]
        gqkv = jnp.stack([gqkv, gqkv_y])
        gqkv_far = swap(gqkv, "grp", 1)
        both = ordered(jnp.stack([both[0], both_far[0], both[1], both_far[1]]), "grp")
        gqkv = ordered(jnp.stack([gqkv[0], gqkv_far[0], gqkv[1], gqkv_far[1]]), "grp")
        gup, gout = quarters_joined(both, (gup[0].shape[0], FF), (gout.shape[0], D + FF))
        gqkv = quarters_joined(gqkv, (gqkv.shape[1], 3 * D))[0]
        gfeed = [gup, gout]
    else:
        grads_last = from_groups(last_of(acts), tuned)
        grads_late = from_groups(late, tuned)
        gup, gout, gqkv = [
            total_of([part.astype(F32) for part in from_groups(grads, tuned)]) for grads in (gup, gout, gqkv)
        ]
        gfeed = [gup, gout]
    grads_of = condition_grads if tuned else condition_grads_plain
    gada, gembed, gtable, bias_grad, message, squares = grads_of(
        spot, marks_all, features, time_act, cond_act_all, early_near, early_other, grads_late, grads_last
    )
    gup, gout = gfeed
    share = bias_vec.shape[0]
    bias_grad = lax.dynamic_slice_in_dim(bias_grad.reshape(-1), me * share, share, 0)
    squares = squares + sum(jnp.sum(part * part) for part in (gup, gqkv, gout, bias_grad))
    message = jnp.concatenate([message, jnp.broadcast_to(squares, (6, width))])
    final = spread(message, "shard")
    grad_norm = jnp.sqrt(total_of([final[i, -1] for i in range(shards)]))
    factor = (CLIP_NORM / jnp.maximum(grad_norm, CLIP_NORM))[0]
    grad_norm = grad_norm[0]
    final = ordered(final, "shard")
    btime = jnp.concatenate([final[:, 0].reshape(-1), final[:, 1].reshape(-1)])
    tail = final[:, 2:-6].reshape(-1, D)
    head_grad = jnp.concatenate([tail[:OUT].T, tail[OUT : OUT + 1, :OUT]])
    loss_sum = tail[OUT + 1, 0]
    btime = jnp.concatenate([jnp.zeros((D,), F32), btime, jnp.zeros((12 * D + FF,), F32)])
    bias_grad = bias_grad + lax.dynamic_slice_in_dim(btime, me * share, share, 0)
    in_grad = jnp.concatenate(
        [gada[:, : 6 * D]]
        + [gqkv[part * width : (part + 1) * width] for part in range(3)]
        + [gup[part * width : (part + 1) * width] for part in range(FF // D)],
        1,
    )
    weights = (in_mats, out_mats, embed_mats, class_table, final_ada, head_mat, bias_vec)
    firsts = (in_mats_first, out_mats_first, embed_first, table_first, final_first, head_first, bias_first)
    seconds = (
        in_mats_second, out_mats_second, embed_second, table_second, final_second, head_second, bias_second
    )
    grads = (in_grad[None], gout[None], gembed.T, gtable.T, gada[:, 6 * D :], head_grad, bias_grad)
    stepped = [
        adamw(weight, moment_one, moment_two, gradient, factor)
        for weight, moment_one, moment_two, gradient in zip(weights, firsts, seconds, grads)
    ]
    return tuple(part[0] for part in stepped) + tuple(part[1] for part in stepped) + tuple(
        part[2] for part in stepped
    ) + (loss_sum, grad_norm)


def solution(mesh):
    images = P(("grp", "shard"))
    placed = (
        P(None, "shard", None),
        P(None, "shard", None),
        P(None, "shard"),
        P(None, "shard"),
        P("shard", None),
        P(),
        P("shard"),
    )
    return jax.shard_map(
        per_device,
        mesh=mesh,
        in_specs=(images,) * 5 + (P(),) + placed * 3,
        out_specs=placed * 3 + (P(), P()),
        check_vma=False,
    )
```

```python
import math
from functools import partial
import numpy as np
import jax
import jax.numpy as jnp
from jax import lax
from jax.sharding import PartitionSpec as P
from jax.experimental import pallas as pl
from jax.experimental.pallas import tpu as pltpu

D = 768
HEADS = 12
HDIM = 64
FF = 3072
PATCH = 16
SEQ = 256
OUT = 32
GRID = 16
STEP = 10
BETA_ONE = 0.9
BETA_TWO = 0.999
LEARN_RATE = 0.05
WEIGHT_DECAY = 0.05
EPS_ADAM = 1e-08
CLIP_NORM = 0.01
TFREQ = 256
NCLASS = 1001
EPS_NORM = 1e-06
BF = jnp.bfloat16
F32 = jnp.float32
VMEM_LIMIT = 60 * 1024 * 1024
COST = 3 * 10**8
PAIR = 2 * HDIM
PAIRS = HEADS // 2
BIASES = 19
B_PATCH, B_TIME, B_CLASS, B_ADA, B_QUERY, B_VALUE, B_PROJ, B_UP, B_DOWN, B_FINAL = 0, 1, 2, 3, 9, 10, 11, 12, 16, 17


def dot(left, right):
    return jnp.dot(left, right, preferred_element_type=F32)


def dot_nt(left, right):
    return lax.dot_general(left, right, (((1,), (1,)), ((), ())), preferred_element_type=F32)


def dot_tn(left, right):
    return lax.dot_general(left, right, (((0,), (0,)), ((), ())), preferred_element_type=F32)


def whole(shape):
    zeros = (0,) * len(shape)
    return pl.BlockSpec(shape, lambda step: zeros, pipeline_mode=pl.Buffered(1))


def fixed(shape):
    zeros = (0,) * len(shape)
    return pl.BlockSpec(shape, lambda step: zeros)


def rows(count, *rest):
    zeros = (0,) * len(rest)
    return pl.BlockSpec((count,) + rest, lambda step: (step,) + zeros)


def shape_of(shape, dtype):
    return jax.ShapeDtypeStruct(shape, dtype)


def norm_parts(array_in):
    centre = array_in - jnp.mean(array_in, -1, keepdims=True)
    inverse = lax.rsqrt(jnp.mean(centre * centre, -1, keepdims=True) + EPS_NORM)
    return centre * inverse, inverse


def norm_back(grad_normed, normed, inverse):
    first = jnp.mean(grad_normed, -1, keepdims=True)
    second = jnp.mean(grad_normed * normed, -1, keepdims=True)
    return inverse * (grad_normed - first - normed * second)


def cost(microseconds):
    return pl.CostEstimate(flops=microseconds * COST, bytes_accessed=0, transcendentals=0)


def head_masks():
    lane = lax.broadcasted_iota(jnp.int32, (1, PAIR), 1)
    return (lane < HDIM, lane >= HDIM)


def both_heads(part, masks):
    return jnp.concatenate([jnp.where(mask, part, jnp.zeros_like(part)) for mask in masks], 0)


def weight_copies(spot_ref, pieces, target, sem):
    if len(pieces) == 1:
        return [pltpu.make_async_copy(pieces[0], target, sem)]
    own, near, pair, other, *direct = pieces
    shard = spot_ref[0]
    quarter = near.shape[2]
    traded = target.shape[1] - (direct[0].shape[1] if direct else 0)
    rest = traded - 3 * quarter
    made = [
        pltpu.make_async_copy(own, target.at[shard], sem),
        pltpu.make_async_copy(pair, target.at[shard ^ 1], sem),
    ]
    for block in range(4):
        count = rest if block == 3 else quarter
        rows_here = slice(block * quarter, block * quarter + count)
        for core, part in enumerate((near, other)):
            for hop in range(3):
                source = part.at[block, hop, quarter - count :] if count < quarter else part.at[block, hop]
                slot = shard ^ (2 * hop + 2 + core)
                made.append(pltpu.make_async_copy(source, target.at[slot, rows_here], sem))
    for core, part in enumerate(direct):
        for hop in range(3):
            slot = shard ^ (2 * hop + 2 + core)
            made.append(pltpu.make_async_copy(part.at[hop], target.at[slot, traded:], sem))
    return made


def run_copies(made, start):
    for copy in made:
        copy.start() if start else copy.wait()


def part_of(weights, part, count):
    width = weights.shape[1] // count
    return weights[:, part * width : (part + 1) * width, :].reshape(D, D)


def attend_kernel(
    spot_ref, noisy_ref, pos_ref, wpatch_ref, mod_ref, bias_ref, *refs, images
):
    pieces, (a_ref, qkv_ref, o_ref, kept_ref, wqkv_ref, sem, out_sem) = refs[:-7], refs[-7:]
    step = pl.program_id(0)
    made = weight_copies(spot_ref, pieces, wqkv_ref, sem)
    keep = pltpu.make_async_copy(wqkv_ref, kept_ref, out_sem)

    @pl.when(step == 0)
    def _():
        run_copies(made, True)
        run_copies(made, False)
        keep.start()

    @pl.when(step == pl.num_programs(0) - 1)
    def _():
        keep.wait()

    masks = head_masks()

    def bias(row):
        return bias_ref[row : row + 1, :]

    def image(index, carry):
        stream = dot(noisy_ref[index], wpatch_ref[...]) + (pos_ref[...] + bias(B_PATCH))
        normed, unused = norm_parts(stream)
        scale = 1.0 + (mod_ref[index, :, D : 2 * D] + bias(B_ADA + 1))
        a = (normed * scale + (mod_ref[index, :, :D] + bias(B_ADA))).astype(BF)
        a_ref[index] = a
        for part in range(3):
            cut = slice(part * D, (part + 1) * D)
            product = dot(a, part_of(wqkv_ref, part, 3))
            if part != 1:
                product = product + bias(B_QUERY if part == 0 else B_VALUE)
            qkv_ref[index, :, cut] = product.astype(BF)
        for pair in range(PAIRS):
            base = pair * PAIR
            queries = qkv_ref[index, :, base : base + PAIR]
            keys = qkv_ref[index, :, D + base : D + base + PAIR]
            values = qkv_ref[index, :, 2 * D + base : 2 * D + base + PAIR]
            scores = dot_nt(both_heads(queries * jnp.asarray(HDIM**-0.5, BF), masks), keys)
            power = jnp.exp(scores - jnp.max(scores, -1, keepdims=True))
            total = jnp.sum(power, -1, keepdims=True)
            mixed = dot((power * (1.0 / total)).astype(BF), values)
            o_ref[index, :, base : base + PAIR] = jnp.where(masks[0], mixed[:SEQ], mixed[SEQ:]).astype(BF)
        return carry

    lax.fori_loop(0, images, image, 0)


ANYWHERE = pl.BlockSpec(memory_space=pl.ANY)


def attend(spot, noisy, pos, wpatch, mod, bias, pieces, shards, images=2):
    batch = noisy.shape[0]
    kept = (shards, 3 * D // shards, D)
    return pl.pallas_call(
        partial(attend_kernel, images=images),
        grid=(batch // images,),
        in_specs=[
            pl.BlockSpec(memory_space=pltpu.SMEM),
            rows(images, SEQ, PATCH),
            whole((SEQ, D)),
            whole((PATCH, D)),
            rows(images, 1, 8 * D),
            whole((BIASES, D)),
        ]
        + [ANYWHERE] * len(pieces),
        out_specs=[rows(images, SEQ, D), rows(images, SEQ, 3 * D), rows(images, SEQ, D), ANYWHERE],
        out_shape=[
            shape_of((batch, SEQ, D), BF),
            shape_of((batch, SEQ, 3 * D), BF),
            shape_of((batch, SEQ, D), BF),
            shape_of(kept, BF),
        ],
        scratch_shapes=[pltpu.VMEM(kept, BF), pltpu.SemaphoreType.DMA, pltpu.SemaphoreType.DMA],
        compiler_params=pltpu.CompilerParams(vmem_limit_bytes=VMEM_LIMIT),
        name="attend",
        cost_estimate=cost(32),
    )(spot, noisy, pos, wpatch, mod, bias, *pieces)


GELU_A = math.sqrt(2.0 / math.pi)
GELU_B = 0.044715


def gelu_both(u):
    square = u * u
    turn = jnp.tanh(u * (GELU_A + (GELU_A * GELU_B) * square))
    half = 0.5 + 0.5 * turn
    value = u * half
    slope = half + (value * (1.0 - half)) * (2.0 * GELU_A + (6.0 * GELU_A * GELU_B) * square)
    return value, slope


def feed_kernel(
    spot_ref, t_ref, noisy_ref, pos_ref, wpatch_ref, o_ref, mod_ref, bias_ref,
    head_ref, hbias_ref, vel_ref, *refs, images, count_all
):
    pieces, refs = refs[:-18], refs[-18:]
    mid_ref, y_ref, m_ref, g_ref, slope_ref, df_ref, ds_ref, dmod_ref, near_ref, far_ref, bdown_ref = refs[:11]
    kept1_ref, kept2_ref, weights_ref, tail_ref, order, sem, out_sem = refs[11:]
    step = pl.program_id(0)
    made = weight_copies(spot_ref, pieces, weights_ref, sem)
    up_width, out_width = kept1_ref.shape[1], kept2_ref.shape[1]
    keeps = [
        pltpu.make_async_copy(weights_ref.at[:, :up_width], kept1_ref, out_sem.at[0]),
        pltpu.make_async_copy(weights_ref.at[:, up_width:], kept2_ref, out_sem.at[1]),
    ]

    @pl.when(step == 0)
    def _():
        run_copies(made, True)
        run_copies(made, False)
        for keep in keeps:
            keep.start()

    @pl.when(step == pl.num_programs(0) - 1)
    def _():
        for keep in keeps:
            keep.wait()

    @pl.when(step == 0)
    def _():
        tail_ref[...] = jnp.zeros_like(tail_ref)
        bdown_ref[...] = jnp.zeros_like(bdown_ref)

    tokens = images * SEQ

    def bias(row):
        return bias_ref[row : row + 1, :]

    def spread(part):
        parts = []
        for index in range(images):
            row = mod_ref[index, :, (part + 2) * D : (part + 3) * D]
            row = row + bias(B_ADA + 2 + part if part < 4 else B_FINAL + part - 4)
            parts.append(jnp.broadcast_to(row, (SEQ, D)))
        return jnp.concatenate(parts, 0)

    def up_part(part):
        rows_of = up_width * D // FF
        return weights_ref[:, part * rows_of : (part + 1) * rows_of, :].reshape(D, D)

    def out_rows(part):
        first, taken = part * D, []
        while first < (part + 1) * D:
            place_of, row = first // out_width, first % out_width
            count = min(out_width - row, (part + 1) * D - first)
            taken.append(weights_ref[place_of, up_width + row : up_width + row + count, :])
            first += count
        return jnp.concatenate(taken, 0)

    position = jnp.concatenate([pos_ref[...] + bias(B_PATCH)] * images, 0)
    stream = dot(noisy_ref[...].reshape(tokens, PATCH), wpatch_ref[...]) + position
    y = dot(o_ref[...].reshape(tokens, D), out_rows(0)) + bias(B_PROJ)
    y_ref[...] = y.astype(BF).reshape(images, SEQ, D)
    mid = stream + spread(0) * y
    mid_ref[...] = mid.reshape(images, SEQ, D)
    normed, unused = norm_parts(mid)
    m = (normed * (1.0 + spread(2)) + spread(1)).astype(BF)
    m_ref[...] = m.reshape(images, SEQ, D)
    feed = jnp.broadcast_to(bias(B_DOWN), (tokens, D))
    for j in range(FF // D):
        cut = slice(j * D, (j + 1) * D)
        g, slope = gelu_both(dot(m, up_part(j)) + bias(B_UP + j))
        g = g.astype(BF)
        g_ref[:, cut] = g
        slope_ref[:, cut] = slope.astype(BF)
        feed = feed + dot(g, out_rows(j + 1))
    gate = spread(3)
    stream = mid + gate * feed
    normed, inverse = norm_parts(stream)
    scale = 1.0 + spread(5)
    z = (normed * scale + spread(4)).astype(BF)
    predicted = dot(z, head_ref[...]) + hbias_ref[...]
    t = jnp.concatenate(
        [jnp.full((SEQ, 1), t_ref[step * images + index], F32) for index in range(images)], 0
    )
    residual = predicted - vel_ref[...].reshape(tokens, OUT)
    weighted = t * residual
    loss = jnp.sum(jnp.sum(weighted * residual, 0, keepdims=True), 1, keepdims=True)
    tail_ref[OUT + 1 : OUT + 2, :] += jnp.broadcast_to(loss, (1, D))
    grad_pred = (2.0 * weighted / count_all).astype(BF)
    tail_ref[OUT : OUT + 1, :OUT] += jnp.sum(grad_pred.astype(F32), 0, keepdims=True)
    tail_ref[:OUT, :] += dot_tn(grad_pred, z)
    dz = dot_nt(grad_pred, head_ref[...])
    ds = norm_back(dz * scale, normed, inverse)
    ds_ref[...] = ds.reshape(images, SEQ, D)
    df = (ds * gate).astype(BF)
    df_ref[...] = df.reshape(images, SEQ, D)
    bdown_ref[...] += jnp.sum(df.astype(F32), 0, keepdims=True)
    for index in range(images):
        cut = slice(index * SEQ, (index + 1) * SEQ)
        dmod_ref[index, :, :D] = jnp.sum(ds[cut] * feed[cut], 0, keepdims=True)
        dmod_ref[index, :, D : 2 * D] = jnp.sum(dz[cut], 0, keepdims=True)
        dmod_ref[index, :, 2 * D :] = jnp.sum(dz[cut] * normed[cut], 0, keepdims=True)

    shards, taken = 2 * near_ref.shape[0], near_ref.shape[1]

    @pl.when(step == pl.num_programs(0) - 1)
    def _():
        for place_of in range(shards):
            order[place_of] = tail_ref[place_of * taken : (place_of + 1) * taken, :]
        for entry in range(shards):
            (far_ref if entry % 2 else near_ref)[entry // 2] = order[spot_ref[0] ^ entry]


def tail_rows(shards):
    return -(-(OUT + 2) // shards)


def feed(spot, t, noisy, pos, wpatch, o, mod, bias, head, hbias, velocity, pieces, shards, count_all, images=2):
    batch = o.shape[0]
    kept1 = (shards, FF // shards, D)
    kept2 = (shards, (D + FF) // shards, D)
    half = (shards // 2, tail_rows(shards), D)
    tokens = batch * SEQ
    return pl.pallas_call(
        partial(feed_kernel, images=images, count_all=count_all),
        grid=(batch // images,),
        in_specs=[
            pl.BlockSpec(memory_space=pltpu.SMEM),
            pl.BlockSpec(memory_space=pltpu.SMEM),
            rows(images, SEQ, PATCH),
            whole((SEQ, D)),
            whole((PATCH, D)),
            rows(images, SEQ, D),
            rows(images, 1, 8 * D),
            whole((BIASES, D)),
            whole((D, OUT)),
            whole((1, OUT)),
            rows(images, SEQ, OUT),
        ]
        + [ANYWHERE] * len(pieces),
        out_specs=[
            rows(images, SEQ, D),
            rows(images, SEQ, D),
            rows(images, SEQ, D),
            rows(images * SEQ, FF),
            rows(images * SEQ, FF),
            rows(images, SEQ, D),
            rows(images, SEQ, D),
            rows(images, 1, 3 * D),
            fixed(half),
            fixed(half),
            fixed((1, D)),
            ANYWHERE,
            ANYWHERE,
        ],
        out_shape=[
            shape_of((batch, SEQ, D), F32),
            shape_of((batch, SEQ, D), BF),
            shape_of((batch, SEQ, D), BF),
            shape_of((tokens, FF), BF),
            shape_of((tokens, FF), BF),
            shape_of((batch, SEQ, D), BF),
            shape_of((batch, SEQ, D), F32),
            shape_of((batch, 1, 3 * D), F32),
            shape_of(half, F32),
            shape_of(half, F32),
            shape_of((1, D), F32),
            shape_of(kept1, BF),
            shape_of(kept2, BF),
        ],
        scratch_shapes=[
            pltpu.VMEM((shards, kept1[1] + kept2[1], D), BF),
            pltpu.VMEM((shards * half[1], D), F32),
            pltpu.VMEM((shards,) + half[1:], F32),
            pltpu.SemaphoreType.DMA,
            pltpu.SemaphoreType.DMA((2,)),
        ],
        compiler_params=pltpu.CompilerParams(vmem_limit_bytes=VMEM_LIMIT),
        name="feed",
        cost_estimate=cost(52),
    )(spot, t, noisy, pos, wpatch, o, mod, bias, head, hbias, velocity, *pieces)


def feed_back_kernel(
    m_ref, df_ref, g_ref, slope_ref, w1_ref, w2_ref, wup_ref, wdown_ref, bup_ref, dm_ref, mt, dft, *, tile
):
    step = pl.program_id(0)

    @pl.when(step == 0)
    def _():
        mt[...] = m_ref[...].T
        dft[...] = df_ref[...].T
        dm_ref[...] = jnp.zeros_like(dm_ref)

    tokens = m_ref.shape[0]
    w1 = w1_ref[...].reshape(D, D)
    w2 = w2_ref[...]
    du_parts = []
    for i in range(tokens // tile):
        cut = slice(i * tile, (i + 1) * tile)
        du = (dot_nt(df_ref[cut, :], w2) * slope_ref[cut, :].astype(F32)).astype(BF)
        du_parts.append(du)
        dm_ref[cut, :] += dot_nt(du, w1)
    du = jnp.concatenate(du_parts, 0)
    bup_ref[...] = jnp.sum(du.astype(F32), 0, keepdims=True)
    wup_ref[...] = dot(mt[...], du).astype(BF).reshape(wup_ref.shape)
    wdown_ref[...] = dot(dft[...], g_ref[...]).T.astype(BF)


def feed_back(m, df, g, slope, w1, wout, first, last, tile=512):
    chunk = D
    shards = w1.shape[0]
    rows_of = D // shards
    tokens = m.shape[0]
    steps = (last - first) // chunk
    base = first // chunk
    return pl.pallas_call(
        partial(feed_back_kernel, tile=tile),
        grid=(steps,),
        in_specs=[
            whole((tokens, D)),
            whole((tokens, D)),
            pl.BlockSpec((tokens, chunk), lambda step: (0, step + base)),
            pl.BlockSpec((tokens, chunk), lambda step: (0, step + base)),
            pl.BlockSpec((shards, rows_of, D), lambda step: (0, step + base, 0)),
            pl.BlockSpec((chunk, D), lambda step: (step + base + D // chunk, 0)),
        ],
        out_specs=[
            pl.BlockSpec((shards, rows_of, D), lambda step: (0, step, 0)),
            pl.BlockSpec((chunk, D), lambda step: (step + base + D // chunk, 0)),
            pl.BlockSpec((1, chunk), lambda step: (0, step)),
            pl.BlockSpec((tokens, D), lambda step: (0, 0), pipeline_mode=pl.Buffered(1)),
        ],
        out_shape=[
            shape_of((shards, steps * rows_of, D), BF),
            shape_of((D + FF, D), BF),
            shape_of((1, last - first), F32),
            shape_of((tokens, D), F32),
        ],
        scratch_shapes=[pltpu.VMEM((D, tokens), BF), pltpu.VMEM((D, tokens), BF)],
        compiler_params=pltpu.CompilerParams(vmem_limit_bytes=VMEM_LIMIT),
        name="feed_back",
        cost_estimate=cost(51),
    )(m, df, g, slope, w1, wout)


def middle_back_kernel(
    mid_ref, dm_ref, ds_ref, y_ref, o_ref, mod_ref, bias_ref, wproj_ref, gout_ref,
    dmid_ref, do_ref, dmod_ref, wproj_out_ref, bproj_ref, total, *, images
):
    step = pl.program_id(0)

    @pl.when(step == 0)
    def _():
        total[...] = jnp.zeros_like(total)
        bproj_ref[...] = jnp.zeros_like(bproj_ref)

    tokens = images * SEQ
    dy_parts = []
    for index in range(images):
        normed, inverse = norm_parts(mid_ref[index])
        dm = dm_ref[index]
        dmid = ds_ref[index] + norm_back(
            dm * (1.0 + (mod_ref[index, :, 4 * D : 5 * D] + bias_ref[B_ADA + 4 : B_ADA + 5, :])), normed, inverse
        )
        dmid_ref[index] = dmid
        dmod_ref[index, :, :D] = jnp.sum(dmid * y_ref[index].astype(F32), 0, keepdims=True)
        dmod_ref[index, :, D : 2 * D] = jnp.sum(dm, 0, keepdims=True)
        dmod_ref[index, :, 2 * D :] = jnp.sum(dm * normed, 0, keepdims=True)
        gate = mod_ref[index, :, 2 * D : 3 * D] + bias_ref[B_ADA + 2 : B_ADA + 3, :]
        dy_parts.append((dmid * gate).astype(BF))
    dy = jnp.concatenate(dy_parts, 0)
    bproj_ref[...] += jnp.sum(dy.astype(F32), 0, keepdims=True)
    do_ref[...] = dot_nt(dy, wproj_ref[...]).astype(BF).reshape(images, SEQ, D)
    total[...] += dot_tn(o_ref[...].reshape(tokens, D), dy)

    @pl.when(step == pl.num_programs(0) - 1)
    def _():
        wproj_out_ref[...] = total[...].astype(BF)


def middle_back(mid, dm, ds, y, o, mod, bias, wout, gout, images=2):
    batch = mid.shape[0]
    return pl.pallas_call(
        partial(middle_back_kernel, images=images),
        grid=(batch // images,),
        in_specs=[
            rows(images, SEQ, D),
            rows(images, SEQ, D),
            rows(images, SEQ, D),
            rows(images, SEQ, D),
            rows(images, SEQ, D),
            rows(images, 1, 8 * D),
            whole((BIASES, D)),
            whole((D, D)),
            pl.BlockSpec(memory_space=pl.ANY),
        ],
        out_specs=[
            rows(images, SEQ, D),
            rows(images, SEQ, D),
            rows(images, 1, 3 * D),
            fixed((D, D)),
            fixed((1, D)),
        ],
        out_shape=[
            shape_of((batch, SEQ, D), F32),
            shape_of((batch, SEQ, D), BF),
            shape_of((batch, 1, 3 * D), F32),
            shape_of((D + FF, D), BF),
            shape_of((1, D), F32),
        ],
        input_output_aliases={8: 3},
        scratch_shapes=[pltpu.VMEM((D, D), F32)],
        compiler_params=pltpu.CompilerParams(vmem_limit_bytes=VMEM_LIMIT),
        name="middle_back",
        cost_estimate=cost(18),
    )(mid, dm, ds, y, o, mod, bias, wout, gout)


def attend_back_kernel(spot_ref, qkv_ref, do_ref, a_ref, dqkv_ref, mine_ref, theirs_ref, bqkv_ref, total, *, images):
    step = pl.program_id(0)

    @pl.when(step == 0)
    def _():
        total[...] = jnp.zeros_like(total)
        bqkv_ref[...] = jnp.zeros_like(bqkv_ref)

    masks = head_masks()
    tokens = images * SEQ

    def image(index, carry):
        for pair in range(PAIRS):
            base = pair * PAIR
            scale = jnp.asarray(HDIM**-0.5, BF)
            queries = both_heads(qkv_ref[index, :, base : base + PAIR] * scale, masks)
            keys = qkv_ref[index, :, D + base : D + base + PAIR]
            values = qkv_ref[index, :, 2 * D + base : 2 * D + base + PAIR]
            grads = both_heads(do_ref[index, :, base : base + PAIR], masks)
            scores = dot_nt(keys, queries)
            power = jnp.exp(scores - jnp.max(scores, 0, keepdims=True))
            prob = power * (1.0 / jnp.sum(power, 0, keepdims=True))
            dprob = dot_nt(values, grads)
            delta = jnp.sum(prob * dprob, 0, keepdims=True)
            dscore = (prob * (dprob - delta)).astype(BF)
            dv = dot(prob.astype(BF), grads)
            dk = dot(dscore, queries)
            dq = dot_tn(dscore, keys * scale)
            dq = jnp.where(masks[0], dq[:SEQ], dq[SEQ:])
            dqkv_ref[index, :, base : base + PAIR] = dq.astype(BF)
            dqkv_ref[index, :, D + base : D + base + PAIR] = dk.astype(BF)
            dqkv_ref[index, :, 2 * D + base : 2 * D + base + PAIR] = dv.astype(BF)
        return carry

    lax.fori_loop(0, images, image, 0)
    dqkv = dqkv_ref[...].reshape(tokens, 3 * D)
    total[...] += dot_tn(a_ref[...].reshape(tokens, D), dqkv)
    bqkv_ref[...] += jnp.sum(dqkv.astype(F32), 0, keepdims=True)

    @pl.when(step == pl.num_programs(0) - 1)
    def _():
        width = mine_ref.shape[1] // 3
        core = lax.rem(spot_ref[0], 2)
        for pair in range(mine_ref.shape[0]):
            for out_ref, side in ((mine_ref, core), (theirs_ref, 1 - core)):
                start = pl.multiple_of((2 * pair + side) * width, 16)
                for part in range(3):
                    block = total[pl.ds(start, width), part * D : (part + 1) * D]
                    out_ref[pair, part * width : (part + 1) * width, :] = block.astype(BF)


def attend_back(spot, qkv, do, a, shards, images=2):
    batch = qkv.shape[0]
    half = (shards // 2, 3 * D // shards, D)
    return pl.pallas_call(
        partial(attend_back_kernel, images=images),
        grid=(batch // images,),
        in_specs=[pl.BlockSpec(memory_space=pltpu.SMEM)]
        + [rows(images, SEQ, 3 * D), rows(images, SEQ, D), rows(images, SEQ, D)],
        out_specs=[rows(images, SEQ, 3 * D), fixed(half), fixed(half), fixed((1, 3 * D))],
        out_shape=[
            shape_of((batch, SEQ, 3 * D), BF),
            shape_of(half, BF),
            shape_of(half, BF),
            shape_of((1, 3 * D), F32),
        ],
        scratch_shapes=[pltpu.VMEM((D, 3 * D), F32)],
        compiler_params=pltpu.CompilerParams(vmem_limit_bytes=VMEM_LIMIT),
        name="attend_back",
        cost_estimate=cost(45),
    )(spot, qkv, do, a)


def stream_back_kernel(
    spot_ref, dqkv_ref, dmid_ref, noisy_ref, pos_ref, wpatch_ref, mod_ref, bias_ref, wqkv_ref,
    dmod_ref, near_ref, far_ref, bpatch_ref, wpatch_out_ref, order, *, images
):
    step = pl.program_id(0)

    @pl.when(step == 0)
    def _():
        wpatch_out_ref[...] = jnp.zeros_like(wpatch_out_ref)
        bpatch_ref[...] = jnp.zeros_like(bpatch_ref)

    tokens = images * SEQ
    dqkv = dqkv_ref[...].reshape(tokens, 3 * D)
    da = sum(dot_nt(dqkv[:, part * D : (part + 1) * D], part_of(wqkv_ref, part, 3)) for part in range(3))
    for index in range(images):
        noisy = noisy_ref[index]
        stream = dot(noisy, wpatch_ref[...]) + (pos_ref[...] + bias_ref[B_PATCH : B_PATCH + 1, :])
        scale = 1.0 + (mod_ref[index, :, D : 2 * D] + bias_ref[B_ADA + 1 : B_ADA + 2, :])
        normed, inverse = norm_parts(stream)
        part = da[index * SEQ : (index + 1) * SEQ]
        dmod_ref[index, :, :D] = jnp.sum(part, 0, keepdims=True)
        dmod_ref[index, :, D:] = jnp.sum(part * normed, 0, keepdims=True)
        dstream = dmid_ref[index] + norm_back(part * scale, normed, inverse)
        embedded = dstream.astype(BF)
        bpatch_ref[...] += jnp.sum(embedded.astype(F32), 0, keepdims=True)
        wpatch_out_ref[...] += dot_tn(noisy, embedded)

    width = near_ref.shape[2]
    shards = D // width

    @pl.when(step == pl.num_programs(0) - 1)
    def _():
        for place_of in range(shards):
            order[place_of] = wpatch_out_ref[:, place_of * width : (place_of + 1) * width]
        for entry in range(shards):
            (far_ref if entry % 2 else near_ref)[entry // 2] = order[spot_ref[0] ^ entry]


def stream_back(spot, dqkv, dmid, noisy, pos, wpatch, mod, bias, wqkv, images=2):
    batch = dqkv.shape[0]
    half = (wqkv.shape[0] // 2, PATCH, D // wqkv.shape[0])
    return pl.pallas_call(
        partial(stream_back_kernel, images=images),
        grid=(batch // images,),
        in_specs=[
            pl.BlockSpec(memory_space=pltpu.SMEM),
            rows(images, SEQ, 3 * D),
            rows(images, SEQ, D),
            rows(images, SEQ, PATCH),
            whole((SEQ, D)),
            whole((PATCH, D)),
            rows(images, 1, 8 * D),
            whole((BIASES, D)),
            whole(wqkv.shape),
        ],
        out_specs=[rows(images, 1, 2 * D), fixed(half), fixed(half), fixed((1, D))],
        out_shape=[
            shape_of((batch, 1, 2 * D), F32),
            shape_of(half, F32),
            shape_of(half, F32),
            shape_of((1, D), F32),
        ],
        scratch_shapes=[pltpu.VMEM((PATCH, D), F32), pltpu.VMEM((2 * half[0],) + half[1:], F32)],
        compiler_params=pltpu.CompilerParams(vmem_limit_bytes=VMEM_LIMIT),
        name="stream_back",
        cost_estimate=cost(19),
    )(spot, dqkv, dmid, noisy, pos, wpatch, mod, bias, wqkv)


MARKS = 4
PATCH_ROW = TFREQ
BIAS_ROW = TFREQ + PATCH
MESSAGE = 304


def condition_kernel(spot_ref, near_ref, other_ref, times_ref, embed_ref, table_ref, *rest, team):
    me = spot_ref[0]
    width = embed_ref.shape[1]
    shards = D // width
    messages = [(other_ref if entry % 2 else near_ref).at[entry // 2] for entry in range(shards)]
    if team:
        in_ref, final_ref, time_pre_ref, condition_ref, marks_ref, wpatch_ref, bias_ref = rest[:7]
        near_mod_ref, far_mod_ref, table, bias_rows, order = rest[7:]
        batch = near_mod_ref.shape[1]
        marks = jnp.concatenate(
            [message[:batch, width : width + MARKS].astype(F32) for message in messages], 0
        )
        marks_ref[...] = marks
    else:
        groups_marks, (marks_ref, features_ref, time_act_ref, act_ref, table, bias_rows, order) = rest[:-7], rest[-7:]
        team_count = groups_marks[0].shape[0]
        for entry, part in enumerate(groups_marks):
            start = pl.multiple_of((spot_ref[1] ^ entry) * team_count, team_count)
            marks_ref[pl.ds(start, team_count), :] = part[...]
        marks = marks_ref[...]
    count = marks.shape[0]
    marks = marks.astype(jnp.int32)
    index = marks[:, 0:1] * 32 + marks[:, 1:2]
    label = marks[:, 2:3] * 32 + marks[:, 3:4]

    for entry in range(shards):
        bias_rows[me ^ entry] = messages[entry][BIAS_ROW : BIAS_ROW + BIASES, :width].astype(F32)
        if team:
            order[me ^ entry] = messages[entry][PATCH_ROW : PATCH_ROW + PATCH, :width]

    def bias_row(row):
        return bias_rows[lax.div(row, BIASES), pl.ds(lax.rem(row, BIASES), 1), :]

    entry = lax.broadcasted_iota(jnp.int32, (count, times_ref.shape[1]), 1)
    moment = jnp.sum(jnp.where(entry == index, times_ref[...], 0.0), 1, keepdims=True)
    half = TFREQ // 2
    frequency = lax.broadcasted_iota(jnp.int32, (1, half), 1).astype(F32)
    angles = moment * jnp.exp(-math.log(10000.0) * frequency / half)
    features = jnp.concatenate([jnp.cos(angles), jnp.sin(angles)], 1).astype(BF)
    table[...] = jnp.zeros_like(table)
    table[:, :NCLASS] = table_ref[...].astype(BF)
    entry = lax.broadcasted_iota(jnp.int32, (count, table.shape[1]), 1)
    onehot = (entry == label).astype(F32).astype(BF)
    condition = dot_nt(onehot, table[...]) + bias_row(B_CLASS * shards + me)
    for entry in range(shards):
        place_of = me ^ entry
        time_pre = dot(features, messages[entry][:TFREQ, :width])
        time_pre = time_pre + bias_row(B_TIME * shards + place_of)
        time_act = (time_pre * (1.0 / (1.0 + jnp.exp(-time_pre)))).astype(BF)
        start = pl.multiple_of(TFREQ + PATCH + place_of * width, 16)
        condition = condition + dot(time_act, embed_ref[pl.ds(start, width), :])
        if team:
            if entry == 0:
                for block in range(shards):
                    time_pre_ref[me ^ block] = time_pre[block * batch : (block + 1) * batch, :]
        else:
            time_act_ref[place_of] = time_act
    act = (condition * (1.0 / (1.0 + jnp.exp(-condition)))).astype(BF)
    if not team:
        features_ref[...] = features
        act_ref[...] = act
        return
    condition_ref[...] = condition
    for place_of in range(shards):
        wpatch_ref[:, place_of * width : (place_of + 1) * width] = order[place_of]
    for row in range(BIASES):
        for column in range(shards):
            holder, inner = divmod(row * shards + column, BIASES)
            bias_ref[row : row + 1, column * width : (column + 1) * width] = bias_rows[
                holder, inner : inner + 1, :
            ]
    part = jnp.concatenate([dot(act, in_ref[0].astype(BF)), dot(act, final_ref[...].astype(BF))], 1)
    for pair in range(shards // 2):
        row = 2 * pair * batch
        near_mod_ref[pair] = part[row : row + batch, :]
        far_mod_ref[pair] = part[row + batch : row + 2 * batch, :]


def condition_call(operands, in_specs, out_shape, width, team):
    shards = D // width
    return pl.pallas_call(
        partial(condition_kernel, team=team),
        grid=(1,),
        in_specs=[pl.BlockSpec(memory_space=pltpu.SMEM)] + in_specs,
        out_specs=[whole(out.shape) for out in out_shape],
        out_shape=out_shape,
        scratch_shapes=[
            pltpu.VMEM((width, 1024), BF),
            pltpu.VMEM((shards, BIASES, width), F32),
            pltpu.VMEM((shards, PATCH, width), BF),
        ],
        compiler_params=pltpu.CompilerParams(vmem_limit_bytes=VMEM_LIMIT),
        name="condition",
        cost_estimate=cost(6),
    )(*operands)


def condition_of_team(spot, near, other, times, embed, table, in_mats, final, batch):
    width = embed.shape[1]
    shards = D // width
    count = shards * batch
    operands = [spot, near, other, times, embed, table, in_mats, final]
    in_specs = [whole(part.shape) for part in operands[1:6]]
    in_specs += [pl.BlockSpec((1, width, 6 * D), lambda step: (0, 0, 0)), whole(final.shape)]
    half = (shards // 2, batch)
    out_shape = [
        shape_of((shards, batch, width), F32),
        shape_of((count, width), F32),
        shape_of((count, MARKS), F32),
        shape_of((PATCH, D), BF),
        shape_of((BIASES, D), F32),
        shape_of(half + (8 * D,), F32),
        shape_of(half + (8 * D,), F32),
    ]
    return condition_call(operands, in_specs, out_shape, width, True)


def condition_of_all(spot, near, other, times, embed, table, marks):
    width = embed.shape[1]
    count = len(marks) * marks[0].shape[0]
    operands = [spot, near, other, times, embed, table] + marks
    out_shape = [
        shape_of((count, MARKS), F32),
        shape_of((count, TFREQ), BF),
        shape_of((D // width, count, width), BF),
        shape_of((count, width), BF),
    ]
    return condition_call(operands, [whole(part.shape) for part in operands[1:]], out_shape, width, False)


def condition_back_kernel(
    spot_ref, near_ref, other_ref, early_near_ref, early_other_ref, condition_ref, in_ref, final_ref, embed_ref,
    late_ref, grad_ref, near_act_ref, far_act_ref, order
):
    me = spot_ref[0]
    pairs, width = near_ref.shape[0], embed_ref.shape[1]
    late = jnp.concatenate([ref[pair] for pair in range(pairs) for ref in (near_ref, other_ref)], 0)
    late_ref[...] = late
    early = [ref[pair, 0] for pair in range(pairs) for ref in (early_near_ref, early_other_ref)]
    early = jnp.concatenate(early, 0)
    grad = dot_nt(late, in_ref[0, :, : 5 * D].astype(BF))
    grad = grad + dot_nt(early[:, :D], in_ref[0, :, 5 * D :].astype(BF))
    grad = grad + dot_nt(early[:, D:], final_ref[...].astype(BF))
    condition = condition_ref[...]
    turn = 1.0 / (1.0 + jnp.exp(-condition))
    grad = grad * (turn * (1.0 + condition * (1.0 - turn)))
    batch = order.shape[1]
    for block in range(2 * pairs):
        order[me ^ block] = grad[block * batch : (block + 1) * batch, :]
    grad = order[...].reshape(grad.shape).astype(BF)
    grad_ref[...] = grad
    for entry in range(2 * pairs):
        start = pl.multiple_of(TFREQ + PATCH + (me ^ entry) * width, 16)
        part = dot_nt(grad, embed_ref[pl.ds(start, width), :])
        (far_act_ref if entry % 2 else near_act_ref)[entry // 2] = part


def condition_back(spot, near, other, early_near, early_other, condition, in_mats, final, embed):
    width = embed.shape[1]
    count = condition.shape[0]
    operands = [spot, near, other, early_near, early_other, condition, in_mats, final, embed]
    in_specs = [pl.BlockSpec(memory_space=pltpu.SMEM)] + [whole(part.shape) for part in operands[1:6]]
    in_specs += [pl.BlockSpec((1, width, 6 * D), lambda step: (0, 0, 0)), whole(final.shape), whole(embed.shape)]
    half = (near.shape[0], count, width)
    out_shape = [
        shape_of((count, 5 * D), BF),
        shape_of((count, width), BF),
        shape_of(half, F32),
        shape_of(half, F32),
    ]
    return pl.pallas_call(
        condition_back_kernel,
        grid=(1,),
        in_specs=in_specs,
        out_specs=[whole(out.shape) for out in out_shape],
        out_shape=out_shape,
        scratch_shapes=[pltpu.VMEM((2 * half[0], near.shape[1], width), F32)],
        compiler_params=pltpu.CompilerParams(vmem_limit_bytes=VMEM_LIMIT),
        name="condition_back",
        cost_estimate=cost(4),
    )(*operands)


BIAS_PARTS = (B_PATCH, B_QUERY, B_VALUE, B_PROJ, B_UP, B_UP + 1, B_UP + 2, B_UP + 3, B_DOWN)


def condition_grads_kernel(spot_ref, marks_ref, features_ref, time_act_ref, act_ref, early_near_ref, early_other_ref, *refs, groups):
    late, last, refs = refs[:groups], refs[groups : 2 * groups], refs[2 * groups :]
    gada_ref, gembed_ref, gtable_ref, bias_ref, message_ref, squares_ref = refs[:6]
    early_all, late_all, grads_all = refs[6:]
    me, group = spot_ref[0], spot_ref[1]
    team = late[0].shape[0]
    width = act_ref.shape[1]
    shards = D // width
    for entry in range(groups):
        here = pl.ds(pl.multiple_of((group ^ entry) * team, team), team)
        early = [ref[pair, entry] for pair in range(shards // 2) for ref in (early_near_ref, early_other_ref)]
        early_all[here, :] = jnp.concatenate(early, 0)
        late_all[here, :] = late[entry][...]
        for part in range(2):
            blocks = []
            for block in range(shards):
                start = pl.multiple_of(part * team + (me ^ block) * (team // shards), 8)
                blocks.append(last[entry][pl.ds(start, team // shards), :])
            grads_all[here, part * width : (part + 1) * width] = jnp.concatenate(blocks, 0).astype(BF)
    rest = [ref[2 * team :, :] for ref in last]
    while len(rest) > 1:
        rest = [rest[i] + rest[i + 1] for i in range(0, len(rest), 2)]
    rest = rest[0]
    act = act_ref[...]
    grad_time = grads_all[:, :width]
    grad_condition = grads_all[:, width:]
    gada_ref[:, : 5 * D] = dot_tn(act, late_all[...])
    gada_ref[:, 5 * D :] = dot_tn(act, early_all[...])
    marks = marks_ref[...].astype(jnp.int32)
    label = marks[:, 2:3] * 32 + marks[:, 3:4]
    entry = lax.broadcasted_iota(jnp.int32, (marks.shape[0], 1024), 1)
    onehot = (entry == label).astype(F32).astype(BF)
    gtable_ref[...] = dot_tn(grad_condition, onehot)[:, :NCLASS]
    early_rows = PATCH + TFREQ
    gembed_ref[:, :PATCH] = rest[:PATCH, :].T
    gembed_ref[:, PATCH:early_rows] = dot_tn(grad_time, features_ref[...])
    for entry in range(shards):
        start = early_rows + entry * width
        gembed_ref[:, start : start + width] = dot_tn(grad_condition, time_act_ref[entry])
    late_sum = jnp.sum(late_all[...].astype(F32), 0, keepdims=True)
    early_sum = jnp.sum(early_all[...].astype(F32), 0, keepdims=True)
    bias_ref[B_TIME : B_ADA, :] = jnp.zeros((2, D), F32)
    for part in range(5):
        bias_ref[B_ADA + part : B_ADA + part + 1, :] = late_sum[:, part * D : (part + 1) * D]
    for part in range(3):
        row = B_FINAL + part - 1 if part else B_ADA + 5
        bias_ref[row : row + 1, :] = early_sum[:, part * D : (part + 1) * D]
    for part, row in enumerate(BIAS_PARTS):
        for column in range(shards):
            first = PATCH + part * shards + column
            bias_ref[row : row + 1, column * width : (column + 1) * width] = rest[first : first + 1, :]
    btime = jnp.sum(grads_all[...].astype(F32), 0, keepdims=True)
    message_ref[0:1, :] = btime[:, :width]
    message_ref[1:2, :] = btime[:, width:]
    tail = rest[PATCH + len(BIAS_PARTS) * shards :, :]
    message_ref[2:, :] = tail
    taken = tail.shape[0] // shards
    row = lax.broadcasted_iota(jnp.int32, tail.shape, 0) // shards + spot_ref[0] * taken
    head = jnp.where(row <= OUT, tail, 0.0)

    def square(part):
        return jnp.sum(jnp.sum(part * part, 0, keepdims=True), 1, keepdims=True)

    squares_ref[...] = square(gada_ref[...]) + square(gembed_ref[...]) + square(gtable_ref[...]) + square(btime) + square(head)


def condition_grads(spot, marks, features, time_act, act, early_near, early_other, late, last):
    groups = len(late)
    count, width = act.shape
    operands = [spot, marks, features, time_act, act, early_near, early_other] + late + last
    shards = D // width
    out_shape = [
        shape_of((width, 8 * D), F32),
        shape_of((width, PATCH + TFREQ + D), F32),
        shape_of((width, NCLASS), F32),
        shape_of((BIASES, D), F32),
        shape_of((2 + tail_rows(shards) * shards, width), F32),
        shape_of((1, 1), F32),
    ]
    return pl.pallas_call(
        partial(condition_grads_kernel, groups=groups),
        grid=(1,),
        in_specs=[pl.BlockSpec(memory_space=pltpu.SMEM)] + [whole(part.shape) for part in operands[1:]],
        out_specs=[whole(out.shape) for out in out_shape],
        out_shape=out_shape,
        scratch_shapes=[
            pltpu.VMEM((count, 3 * D), BF),
            pltpu.VMEM((count, 5 * D), BF),
            pltpu.VMEM((count, 2 * width), BF),
        ],
        compiler_params=pltpu.CompilerParams(vmem_limit_bytes=VMEM_LIMIT),
        name="condition_grads",
        cost_estimate=cost(6),
    )(*operands)


def swap(array_in, axis, hop):
    count = lax.axis_size(axis)
    return lax.ppermute(array_in, axis, [(place_of, place_of ^ hop) for place_of in range(count)])


def spread(array_in, axis):
    count = lax.axis_size(axis)
    if axis == "shard":
        near = jnp.stack([array_in] + [swap(array_in, axis, hop) for hop in range(2, count, 2)])
        return jnp.stack([near, swap(near, axis, 1)], 1).reshape((count,) + array_in.shape)
    return jnp.stack([array_in] + [swap(array_in, axis, hop) for hop in range(1, count)])


def total_of(parts):
    while len(parts) > 1:
        parts = [parts[i] + parts[i + 1] for i in range(0, len(parts), 2)]
    return parts[0]


def exchange_sum(near):
    return total_of([near[0]] + [swap(near[hop], "shard", 2 * hop) for hop in range(1, near.shape[0])])


def from_groups(array_in, tuned, first=1):
    count = lax.axis_size("grp")
    if tuned:
        pair = jnp.stack([array_in, swap(array_in, "grp", first)])
        far = swap(pair, "grp", 3 - first)
        parts = [pair[0], pair[1], far[0], far[1]]
        return parts if first == 1 else [parts[0], parts[2], parts[1], parts[3]]
    parts = jnp.broadcast_to(array_in[None], (count,) + array_in.shape)
    parts = ordered(lax.all_to_all(parts, "grp", 0, 0, tiled=True), "grp")
    return [parts[i] for i in range(count)]


def ordered(array_in, axis):
    count = lax.axis_size(axis)
    place_of = lax.axis_index(axis)
    bit = 1
    while bit < count:
        pairs = array_in.reshape((count // (2 * bit), 2, bit) + array_in.shape[1:])
        array_in = jnp.where(place_of & bit != 0, pairs[:, ::-1], pairs).reshape(array_in.shape)
        bit *= 2
    return array_in


def sum_spread(array_in, axis):
    parts = spread(array_in, axis)
    return total_of([parts[i] for i in range(parts.shape[0])])


def tie(arrays, after):
    return lax.optimization_barrier((arrays, after))[0]


DIRECT = 224


def rows_near(own):
    rows_all = own.shape[0]
    quarter = -(-rows_all // 64) * 16
    group = lax.axis_index("grp")
    start = jnp.where(group == 3, rows_all - quarter, group * quarter)
    part = lax.dynamic_slice_in_dim(own, start, quarter, 0)
    return [swap(part, "shard", hop) for hop in (2, 4, 6)]


def rows_far(near):
    return lax.all_gather(jnp.stack(near), "grp")


def rows_all(own, far):
    return [own, far, swap(own, "shard", 1), swap(far, "shard", 1)]


def quarter_start(rows_all, quarter, group):
    return jnp.where(group == 3, rows_all - quarter, group * quarter)


def cores_summed(grads):
    pairs = grads.reshape((4, 2) + grads.shape[1:])
    core = lax.axis_index("shard") % 2
    theirs = lax.dynamic_index_in_dim(pairs, 1 - core, 1, keepdims=False)
    mine = lax.dynamic_index_in_dim(pairs, core, 1, keepdims=False)
    return lower(mine.astype(F32) + swap(theirs, "shard", 1).astype(F32))


def groups_traded(grads):
    group = lax.axis_index("grp")
    rows_all = grads.shape[1]
    quarter = -(-rows_all // 64) * 16
    parts = []
    for hop in range(4):
        start = quarter_start(rows_all, quarter, group ^ hop)
        part = lax.dynamic_slice_in_dim(grads, start, quarter, 1)
        parts.append(swap(part, "grp", hop) if hop else part)
    return parts


def shards_traded(parts):
    return chips_traded(total_of([part.astype(F32) for part in parts]))


def chips_traded(total):
    low = lower(total)
    chip = lax.axis_index("shard") // 2
    own = lax.dynamic_index_in_dim(total, chip, 0, keepdims=False)
    return [own] + [
        swap(lax.dynamic_index_in_dim(low, chip ^ hop, 0, keepdims=False), "shard", 2 * hop) for hop in (1, 2, 3)
    ]


def shards_summed(parts):
    return lower(total_of([part.astype(F32) for part in parts]))


def quarters_joined(parts, *sizes):
    joined, first = [], 0
    for quarter, count in sizes:
        part = parts[:, first : first + quarter]
        first += quarter
        skipped = 4 * quarter - count // 8
        joined.append(jnp.concatenate([part[0], part[1], part[2], part[3, skipped:]]).astype(F32))
    return joined


def halves_added(part, bit):
    axis = part.ndim - 2
    half = part.shape[axis] // 2
    side = (lax.axis_index("grp") // bit) % 2
    ours = lax.dynamic_slice_in_dim(part, side * half, half, axis)
    theirs = lax.dynamic_slice_in_dim(part, (1 - side) * half, half, axis)
    return [ours, swap(theirs, "grp", bit)]


def matmul(formula, left, right):
    return jnp.einsum(formula, left, right, preferred_element_type=F32)


def lower(array_in):
    return array_in.astype(BF)


def summed(array_in, axes):
    return jnp.sum(array_in.astype(F32), axes)


def position_table():
    quarter = D // 4
    angular = np.exp(-math.log(10000.0) * np.arange(quarter) / quarter)
    position = np.arange(GRID * GRID)
    column = (position % GRID)[:, None] * angular
    row_pos = (position // GRID)[:, None] * angular
    table = np.concatenate([np.sin(column), np.cos(column), np.sin(row_pos), np.cos(row_pos)], 1)
    return jnp.asarray(table.astype(np.float32))


def pick_times(time_index, times):
    matches = time_index[:, None] == jnp.arange(times.shape[0], dtype=jnp.int32)[None, :]
    return jnp.sum(jnp.where(matches, times[None, :], 0.0), 1)


def condition_grads_plain(spot, marks, features, time_act, act, early_near, early_other, late, last):
    team, width = late[0].shape[0], act.shape[1]
    shards = D // width

    def in_exchange(part):
        part = part.reshape(2, shards, team // shards, width).transpose(1, 0, 2, 3)
        return ordered(part, "shard").transpose(1, 0, 2, 3).reshape(2 * team, width)

    early = jnp.stack([early_near, early_other], 1).transpose(2, 0, 1, 3, 4)
    early = early.reshape(len(late), team, 3 * D)
    early, late, last_all = [
        ordered(jnp.stack(parts), "grp").reshape(-1, parts[0].shape[1])
        for parts in (list(early), late, [in_exchange(part[: 2 * team]) for part in last])
    ]
    last_all = lower(last_all).reshape(-1, 2, team, width)
    grad_time, grad_condition = last_all[:, 0].reshape(-1, width), last_all[:, 1].reshape(-1, width)
    rest = total_of([part[2 * team :] for part in last])
    gada = jnp.concatenate([matmul("bd,be->de", act, late), matmul("bd,be->de", act, early)], 1)
    labels = (marks[:, 2:3] * 32.0 + marks[:, 3:4]).astype(jnp.int32)
    onehot = lower((labels == jnp.arange(NCLASS, dtype=jnp.int32)[None, :]).astype(F32))
    gtable = matmul("bd,bn->dn", grad_condition, onehot)
    gembed = jnp.concatenate(
        [
            rest[:PATCH].T,
            matmul("bd,bf->df", grad_time, features),
            matmul("be,sbd->esd", grad_condition, time_act).reshape(width, D),
        ],
        1,
    )
    bias = jnp.zeros((BIASES, D), F32)
    bias = bias.at[B_ADA : B_ADA + 5].set(summed(late, 0).reshape(5, D))
    early_sum = summed(early, 0).reshape(3, D)
    bias = bias.at[B_ADA + 5].set(early_sum[0]).at[B_FINAL:].set(early_sum[1:])
    parts = rest[PATCH : PATCH + len(BIAS_PARTS) * shards].reshape(len(BIAS_PARTS), D)
    for part, row in enumerate(BIAS_PARTS):
        bias = bias.at[row].set(parts[part])
    btime = jnp.stack([summed(grad_time, 0), summed(grad_condition, 0)])
    tail = rest[PATCH + len(BIAS_PARTS) * shards :]
    taken = tail.shape[0] // shards
    row = jnp.arange(tail.shape[0], dtype=jnp.int32)[:, None] // shards + spot[0] * taken
    head = jnp.where(row <= OUT, tail, 0.0)
    squares = sum(jnp.sum(part * part) for part in (gada, gembed, gtable, btime, head))
    return gada, gembed, gtable, bias, jnp.concatenate([btime, tail]), squares.reshape(1, 1)


def adamw(weight, moment_one, moment_two, gradient, factor):
    gradient = gradient * factor
    moment_one = BETA_ONE * moment_one + (1.0 - BETA_ONE) * gradient
    moment_two = BETA_TWO * moment_two + (1.0 - BETA_TWO) * gradient * gradient
    fix_one = 1.0 - BETA_ONE**STEP
    fix_two = 1.0 - BETA_TWO**STEP
    update = (
        moment_one / fix_one / (jnp.sqrt(moment_two / fix_two) + EPS_ADAM) + WEIGHT_DECAY * weight
    )
    return (weight - LEARN_RATE * update, moment_one, moment_two)


def per_device(
    latents, noise, velocity, labels, time_index, times,
    in_mats, out_mats, embed_mats, class_table, final_ada, head_mat, bias_vec,
    in_mats_first, out_mats_first, embed_first, table_first, final_first, head_first, bias_first,
    in_mats_second, out_mats_second, embed_second, table_second, final_second, head_second, bias_second,
):
    shards = lax.axis_size("shard")
    groups = lax.axis_size("grp")
    me = lax.axis_index("shard")
    mine = lax.axis_index("grp")
    batch = latents.shape[0]
    width = embed_mats.shape[1]
    team = shards * batch
    tuned = groups == 4 and shards == 8

    embed_low = lower(embed_mats)
    marks = jnp.stack([time_index // 32, time_index % 32, labels // 32, labels % 32], 1).astype(BF)
    marks = jnp.pad(marks, ((0, TFREQ - batch), (0, 128 - width - MARKS)))
    message = jnp.concatenate(
        [embed_low[PATCH : PATCH + TFREQ], embed_low[:PATCH], lower(bias_vec).reshape(BIASES, width)]
    )
    message = jnp.pad(message, ((0, MESSAGE - message.shape[0]), (0, 128 - width)))
    message = message + jnp.pad(marks, ((0, MESSAGE - TFREQ), (width, 0)))
    arrived = [swap(message, "shard", hop) for hop in range(2, shards, 2)]
    near_message = jnp.stack([message] + arrived)
    other_message = swap(near_message, "shard", 1)
    in_mats_early, out_mats_early = tie((in_mats, out_mats), message)

    def rows_of(first, count):
        return [lower(in_mats_early[0, :, first + part * D : first + (part + 1) * D]) for part in range(count)]

    own_qkv = jnp.concatenate(rows_of(6 * D, 3))
    own_feed = jnp.concatenate(rows_of(9 * D, FF // D) + [lower(out_mats_early[0])])
    spot = jnp.stack([me, mine]).astype(jnp.int32)
    if tuned:
        near_qkv = rows_near(own_qkv)
        traded = own_feed.shape[0] - DIRECT
        near_feed = rows_near(own_feed[:traded])
    else:
        qkv_pieces, feed_pieces = [[lax.all_gather(own, "shard")] for own in (own_qkv, own_feed)]
    times_row = jnp.pad(times, (0, -times.shape[0] % 128))[None]
    time_pre, condition, marks_team, wpatch, biases, near_mod, far_mod = condition_of_team(
        spot, near_message, other_message, times_row, embed_low, class_table.T, in_mats, final_ada, batch
    )
    if tuned:
        far_qkv = rows_far(tie(near_qkv, time_pre))
    near_mod = near_mod + swap(far_mod, "shard", 1)
    mods = lower(near_mod)
    mods = [near_mod[0]] + [swap(mods[hop], "shard", 2 * hop) for hop in range(1, shards // 2)]
    mod = total_of([part.astype(F32) for part in mods])[:, None, :]
    if tuned:
        far_feed = rows_far(tie(near_feed, (far_qkv, mod)))
    if tuned:
        direct = [swap(tie(own_feed[traded:], mod), "shard", hop) for hop in (2, 4, 6)]
    latents, noise, velocity, head_mat_late, marks_team = tie(
        (latents, noise, velocity, head_mat, marks_team), near_mod
    )
    if tuned:
        far_qkv = tie(far_qkv, near_mod)
        qkv_pieces = rows_all(own_qkv, far_qkv)
    moment = pick_times(time_index, times)
    noisy = lower((1.0 - moment)[:, None, None] * latents + moment[:, None, None] * noise)
    pos = position_table()
    a, qkv, o, wqkv = attend(spot, noisy, pos, wpatch, mod, biases, qkv_pieces, shards)
    if tuned:
        o, direct = lax.optimization_barrier((o, direct))
        direct = jnp.stack(direct)
        feed_pieces = rows_all(tie(own_feed, o), tie(far_feed, o)) + [direct, swap(direct, "shard", 1)]
    count_all = float(groups * shards * batch * SEQ * OUT)
    head_low = lower(head_mat_late)
    mid, y, m, g, slope, df, ds, dmod_feed, near_tail, far_tail, bdown, wup, wout = feed(
        spot, moment, noisy, pos, wpatch, o, mod, biases, head_low[:D],
        head_low[D:].astype(F32), velocity, feed_pieces, shards, count_all,
    )
    wout = wout.reshape(D + FF, D)
    tokens = batch * SEQ
    if tuned:
        marks_all = [marks_team] + [swap(marks_team, "grp", hop) for hop in (1, 2, 3)]
        mid, df, dmod_feed, marks_all = lax.optimization_barrier((mid, df, dmod_feed, marks_all))
    else:
        marks_all = from_groups(marks_team, tuned)
    early = lower(dmod_feed[:, 0])
    early = [early] + [swap(early, "grp", hop) for hop in range(1, groups)] if tuned else from_groups(early, tuned)
    gup, gout, bup, dm = feed_back(
        m.reshape(tokens, D), df.reshape(tokens, D), g, slope, wup, wout, 0, FF
    )
    gup, gout, bup, dm, early = lax.optimization_barrier((gup, gout, bup, dm, early))
    gup = lax.psum_scatter(gup, "shard", scatter_dimension=0)
    early = jnp.stack(early)
    early_far = [swap(early, "shard", hop) for hop in range(2, shards, 2)]
    dmid, do, dmod_mid, gout, bproj = middle_back(
        mid, dm.reshape(batch, SEQ, D), tie(ds, early), y, o, mod, biases, wout, gout
    )

    dmid, do, dmod_mid, gout, bproj, early, early_far = lax.optimization_barrier(
        (dmid, do, dmod_mid, gout, bproj, early, early_far)
    )

    marks_all, features, time_act, cond_act_all = condition_of_all(
        spot, near_message, other_message, times_row, embed_low, class_table.T, tie(marks_all, dmid)
    )
    gout = gout.reshape(shards, (D + FF) // shards, D)
    if tuned:
        gout = cores_summed(gout)
        early_near = jnp.stack([early] + early_far)
        near_tail, far_tail = [part.reshape(shards // 2, -1, width) for part in tie((near_tail, far_tail), dmid)]
        do = tie(do, (gout, early_near, near_tail, far_tail, features))
        gout_parts = groups_traded(gout)
    else:
        near_tail, far_tail = [part.reshape(shards // 2, -1, width) for part in (near_tail, far_tail)]
        early_near = jnp.stack([early] + early_far)
        gout = lax.psum_scatter(gout, "shard", scatter_dimension=0)
    early_other = swap(early_near, "shard", 1)
    dqkv, gqkv, gqkv_far, bqkv = attend_back(spot, qkv, do, a, shards)
    if tuned:
        dqkv, gqkv, gqkv_far, bqkv, gout_parts, early_other = lax.optimization_barrier(
            (dqkv, gqkv, gqkv_far, bqkv, gout_parts, early_other)
        )
    if tuned:
        gqkv = halves_added(lower(gqkv.astype(F32) + swap(gqkv_far, "shard", 1).astype(F32)), 2)
        gout_parts = shards_traded(gout_parts)
        dmid, dmod_mid, gup, bqkv, bproj, bup, bdown = tie(
            (dmid, dmod_mid, gup, bqkv, bproj, bup, bdown), gout_parts[0]
        )
        gup = halves_added(gup, 2)
    else:
        gqkv = jnp.stack([gqkv, gqkv_far], 1)
        gqkv = jnp.where(me % 2 == 0, gqkv, gqkv[:, ::-1]).reshape((shards,) + gqkv.shape[2:])
        gqkv = lax.psum_scatter(gqkv, "shard", scatter_dimension=0)
    dmod_attn, near_patch, far_patch, bpatch = stream_back(
        spot, dqkv, dmid, noisy, pos, wpatch, mod, biases, wqkv
    )
    if tuned:
        dmod_attn, near_patch, far_patch, bpatch, gup, gout_parts, gqkv = lax.optimization_barrier(
            (dmod_attn, near_patch, far_patch, bpatch, gup, gout_parts, gqkv)
        )
        gup, gout = shards_summed(gup), shards_summed(gout_parts)
        gqkv, gup = halves_added(shards_summed(gqkv), 1), halves_added(gup, 1)
    late = lower(jnp.concatenate([dmod_attn[:, 0], dmod_mid[:, 0]], 1))

    near_late = jnp.stack([late] + [swap(late, "shard", hop) for hop in range(2, shards, 2)])
    other_late = swap(near_late, "shard", 1)
    if tuned:
        gup, other_late, gqkv = tie((gup, other_late, gqkv), gout)
    late, grad_condition, near_act, far_act = condition_back(
        spot, near_late, other_late, early_near, early_other, condition, in_mats, final_ada, embed_low
    )
    bias_part = jnp.concatenate([bpatch, bqkv[:, :D], bqkv[:, 2 * D :], bproj, bup, bdown], 1)
    bias_part = jnp.broadcast_to(bias_part.reshape(1, -1, width), (shards // 2, len(BIAS_PARTS) * shards, width))

    far_act = jnp.concatenate([far_act, far_patch, bias_part, far_tail], 1)
    near_act = jnp.concatenate([near_act, near_patch, bias_part, near_tail], 1)
    near_act = near_act + swap(far_act, "shard", 1)
    acts = [near_act[0]] + [swap(near_act[hop], "shard", 2 * hop) for hop in range(1, near_act.shape[0])]

    def last_of(acts):
        act_part = total_of(acts)
        unused, time_pull = jax.vjp(jax.nn.silu, time_pre)
        grad_time = lower(time_pull(act_part[:team].reshape(time_pre.shape))[0]).reshape(team, width)
        return jnp.concatenate([grad_time.astype(F32), grad_condition.astype(F32), act_part[team:]])

    if tuned:
        late_x, late_y = swap(late, "grp", 1), swap(late, "grp", 2)
        acts, late_x, late_y, gqkv = lax.optimization_barrier((acts, late_x, late_y, gqkv))
        last = last_of(acts)
        gqkv = shards_traded(gqkv)
        gup = shards_summed(gup)
        both = jnp.concatenate([gup, gout])
        last_x, late_xy, both_x = swap(last, "grp", 1), swap(late_x, "grp", 2), swap(both, "grp", 1)
        last_x, late_xy, both_x, gqkv = lax.optimization_barrier((last_x, late_xy, both_x, gqkv))
        gqkv = shards_summed(gqkv)
        pair = jnp.stack([last, last_x])
        both = jnp.stack([both, both_x])
        last_far, both_far, gqkv_x = swap(pair, "grp", 2), swap(both, "grp", 2), swap(gqkv, "grp", 1)
        last_far, gqkv_x = lax.optimization_barrier((last_far, gqkv_x))
        grads_last = [last, last_x, last_far[0], last_far[1]]
        grads_late = [late, late_x, late_y, late_xy]
        gqkv = jnp.stack([gqkv, gqkv_x])
        gqkv_far = swap(gqkv, "grp", 2)
        both = ordered(jnp.concatenate([both, both_far]), "grp")
        gqkv = ordered(jnp.concatenate([gqkv, gqkv_far]), "grp")
        gup, gout = quarters_joined(both, (gup.shape[0], FF), (gout.shape[0], D + FF))
        gqkv = quarters_joined(gqkv, (gqkv.shape[1], 3 * D))[0]
        gfeed = [gup, gout]
    else:
        grads_last = from_groups(last_of(acts), tuned)
        grads_late = from_groups(late, tuned)
        gup, gout, gqkv = [
            total_of([part.astype(F32) for part in from_groups(grads, tuned)]) for grads in (gup, gout, gqkv)
        ]
        gfeed = [gup, gout]
    grads_of = condition_grads if tuned else condition_grads_plain
    gada, gembed, gtable, bias_grad, message, squares = grads_of(
        spot, marks_all, features, time_act, cond_act_all, early_near, early_other, grads_late, grads_last
    )
    gup, gout = gfeed
    share = bias_vec.shape[0]
    bias_grad = lax.dynamic_slice_in_dim(bias_grad.reshape(-1), me * share, share, 0)
    squares = squares + sum(jnp.sum(part * part) for part in (gup, gqkv, gout, bias_grad))
    message = jnp.concatenate([message, jnp.broadcast_to(squares, (6, width))])
    final = spread(message, "shard")
    grad_norm = jnp.sqrt(total_of([final[i, -1] for i in range(shards)]))
    factor = (CLIP_NORM / jnp.maximum(grad_norm, CLIP_NORM))[0]
    grad_norm = grad_norm[0]
    final = ordered(final, "shard")
    btime = jnp.concatenate([final[:, 0].reshape(-1), final[:, 1].reshape(-1)])
    tail = final[:, 2:-6].reshape(-1, D)
    head_grad = jnp.concatenate([tail[:OUT].T, tail[OUT : OUT + 1, :OUT]])
    loss_sum = tail[OUT + 1, 0]
    btime = jnp.concatenate([jnp.zeros((D,), F32), btime, jnp.zeros((12 * D + FF,), F32)])
    bias_grad = bias_grad + lax.dynamic_slice_in_dim(btime, me * share, share, 0)
    in_grad = jnp.concatenate(
        [gada[:, : 6 * D]]
        + [gqkv[part * width : (part + 1) * width] for part in range(3)]
        + [gup[part * width : (part + 1) * width] for part in range(FF // D)],
        1,
    )
    weights = (in_mats, out_mats, embed_mats, class_table, final_ada, head_mat, bias_vec)
    firsts = (in_mats_first, out_mats_first, embed_first, table_first, final_first, head_first, bias_first)
    seconds = (
        in_mats_second, out_mats_second, embed_second, table_second, final_second, head_second, bias_second
    )
    grads = (in_grad[None], gout[None], gembed.T, gtable.T, gada[:, 6 * D :], head_grad, bias_grad)
    stepped = [
        adamw(weight, moment_one, moment_two, gradient, factor)
        for weight, moment_one, moment_two, gradient in zip(weights, firsts, seconds, grads)
    ]
    return tuple(part[0] for part in stepped) + tuple(part[1] for part in stepped) + tuple(
        part[2] for part in stepped
    ) + (loss_sum, grad_norm)


def solution(mesh):
    images = P(("grp", "shard"))
    placed = (
        P(None, "shard", None),
        P(None, "shard", None),
        P(None, "shard"),
        P(None, "shard"),
        P("shard", None),
        P(),
        P("shard"),
    )
    return jax.shard_map(
        per_device,
        mesh=mesh,
        in_specs=(images,) * 5 + (P(),) + placed * 3,
        out_specs=placed * 3 + (P(), P()),
        check_vma=False,
    )
```

```python
import math
from functools import partial
import numpy as np
import jax
import jax.numpy as jnp
from jax import lax
from jax.sharding import PartitionSpec as P
from jax.experimental import pallas as pl
from jax.experimental.pallas import tpu as pltpu

D = 768
HEADS = 12
HDIM = 64
FF = 3072
PATCH = 16
SEQ = 256
OUT = 32
GRID = 16
STEP = 10
BETA_ONE = 0.9
BETA_TWO = 0.999
LEARN_RATE = 0.05
WEIGHT_DECAY = 0.05
EPS_ADAM = 1e-08
CLIP_NORM = 0.01
TFREQ = 256
NCLASS = 1001
EPS_NORM = 1e-06
BF = jnp.bfloat16
F32 = jnp.float32
VMEM_LIMIT = 60 * 1024 * 1024
COST = 3 * 10**8
PAIR = 2 * HDIM
PAIRS = HEADS // 2
BIASES = 19
B_PATCH, B_TIME, B_CLASS, B_ADA, B_QUERY, B_VALUE, B_PROJ, B_UP, B_DOWN, B_FINAL = 0, 1, 2, 3, 9, 10, 11, 12, 16, 17


def dot(left, right):
    return jnp.dot(left, right, preferred_element_type=F32)


def dot_nt(left, right):
    return lax.dot_general(left, right, (((1,), (1,)), ((), ())), preferred_element_type=F32)


def dot_tn(left, right):
    return lax.dot_general(left, right, (((0,), (0,)), ((), ())), preferred_element_type=F32)


def whole(shape):
    zeros = (0,) * len(shape)
    return pl.BlockSpec(shape, lambda step: zeros, pipeline_mode=pl.Buffered(1))


def fixed(shape):
    zeros = (0,) * len(shape)
    return pl.BlockSpec(shape, lambda step: zeros)


def rows(count, *rest):
    zeros = (0,) * len(rest)
    return pl.BlockSpec((count,) + rest, lambda step: (step,) + zeros)


def shape_of(shape, dtype):
    return jax.ShapeDtypeStruct(shape, dtype)


def norm_parts(array_in):
    centre = array_in - jnp.mean(array_in, -1, keepdims=True)
    inverse = lax.rsqrt(jnp.mean(centre * centre, -1, keepdims=True) + EPS_NORM)
    return centre * inverse, inverse


def norm_back(grad_normed, normed, inverse):
    first = jnp.mean(grad_normed, -1, keepdims=True)
    second = jnp.mean(grad_normed * normed, -1, keepdims=True)
    return inverse * (grad_normed - first - normed * second)


def cost(microseconds):
    return pl.CostEstimate(flops=microseconds * COST, bytes_accessed=0, transcendentals=0)


def head_masks():
    lane = lax.broadcasted_iota(jnp.int32, (1, PAIR), 1)
    return (lane < HDIM, lane >= HDIM)


def both_heads(part, masks):
    return jnp.concatenate([jnp.where(mask, part, jnp.zeros_like(part)) for mask in masks], 0)


def weight_copies(spot_ref, pieces, target, sem):
    if len(pieces) == 1:
        return [pltpu.make_async_copy(pieces[0], target, sem)]
    own, near, pair, other, *direct = pieces
    shard = spot_ref[0]
    quarter = near.shape[2]
    traded = target.shape[1] - (direct[0].shape[1] if direct else 0)
    rest = traded - 3 * quarter
    made = [
        pltpu.make_async_copy(own, target.at[shard], sem),
        pltpu.make_async_copy(pair, target.at[shard ^ 1], sem),
    ]
    for block in range(4):
        count = rest if block == 3 else quarter
        rows_here = slice(block * quarter, block * quarter + count)
        for core, part in enumerate((near, other)):
            for hop in range(3):
                source = part.at[block, hop, quarter - count :] if count < quarter else part.at[block, hop]
                slot = shard ^ (2 * hop + 2 + core)
                made.append(pltpu.make_async_copy(source, target.at[slot, rows_here], sem))
    for core, part in enumerate(direct):
        for hop in range(3):
            slot = shard ^ (2 * hop + 2 + core)
            made.append(pltpu.make_async_copy(part.at[hop], target.at[slot, traded:], sem))
    return made


def run_copies(made, start):
    for copy in made:
        copy.start() if start else copy.wait()


def part_of(weights, part, count):
    width = weights.shape[1] // count
    return weights[:, part * width : (part + 1) * width, :].reshape(D, D)


def attend_kernel(
    spot_ref, noisy_ref, pos_ref, wpatch_ref, mod_ref, bias_ref, *refs, images
):
    pieces, (a_ref, qkv_ref, o_ref, kept_ref, wqkv_ref, sem, out_sem) = refs[:-7], refs[-7:]
    step = pl.program_id(0)
    made = weight_copies(spot_ref, pieces, wqkv_ref, sem)
    keep = pltpu.make_async_copy(wqkv_ref, kept_ref, out_sem)

    @pl.when(step == 0)
    def _():
        run_copies(made, True)
        run_copies(made, False)
        keep.start()

    @pl.when(step == pl.num_programs(0) - 1)
    def _():
        keep.wait()

    masks = head_masks()

    def bias(row):
        return bias_ref[row : row + 1, :]

    def image(index, carry):
        stream = dot(noisy_ref[index], wpatch_ref[...]) + (pos_ref[...] + bias(B_PATCH))
        normed, unused = norm_parts(stream)
        scale = 1.0 + (mod_ref[index, :, D : 2 * D] + bias(B_ADA + 1))
        a = (normed * scale + (mod_ref[index, :, :D] + bias(B_ADA))).astype(BF)
        a_ref[index] = a
        for part in range(3):
            cut = slice(part * D, (part + 1) * D)
            product = dot(a, part_of(wqkv_ref, part, 3))
            if part != 1:
                product = product + bias(B_QUERY if part == 0 else B_VALUE)
            qkv_ref[index, :, cut] = product.astype(BF)
        for pair in range(PAIRS):
            base = pair * PAIR
            queries = qkv_ref[index, :, base : base + PAIR]
            keys = qkv_ref[index, :, D + base : D + base + PAIR]
            values = qkv_ref[index, :, 2 * D + base : 2 * D + base + PAIR]
            scores = dot_nt(both_heads(queries * jnp.asarray(HDIM**-0.5, BF), masks), keys)
            power = jnp.exp(scores - jnp.max(scores, -1, keepdims=True))
            total = jnp.sum(power, -1, keepdims=True)
            mixed = dot((power * (1.0 / total)).astype(BF), values)
            o_ref[index, :, base : base + PAIR] = jnp.where(masks[0], mixed[:SEQ], mixed[SEQ:]).astype(BF)
        return carry

    lax.fori_loop(0, images, image, 0)


ANYWHERE = pl.BlockSpec(memory_space=pl.ANY)


def attend(spot, noisy, pos, wpatch, mod, bias, pieces, shards, images=1):
    batch = noisy.shape[0]
    kept = (shards, 3 * D // shards, D)
    return pl.pallas_call(
        partial(attend_kernel, images=images),
        grid=(batch // images,),
        in_specs=[
            pl.BlockSpec(memory_space=pltpu.SMEM),
            rows(images, SEQ, PATCH),
            whole((SEQ, D)),
            whole((PATCH, D)),
            rows(images, 1, 8 * D),
            whole((BIASES, D)),
        ]
        + [ANYWHERE] * len(pieces),
        out_specs=[rows(images, SEQ, D), rows(images, SEQ, 3 * D), rows(images, SEQ, D), ANYWHERE],
        out_shape=[
            shape_of((batch, SEQ, D), BF),
            shape_of((batch, SEQ, 3 * D), BF),
            shape_of((batch, SEQ, D), BF),
            shape_of(kept, BF),
        ],
        scratch_shapes=[pltpu.VMEM(kept, BF), pltpu.SemaphoreType.DMA, pltpu.SemaphoreType.DMA],
        compiler_params=pltpu.CompilerParams(vmem_limit_bytes=VMEM_LIMIT),
        name="attend",
        cost_estimate=cost(32),
    )(spot, noisy, pos, wpatch, mod, bias, *pieces)


GELU_A = math.sqrt(2.0 / math.pi)
GELU_B = 0.044715


def gelu_both(u):
    square = u * u
    turn = jnp.tanh(u * (GELU_A + (GELU_A * GELU_B) * square))
    half = 0.5 + 0.5 * turn
    value = u * half
    slope = half + (value * (1.0 - half)) * (2.0 * GELU_A + (6.0 * GELU_A * GELU_B) * square)
    return value, slope


def feed_kernel(
    spot_ref, t_ref, noisy_ref, pos_ref, wpatch_ref, o_ref, mod_ref, bias_ref,
    head_ref, hbias_ref, vel_ref, *refs, images, count_all
):
    pieces, refs = refs[:-18], refs[-18:]
    mid_ref, y_ref, m_ref, g_ref, slope_ref, df_ref, ds_ref, dmod_ref, near_ref, far_ref, bdown_ref = refs[:11]
    kept1_ref, kept2_ref, weights_ref, tail_ref, order, sem, out_sem = refs[11:]
    step = pl.program_id(0)
    made = weight_copies(spot_ref, pieces, weights_ref, sem)
    up_width, out_width = kept1_ref.shape[1], kept2_ref.shape[1]
    keeps = [
        pltpu.make_async_copy(weights_ref.at[:, :up_width], kept1_ref, out_sem.at[0]),
        pltpu.make_async_copy(weights_ref.at[:, up_width:], kept2_ref, out_sem.at[1]),
    ]

    @pl.when(step == 0)
    def _():
        run_copies(made, True)
        run_copies(made, False)
        for keep in keeps:
            keep.start()

    @pl.when(step == pl.num_programs(0) - 1)
    def _():
        for keep in keeps:
            keep.wait()

    @pl.when(step == 0)
    def _():
        tail_ref[...] = jnp.zeros_like(tail_ref)
        bdown_ref[...] = jnp.zeros_like(bdown_ref)

    tokens = images * SEQ

    def bias(row):
        return bias_ref[row : row + 1, :]

    def spread(part):
        parts = []
        for index in range(images):
            row = mod_ref[index, :, (part + 2) * D : (part + 3) * D]
            row = row + bias(B_ADA + 2 + part if part < 4 else B_FINAL + part - 4)
            parts.append(jnp.broadcast_to(row, (SEQ, D)))
        return jnp.concatenate(parts, 0)

    def up_part(part):
        rows_of = up_width * D // FF
        return weights_ref[:, part * rows_of : (part + 1) * rows_of, :].reshape(D, D)

    def out_rows(part):
        first, taken = part * D, []
        while first < (part + 1) * D:
            place_of, row = first // out_width, first % out_width
            count = min(out_width - row, (part + 1) * D - first)
            taken.append(weights_ref[place_of, up_width + row : up_width + row + count, :])
            first += count
        return jnp.concatenate(taken, 0)

    position = jnp.concatenate([pos_ref[...] + bias(B_PATCH)] * images, 0)
    stream = dot(noisy_ref[...].reshape(tokens, PATCH), wpatch_ref[...]) + position
    y = dot(o_ref[...].reshape(tokens, D), out_rows(0)) + bias(B_PROJ)
    y_ref[...] = y.astype(BF).reshape(images, SEQ, D)
    mid = stream + spread(0) * y
    mid_ref[...] = mid.reshape(images, SEQ, D)
    normed, unused = norm_parts(mid)
    m = (normed * (1.0 + spread(2)) + spread(1)).astype(BF)
    m_ref[...] = m.reshape(images, SEQ, D)
    feed = jnp.broadcast_to(bias(B_DOWN), (tokens, D))
    for j in range(FF // D):
        cut = slice(j * D, (j + 1) * D)
        g, slope = gelu_both(dot(m, up_part(j)) + bias(B_UP + j))
        g = g.astype(BF)
        g_ref[:, cut] = g
        slope_ref[:, cut] = slope.astype(BF)
        feed = feed + dot(g, out_rows(j + 1))
    gate = spread(3)
    stream = mid + gate * feed
    normed, inverse = norm_parts(stream)
    scale = 1.0 + spread(5)
    z = (normed * scale + spread(4)).astype(BF)
    predicted = dot(z, head_ref[...]) + hbias_ref[...]
    t = jnp.concatenate(
        [jnp.full((SEQ, 1), t_ref[step * images + index], F32) for index in range(images)], 0
    )
    residual = predicted - vel_ref[...].reshape(tokens, OUT)
    weighted = t * residual
    loss = jnp.sum(jnp.sum(weighted * residual, 0, keepdims=True), 1, keepdims=True)
    tail_ref[OUT + 1 : OUT + 2, :] += jnp.broadcast_to(loss, (1, D))
    grad_pred = (2.0 * weighted / count_all).astype(BF)
    tail_ref[OUT : OUT + 1, :OUT] += jnp.sum(grad_pred.astype(F32), 0, keepdims=True)
    tail_ref[:OUT, :] += dot_tn(grad_pred, z)
    dz = dot_nt(grad_pred, head_ref[...])
    ds = norm_back(dz * scale, normed, inverse)
    ds_ref[...] = ds.reshape(images, SEQ, D)
    df = (ds * gate).astype(BF)
    df_ref[...] = df.reshape(images, SEQ, D)
    bdown_ref[...] += jnp.sum(df.astype(F32), 0, keepdims=True)
    for index in range(images):
        cut = slice(index * SEQ, (index + 1) * SEQ)
        dmod_ref[index, :, :D] = jnp.sum(ds[cut] * feed[cut], 0, keepdims=True)
        dmod_ref[index, :, D : 2 * D] = jnp.sum(dz[cut], 0, keepdims=True)
        dmod_ref[index, :, 2 * D :] = jnp.sum(dz[cut] * normed[cut], 0, keepdims=True)

    shards, taken = 2 * near_ref.shape[0], near_ref.shape[1]

    @pl.when(step == pl.num_programs(0) - 1)
    def _():
        for place_of in range(shards):
            order[place_of] = tail_ref[place_of * taken : (place_of + 1) * taken, :]
        for entry in range(shards):
            (far_ref if entry % 2 else near_ref)[entry // 2] = order[spot_ref[0] ^ entry]


def tail_rows(shards):
    return -(-(OUT + 2) // shards)


def feed(spot, t, noisy, pos, wpatch, o, mod, bias, head, hbias, velocity, pieces, shards, count_all, images=2):
    batch = o.shape[0]
    kept1 = (shards, FF // shards, D)
    kept2 = (shards, (D + FF) // shards, D)
    half = (shards // 2, tail_rows(shards), D)
    tokens = batch * SEQ
    return pl.pallas_call(
        partial(feed_kernel, images=images, count_all=count_all),
        grid=(batch // images,),
        in_specs=[
            pl.BlockSpec(memory_space=pltpu.SMEM),
            pl.BlockSpec(memory_space=pltpu.SMEM),
            rows(images, SEQ, PATCH),
            whole((SEQ, D)),
            whole((PATCH, D)),
            rows(images, SEQ, D),
            rows(images, 1, 8 * D),
            whole((BIASES, D)),
            whole((D, OUT)),
            whole((1, OUT)),
            rows(images, SEQ, OUT),
        ]
        + [ANYWHERE] * len(pieces),
        out_specs=[
            rows(images, SEQ, D),
            rows(images, SEQ, D),
            rows(images, SEQ, D),
            rows(images * SEQ, FF),
            rows(images * SEQ, FF),
            rows(images, SEQ, D),
            rows(images, SEQ, D),
            rows(images, 1, 3 * D),
            fixed(half),
            fixed(half),
            fixed((1, D)),
            ANYWHERE,
            ANYWHERE,
        ],
        out_shape=[
            shape_of((batch, SEQ, D), F32),
            shape_of((batch, SEQ, D), BF),
            shape_of((batch, SEQ, D), BF),
            shape_of((tokens, FF), BF),
            shape_of((tokens, FF), BF),
            shape_of((batch, SEQ, D), BF),
            shape_of((batch, SEQ, D), F32),
            shape_of((batch, 1, 3 * D), F32),
            shape_of(half, F32),
            shape_of(half, F32),
            shape_of((1, D), F32),
            shape_of(kept1, BF),
            shape_of(kept2, BF),
        ],
        scratch_shapes=[
            pltpu.VMEM((shards, kept1[1] + kept2[1], D), BF),
            pltpu.VMEM((shards * half[1], D), F32),
            pltpu.VMEM((shards,) + half[1:], F32),
            pltpu.SemaphoreType.DMA,
            pltpu.SemaphoreType.DMA((2,)),
        ],
        compiler_params=pltpu.CompilerParams(vmem_limit_bytes=VMEM_LIMIT),
        name="feed",
        cost_estimate=cost(52),
    )(spot, t, noisy, pos, wpatch, o, mod, bias, head, hbias, velocity, *pieces)


def feed_back_kernel(
    m_ref, df_ref, g_ref, slope_ref, w1_ref, w2_ref, wup_ref, wdown_ref, bup_ref, dm_ref, mt, dft, *, tile
):
    step = pl.program_id(0)

    @pl.when(step == 0)
    def _():
        mt[...] = m_ref[...].T
        dft[...] = df_ref[...].T
        dm_ref[...] = jnp.zeros_like(dm_ref)

    tokens = m_ref.shape[0]
    w1 = w1_ref[...].reshape(D, D)
    w2 = w2_ref[...]
    du_parts = []
    for i in range(tokens // tile):
        cut = slice(i * tile, (i + 1) * tile)
        du = (dot_nt(df_ref[cut, :], w2) * slope_ref[cut, :].astype(F32)).astype(BF)
        du_parts.append(du)
        dm_ref[cut, :] += dot_nt(du, w1)
    du = jnp.concatenate(du_parts, 0)
    bup_ref[...] = jnp.sum(du.astype(F32), 0, keepdims=True)
    wup_ref[...] = dot(mt[...], du).astype(BF).reshape(wup_ref.shape)
    wdown_ref[...] = dot(dft[...], g_ref[...]).T.astype(BF)


def feed_back(m, df, g, slope, w1, wout, first, last, tile=512):
    chunk = D
    shards = w1.shape[0]
    rows_of = D // shards
    tokens = m.shape[0]
    steps = (last - first) // chunk
    base = first // chunk
    return pl.pallas_call(
        partial(feed_back_kernel, tile=tile),
        grid=(steps,),
        in_specs=[
            whole((tokens, D)),
            whole((tokens, D)),
            pl.BlockSpec((tokens, chunk), lambda step: (0, step + base)),
            pl.BlockSpec((tokens, chunk), lambda step: (0, step + base)),
            pl.BlockSpec((shards, rows_of, D), lambda step: (0, step + base, 0)),
            pl.BlockSpec((chunk, D), lambda step: (step + base + D // chunk, 0)),
        ],
        out_specs=[
            pl.BlockSpec((shards, rows_of, D), lambda step: (0, step, 0)),
            pl.BlockSpec((chunk, D), lambda step: (step + base + D // chunk, 0)),
            pl.BlockSpec((1, chunk), lambda step: (0, step)),
            pl.BlockSpec((tokens, D), lambda step: (0, 0), pipeline_mode=pl.Buffered(1)),
        ],
        out_shape=[
            shape_of((shards, steps * rows_of, D), BF),
            shape_of((D + FF, D), BF),
            shape_of((1, last - first), F32),
            shape_of((tokens, D), F32),
        ],
        scratch_shapes=[pltpu.VMEM((D, tokens), BF), pltpu.VMEM((D, tokens), BF)],
        compiler_params=pltpu.CompilerParams(vmem_limit_bytes=VMEM_LIMIT),
        name="feed_back",
        cost_estimate=cost(51),
    )(m, df, g, slope, w1, wout)


def middle_back_kernel(
    mid_ref, dm_ref, ds_ref, y_ref, o_ref, mod_ref, bias_ref, wproj_ref, gout_ref,
    dmid_ref, do_ref, dmod_ref, wproj_out_ref, bproj_ref, total, *, images
):
    step = pl.program_id(0)

    @pl.when(step == 0)
    def _():
        total[...] = jnp.zeros_like(total)
        bproj_ref[...] = jnp.zeros_like(bproj_ref)

    tokens = images * SEQ
    dy_parts = []
    for index in range(images):
        normed, inverse = norm_parts(mid_ref[index])
        dm = dm_ref[index]
        dmid = ds_ref[index] + norm_back(
            dm * (1.0 + (mod_ref[index, :, 4 * D : 5 * D] + bias_ref[B_ADA + 4 : B_ADA + 5, :])), normed, inverse
        )
        dmid_ref[index] = dmid
        dmod_ref[index, :, :D] = jnp.sum(dmid * y_ref[index].astype(F32), 0, keepdims=True)
        dmod_ref[index, :, D : 2 * D] = jnp.sum(dm, 0, keepdims=True)
        dmod_ref[index, :, 2 * D :] = jnp.sum(dm * normed, 0, keepdims=True)
        gate = mod_ref[index, :, 2 * D : 3 * D] + bias_ref[B_ADA + 2 : B_ADA + 3, :]
        dy_parts.append((dmid * gate).astype(BF))
    dy = jnp.concatenate(dy_parts, 0)
    bproj_ref[...] += jnp.sum(dy.astype(F32), 0, keepdims=True)
    do_ref[...] = dot_nt(dy, wproj_ref[...]).astype(BF).reshape(images, SEQ, D)
    total[...] += dot_tn(o_ref[...].reshape(tokens, D), dy)

    @pl.when(step == pl.num_programs(0) - 1)
    def _():
        wproj_out_ref[...] = total[...].astype(BF)


def middle_back(mid, dm, ds, y, o, mod, bias, wout, gout, images=2):
    batch = mid.shape[0]
    return pl.pallas_call(
        partial(middle_back_kernel, images=images),
        grid=(batch // images,),
        in_specs=[
            rows(images, SEQ, D),
            rows(images, SEQ, D),
            rows(images, SEQ, D),
            rows(images, SEQ, D),
            rows(images, SEQ, D),
            rows(images, 1, 8 * D),
            whole((BIASES, D)),
            whole((D, D)),
            pl.BlockSpec(memory_space=pl.ANY),
        ],
        out_specs=[
            rows(images, SEQ, D),
            rows(images, SEQ, D),
            rows(images, 1, 3 * D),
            fixed((D, D)),
            fixed((1, D)),
        ],
        out_shape=[
            shape_of((batch, SEQ, D), F32),
            shape_of((batch, SEQ, D), BF),
            shape_of((batch, 1, 3 * D), F32),
            shape_of((D + FF, D), BF),
            shape_of((1, D), F32),
        ],
        input_output_aliases={8: 3},
        scratch_shapes=[pltpu.VMEM((D, D), F32)],
        compiler_params=pltpu.CompilerParams(vmem_limit_bytes=VMEM_LIMIT),
        name="middle_back",
        cost_estimate=cost(18),
    )(mid, dm, ds, y, o, mod, bias, wout, gout)


def attend_back_kernel(spot_ref, qkv_ref, do_ref, a_ref, dqkv_ref, mine_ref, theirs_ref, bqkv_ref, total, *, images):
    step = pl.program_id(0)

    @pl.when(step == 0)
    def _():
        total[...] = jnp.zeros_like(total)
        bqkv_ref[...] = jnp.zeros_like(bqkv_ref)

    masks = head_masks()
    tokens = images * SEQ

    def image(index, carry):
        for pair in range(PAIRS):
            base = pair * PAIR
            scale = jnp.asarray(HDIM**-0.5, BF)
            queries = both_heads(qkv_ref[index, :, base : base + PAIR] * scale, masks)
            keys = qkv_ref[index, :, D + base : D + base + PAIR]
            values = qkv_ref[index, :, 2 * D + base : 2 * D + base + PAIR]
            grads = both_heads(do_ref[index, :, base : base + PAIR], masks)
            scores = dot_nt(keys, queries)
            power = jnp.exp(scores - jnp.max(scores, 0, keepdims=True))
            prob = power * (1.0 / jnp.sum(power, 0, keepdims=True))
            dprob = dot_nt(values, grads)
            delta = jnp.sum(prob * dprob, 0, keepdims=True)
            dscore = (prob * (dprob - delta)).astype(BF)
            dv = dot(prob.astype(BF), grads)
            dk = dot(dscore, queries)
            dq = dot_tn(dscore, keys * scale)
            dq = jnp.where(masks[0], dq[:SEQ], dq[SEQ:])
            dqkv_ref[index, :, base : base + PAIR] = dq.astype(BF)
            dqkv_ref[index, :, D + base : D + base + PAIR] = dk.astype(BF)
            dqkv_ref[index, :, 2 * D + base : 2 * D + base + PAIR] = dv.astype(BF)
        return carry

    lax.fori_loop(0, images, image, 0)
    dqkv = dqkv_ref[...].reshape(tokens, 3 * D)
    total[...] += dot_tn(a_ref[...].reshape(tokens, D), dqkv)
    bqkv_ref[...] += jnp.sum(dqkv.astype(F32), 0, keepdims=True)

    @pl.when(step == pl.num_programs(0) - 1)
    def _():
        width = mine_ref.shape[1] // 3
        core = lax.rem(spot_ref[0], 2)
        for pair in range(mine_ref.shape[0]):
            for out_ref, side in ((mine_ref, core), (theirs_ref, 1 - core)):
                start = pl.multiple_of((2 * pair + side) * width, 16)
                for part in range(3):
                    block = total[pl.ds(start, width), part * D : (part + 1) * D]
                    out_ref[pair, part * width : (part + 1) * width, :] = block.astype(BF)


def attend_back(spot, qkv, do, a, shards, images=1):
    batch = qkv.shape[0]
    half = (shards // 2, 3 * D // shards, D)
    return pl.pallas_call(
        partial(attend_back_kernel, images=images),
        grid=(batch // images,),
        in_specs=[pl.BlockSpec(memory_space=pltpu.SMEM)]
        + [rows(images, SEQ, 3 * D), rows(images, SEQ, D), rows(images, SEQ, D)],
        out_specs=[rows(images, SEQ, 3 * D), fixed(half), fixed(half), fixed((1, 3 * D))],
        out_shape=[
            shape_of((batch, SEQ, 3 * D), BF),
            shape_of(half, BF),
            shape_of(half, BF),
            shape_of((1, 3 * D), F32),
        ],
        scratch_shapes=[pltpu.VMEM((D, 3 * D), F32)],
        compiler_params=pltpu.CompilerParams(vmem_limit_bytes=VMEM_LIMIT),
        name="attend_back",
        cost_estimate=cost(45),
    )(spot, qkv, do, a)


def stream_back_kernel(
    spot_ref, dqkv_ref, dmid_ref, noisy_ref, pos_ref, wpatch_ref, mod_ref, bias_ref, wqkv_ref,
    dmod_ref, near_ref, far_ref, bpatch_ref, wpatch_out_ref, order, *, images
):
    step = pl.program_id(0)

    @pl.when(step == 0)
    def _():
        wpatch_out_ref[...] = jnp.zeros_like(wpatch_out_ref)
        bpatch_ref[...] = jnp.zeros_like(bpatch_ref)

    tokens = images * SEQ
    dqkv = dqkv_ref[...].reshape(tokens, 3 * D)
    da = sum(dot_nt(dqkv[:, part * D : (part + 1) * D], part_of(wqkv_ref, part, 3)) for part in range(3))
    for index in range(images):
        noisy = noisy_ref[index]
        stream = dot(noisy, wpatch_ref[...]) + (pos_ref[...] + bias_ref[B_PATCH : B_PATCH + 1, :])
        scale = 1.0 + (mod_ref[index, :, D : 2 * D] + bias_ref[B_ADA + 1 : B_ADA + 2, :])
        normed, inverse = norm_parts(stream)
        part = da[index * SEQ : (index + 1) * SEQ]
        dmod_ref[index, :, :D] = jnp.sum(part, 0, keepdims=True)
        dmod_ref[index, :, D:] = jnp.sum(part * normed, 0, keepdims=True)
        dstream = dmid_ref[index] + norm_back(part * scale, normed, inverse)
        embedded = dstream.astype(BF)
        bpatch_ref[...] += jnp.sum(embedded.astype(F32), 0, keepdims=True)
        wpatch_out_ref[...] += dot_tn(noisy, embedded)

    width = near_ref.shape[2]
    shards = D // width

    @pl.when(step == pl.num_programs(0) - 1)
    def _():
        for place_of in range(shards):
            order[place_of] = wpatch_out_ref[:, place_of * width : (place_of + 1) * width]
        for entry in range(shards):
            (far_ref if entry % 2 else near_ref)[entry // 2] = order[spot_ref[0] ^ entry]


def stream_back(spot, dqkv, dmid, noisy, pos, wpatch, mod, bias, wqkv, images=2):
    batch = dqkv.shape[0]
    half = (wqkv.shape[0] // 2, PATCH, D // wqkv.shape[0])
    return pl.pallas_call(
        partial(stream_back_kernel, images=images),
        grid=(batch // images,),
        in_specs=[
            pl.BlockSpec(memory_space=pltpu.SMEM),
            rows(images, SEQ, 3 * D),
            rows(images, SEQ, D),
            rows(images, SEQ, PATCH),
            whole((SEQ, D)),
            whole((PATCH, D)),
            rows(images, 1, 8 * D),
            whole((BIASES, D)),
            whole(wqkv.shape),
        ],
        out_specs=[rows(images, 1, 2 * D), fixed(half), fixed(half), fixed((1, D))],
        out_shape=[
            shape_of((batch, 1, 2 * D), F32),
            shape_of(half, F32),
            shape_of(half, F32),
            shape_of((1, D), F32),
        ],
        scratch_shapes=[pltpu.VMEM((PATCH, D), F32), pltpu.VMEM((2 * half[0],) + half[1:], F32)],
        compiler_params=pltpu.CompilerParams(vmem_limit_bytes=VMEM_LIMIT),
        name="stream_back",
        cost_estimate=cost(19),
    )(spot, dqkv, dmid, noisy, pos, wpatch, mod, bias, wqkv)


MARKS = 4
PATCH_ROW = TFREQ
BIAS_ROW = TFREQ + PATCH
MESSAGE = 304


def condition_kernel(spot_ref, near_ref, other_ref, times_ref, embed_ref, table_ref, *rest, team):
    me = spot_ref[0]
    width = embed_ref.shape[1]
    shards = D // width
    messages = [(other_ref if entry % 2 else near_ref).at[entry // 2] for entry in range(shards)]
    if team:
        in_ref, final_ref, time_pre_ref, condition_ref, marks_ref, wpatch_ref, bias_ref = rest[:7]
        near_mod_ref, far_mod_ref, table, bias_rows, order = rest[7:]
        batch = near_mod_ref.shape[1]
        marks = jnp.concatenate(
            [message[:batch, width : width + MARKS].astype(F32) for message in messages], 0
        )
        marks_ref[...] = marks
    else:
        groups_marks, (marks_ref, features_ref, time_act_ref, act_ref, table, bias_rows, order) = rest[:-7], rest[-7:]
        team_count = groups_marks[0].shape[0]
        for entry, part in enumerate(groups_marks):
            start = pl.multiple_of((spot_ref[1] ^ entry) * team_count, team_count)
            marks_ref[pl.ds(start, team_count), :] = part[...]
        marks = marks_ref[...]
    count = marks.shape[0]
    marks = marks.astype(jnp.int32)
    index = marks[:, 0:1] * 32 + marks[:, 1:2]
    label = marks[:, 2:3] * 32 + marks[:, 3:4]

    for entry in range(shards):
        bias_rows[me ^ entry] = messages[entry][BIAS_ROW : BIAS_ROW + BIASES, :width].astype(F32)
        if team:
            order[me ^ entry] = messages[entry][PATCH_ROW : PATCH_ROW + PATCH, :width]

    def bias_row(row):
        return bias_rows[lax.div(row, BIASES), pl.ds(lax.rem(row, BIASES), 1), :]

    entry = lax.broadcasted_iota(jnp.int32, (count, times_ref.shape[1]), 1)
    moment = jnp.sum(jnp.where(entry == index, times_ref[...], 0.0), 1, keepdims=True)
    half = TFREQ // 2
    frequency = lax.broadcasted_iota(jnp.int32, (1, half), 1).astype(F32)
    angles = moment * jnp.exp(-math.log(10000.0) * frequency / half)
    features = jnp.concatenate([jnp.cos(angles), jnp.sin(angles)], 1).astype(BF)
    table[...] = jnp.zeros_like(table)
    table[:, :NCLASS] = table_ref[...].astype(BF)
    entry = lax.broadcasted_iota(jnp.int32, (count, table.shape[1]), 1)
    onehot = (entry == label).astype(F32).astype(BF)
    condition = dot_nt(onehot, table[...]) + bias_row(B_CLASS * shards + me)
    for entry in range(shards):
        place_of = me ^ entry
        time_pre = dot(features, messages[entry][:TFREQ, :width])
        time_pre = time_pre + bias_row(B_TIME * shards + place_of)
        time_act = (time_pre * (1.0 / (1.0 + jnp.exp(-time_pre)))).astype(BF)
        start = pl.multiple_of(TFREQ + PATCH + place_of * width, 16)
        condition = condition + dot(time_act, embed_ref[pl.ds(start, width), :])
        if team:
            if entry == 0:
                for block in range(shards):
                    time_pre_ref[me ^ block] = time_pre[block * batch : (block + 1) * batch, :]
        else:
            time_act_ref[place_of] = time_act
    act = (condition * (1.0 / (1.0 + jnp.exp(-condition)))).astype(BF)
    if not team:
        features_ref[...] = features
        act_ref[...] = act
        return
    condition_ref[...] = condition
    for place_of in range(shards):
        wpatch_ref[:, place_of * width : (place_of + 1) * width] = order[place_of]
    for row in range(BIASES):
        for column in range(shards):
            holder, inner = divmod(row * shards + column, BIASES)
            bias_ref[row : row + 1, column * width : (column + 1) * width] = bias_rows[
                holder, inner : inner + 1, :
            ]
    part = jnp.concatenate([dot(act, in_ref[0].astype(BF)), dot(act, final_ref[...].astype(BF))], 1)
    for pair in range(shards // 2):
        row = 2 * pair * batch
        near_mod_ref[pair] = part[row : row + batch, :]
        far_mod_ref[pair] = part[row + batch : row + 2 * batch, :]


def condition_call(operands, in_specs, out_shape, width, team):
    shards = D // width
    return pl.pallas_call(
        partial(condition_kernel, team=team),
        grid=(1,),
        in_specs=[pl.BlockSpec(memory_space=pltpu.SMEM)] + in_specs,
        out_specs=[whole(out.shape) for out in out_shape],
        out_shape=out_shape,
        scratch_shapes=[
            pltpu.VMEM((width, 1024), BF),
            pltpu.VMEM((shards, BIASES, width), F32),
            pltpu.VMEM((shards, PATCH, width), BF),
        ],
        compiler_params=pltpu.CompilerParams(vmem_limit_bytes=VMEM_LIMIT),
        name="condition",
        cost_estimate=cost(6),
    )(*operands)


def condition_of_team(spot, near, other, times, embed, table, in_mats, final, batch):
    width = embed.shape[1]
    shards = D // width
    count = shards * batch
    operands = [spot, near, other, times, embed, table, in_mats, final]
    in_specs = [whole(part.shape) for part in operands[1:6]]
    in_specs += [pl.BlockSpec((1, width, 6 * D), lambda step: (0, 0, 0)), whole(final.shape)]
    half = (shards // 2, batch)
    out_shape = [
        shape_of((shards, batch, width), F32),
        shape_of((count, width), F32),
        shape_of((count, MARKS), F32),
        shape_of((PATCH, D), BF),
        shape_of((BIASES, D), F32),
        shape_of(half + (8 * D,), F32),
        shape_of(half + (8 * D,), F32),
    ]
    return condition_call(operands, in_specs, out_shape, width, True)


def condition_of_all(spot, near, other, times, embed, table, marks):
    width = embed.shape[1]
    count = len(marks) * marks[0].shape[0]
    operands = [spot, near, other, times, embed, table] + marks
    out_shape = [
        shape_of((count, MARKS), F32),
        shape_of((count, TFREQ), BF),
        shape_of((D // width, count, width), BF),
        shape_of((count, width), BF),
    ]
    return condition_call(operands, [whole(part.shape) for part in operands[1:]], out_shape, width, False)


def condition_back_kernel(
    spot_ref, near_ref, other_ref, early_near_ref, early_other_ref, condition_ref, in_ref, final_ref, embed_ref,
    late_ref, grad_ref, near_act_ref, far_act_ref, order
):
    me = spot_ref[0]
    pairs, width = near_ref.shape[0], embed_ref.shape[1]
    late = jnp.concatenate([ref[pair] for pair in range(pairs) for ref in (near_ref, other_ref)], 0)
    late_ref[...] = late
    early = [ref[pair, 0] for pair in range(pairs) for ref in (early_near_ref, early_other_ref)]
    early = jnp.concatenate(early, 0)
    grad = dot_nt(late, in_ref[0, :, : 5 * D].astype(BF))
    grad = grad + dot_nt(early[:, :D], in_ref[0, :, 5 * D :].astype(BF))
    grad = grad + dot_nt(early[:, D:], final_ref[...].astype(BF))
    condition = condition_ref[...]
    turn = 1.0 / (1.0 + jnp.exp(-condition))
    grad = grad * (turn * (1.0 + condition * (1.0 - turn)))
    batch = order.shape[1]
    for block in range(2 * pairs):
        order[me ^ block] = grad[block * batch : (block + 1) * batch, :]
    grad = order[...].reshape(grad.shape).astype(BF)
    grad_ref[...] = grad
    for entry in range(2 * pairs):
        start = pl.multiple_of(TFREQ + PATCH + (me ^ entry) * width, 16)
        part = dot_nt(grad, embed_ref[pl.ds(start, width), :])
        (far_act_ref if entry % 2 else near_act_ref)[entry // 2] = part


def condition_back(spot, near, other, early_near, early_other, condition, in_mats, final, embed):
    width = embed.shape[1]
    count = condition.shape[0]
    operands = [spot, near, other, early_near, early_other, condition, in_mats, final, embed]
    in_specs = [pl.BlockSpec(memory_space=pltpu.SMEM)] + [whole(part.shape) for part in operands[1:6]]
    in_specs += [pl.BlockSpec((1, width, 6 * D), lambda step: (0, 0, 0)), whole(final.shape), whole(embed.shape)]
    half = (near.shape[0], count, width)
    out_shape = [
        shape_of((count, 5 * D), BF),
        shape_of((count, width), BF),
        shape_of(half, F32),
        shape_of(half, F32),
    ]
    return pl.pallas_call(
        condition_back_kernel,
        grid=(1,),
        in_specs=in_specs,
        out_specs=[whole(out.shape) for out in out_shape],
        out_shape=out_shape,
        scratch_shapes=[pltpu.VMEM((2 * half[0], near.shape[1], width), F32)],
        compiler_params=pltpu.CompilerParams(vmem_limit_bytes=VMEM_LIMIT),
        name="condition_back",
        cost_estimate=cost(4),
    )(*operands)


BIAS_PARTS = (B_PATCH, B_QUERY, B_VALUE, B_PROJ, B_UP, B_UP + 1, B_UP + 2, B_UP + 3, B_DOWN)


def condition_grads_kernel(spot_ref, marks_ref, features_ref, time_act_ref, act_ref, early_near_ref, early_other_ref, *refs, groups):
    late, last, refs = refs[:groups], refs[groups : 2 * groups], refs[2 * groups :]
    gada_ref, gembed_ref, gtable_ref, bias_ref, message_ref, squares_ref = refs[:6]
    early_all, late_all, grads_all = refs[6:]
    me, group = spot_ref[0], spot_ref[1]
    team = late[0].shape[0]
    width = act_ref.shape[1]
    shards = D // width
    for entry in range(groups):
        here = pl.ds(pl.multiple_of((group ^ entry) * team, team), team)
        early = [ref[pair, entry] for pair in range(shards // 2) for ref in (early_near_ref, early_other_ref)]
        early_all[here, :] = jnp.concatenate(early, 0)
        late_all[here, :] = late[entry][...]
        for part in range(2):
            blocks = []
            for block in range(shards):
                start = pl.multiple_of(part * team + (me ^ block) * (team // shards), 8)
                blocks.append(last[entry][pl.ds(start, team // shards), :])
            grads_all[here, part * width : (part + 1) * width] = jnp.concatenate(blocks, 0).astype(BF)
    rest = [ref[2 * team :, :] for ref in last]
    while len(rest) > 1:
        rest = [rest[i] + rest[i + 1] for i in range(0, len(rest), 2)]
    rest = rest[0]
    act = act_ref[...]
    grad_time = grads_all[:, :width]
    grad_condition = grads_all[:, width:]
    gada_ref[:, : 5 * D] = dot_tn(act, late_all[...])
    gada_ref[:, 5 * D :] = dot_tn(act, early_all[...])
    marks = marks_ref[...].astype(jnp.int32)
    label = marks[:, 2:3] * 32 + marks[:, 3:4]
    entry = lax.broadcasted_iota(jnp.int32, (marks.shape[0], 1024), 1)
    onehot = (entry == label).astype(F32).astype(BF)
    gtable_ref[...] = dot_tn(grad_condition, onehot)[:, :NCLASS]
    early_rows = PATCH + TFREQ
    gembed_ref[:, :PATCH] = rest[:PATCH, :].T
    gembed_ref[:, PATCH:early_rows] = dot_tn(grad_time, features_ref[...])
    for entry in range(shards):
        start = early_rows + entry * width
        gembed_ref[:, start : start + width] = dot_tn(grad_condition, time_act_ref[entry])
    late_sum = jnp.sum(late_all[...].astype(F32), 0, keepdims=True)
    early_sum = jnp.sum(early_all[...].astype(F32), 0, keepdims=True)
    bias_ref[B_TIME : B_ADA, :] = jnp.zeros((2, D), F32)
    for part in range(5):
        bias_ref[B_ADA + part : B_ADA + part + 1, :] = late_sum[:, part * D : (part + 1) * D]
    for part in range(3):
        row = B_FINAL + part - 1 if part else B_ADA + 5
        bias_ref[row : row + 1, :] = early_sum[:, part * D : (part + 1) * D]
    for part, row in enumerate(BIAS_PARTS):
        for column in range(shards):
            first = PATCH + part * shards + column
            bias_ref[row : row + 1, column * width : (column + 1) * width] = rest[first : first + 1, :]
    btime = jnp.sum(grads_all[...].astype(F32), 0, keepdims=True)
    message_ref[0:1, :] = btime[:, :width]
    message_ref[1:2, :] = btime[:, width:]
    tail = rest[PATCH + len(BIAS_PARTS) * shards :, :]
    message_ref[2:, :] = tail
    taken = tail.shape[0] // shards
    row = lax.broadcasted_iota(jnp.int32, tail.shape, 0) // shards + spot_ref[0] * taken
    head = jnp.where(row <= OUT, tail, 0.0)

    def square(part):
        return jnp.sum(jnp.sum(part * part, 0, keepdims=True), 1, keepdims=True)

    squares_ref[...] = square(gada_ref[...]) + square(gembed_ref[...]) + square(gtable_ref[...]) + square(btime) + square(head)


def condition_grads(spot, marks, features, time_act, act, early_near, early_other, late, last):
    groups = len(late)
    count, width = act.shape
    operands = [spot, marks, features, time_act, act, early_near, early_other] + late + last
    shards = D // width
    out_shape = [
        shape_of((width, 8 * D), F32),
        shape_of((width, PATCH + TFREQ + D), F32),
        shape_of((width, NCLASS), F32),
        shape_of((BIASES, D), F32),
        shape_of((2 + tail_rows(shards) * shards, width), F32),
        shape_of((1, 1), F32),
    ]
    return pl.pallas_call(
        partial(condition_grads_kernel, groups=groups),
        grid=(1,),
        in_specs=[pl.BlockSpec(memory_space=pltpu.SMEM)] + [whole(part.shape) for part in operands[1:]],
        out_specs=[whole(out.shape) for out in out_shape],
        out_shape=out_shape,
        scratch_shapes=[
            pltpu.VMEM((count, 3 * D), BF),
            pltpu.VMEM((count, 5 * D), BF),
            pltpu.VMEM((count, 2 * width), BF),
        ],
        compiler_params=pltpu.CompilerParams(vmem_limit_bytes=VMEM_LIMIT),
        name="condition_grads",
        cost_estimate=cost(6),
    )(*operands)


def swap(array_in, axis, hop):
    count = lax.axis_size(axis)
    return lax.ppermute(array_in, axis, [(place_of, place_of ^ hop) for place_of in range(count)])


def spread(array_in, axis):
    count = lax.axis_size(axis)
    if axis == "shard":
        near = jnp.stack([array_in] + [swap(array_in, axis, hop) for hop in range(2, count, 2)])
        return jnp.stack([near, swap(near, axis, 1)], 1).reshape((count,) + array_in.shape)
    return jnp.stack([array_in] + [swap(array_in, axis, hop) for hop in range(1, count)])


def total_of(parts):
    while len(parts) > 1:
        parts = [parts[i] + parts[i + 1] for i in range(0, len(parts), 2)]
    return parts[0]


def exchange_sum(near):
    return total_of([near[0]] + [swap(near[hop], "shard", 2 * hop) for hop in range(1, near.shape[0])])


def from_groups(array_in, tuned, first=1):
    count = lax.axis_size("grp")
    if tuned:
        pair = jnp.stack([array_in, swap(array_in, "grp", first)])
        far = swap(pair, "grp", 3 - first)
        parts = [pair[0], pair[1], far[0], far[1]]
        return parts if first == 1 else [parts[0], parts[2], parts[1], parts[3]]
    parts = jnp.broadcast_to(array_in[None], (count,) + array_in.shape)
    parts = ordered(lax.all_to_all(parts, "grp", 0, 0, tiled=True), "grp")
    return [parts[i] for i in range(count)]


def ordered(array_in, axis):
    count = lax.axis_size(axis)
    place_of = lax.axis_index(axis)
    bit = 1
    while bit < count:
        pairs = array_in.reshape((count // (2 * bit), 2, bit) + array_in.shape[1:])
        array_in = jnp.where(place_of & bit != 0, pairs[:, ::-1], pairs).reshape(array_in.shape)
        bit *= 2
    return array_in


def sum_spread(array_in, axis):
    parts = spread(array_in, axis)
    return total_of([parts[i] for i in range(parts.shape[0])])


def tie(arrays, after):
    return lax.optimization_barrier((arrays, after))[0]


DIRECT = 224


def rows_near(own):
    rows_all = own.shape[0]
    quarter = -(-rows_all // 64) * 16
    group = lax.axis_index("grp")
    start = jnp.where(group == 3, rows_all - quarter, group * quarter)
    part = lax.dynamic_slice_in_dim(own, start, quarter, 0)
    return [swap(part, "shard", hop) for hop in (2, 4, 6)]


def rows_far(near):
    return lax.all_gather(jnp.stack(near), "grp")


def rows_all(own, far):
    return [own, far, swap(own, "shard", 1), swap(far, "shard", 1)]


def quarter_start(rows_all, quarter, group):
    return jnp.where(group == 3, rows_all - quarter, group * quarter)


def cores_summed(grads):
    pairs = grads.reshape((4, 2) + grads.shape[1:])
    core = lax.axis_index("shard") % 2
    theirs = lax.dynamic_index_in_dim(pairs, 1 - core, 1, keepdims=False)
    mine = lax.dynamic_index_in_dim(pairs, core, 1, keepdims=False)
    return lower(mine.astype(F32) + swap(theirs, "shard", 1).astype(F32))


def groups_traded(grads):
    group = lax.axis_index("grp")
    rows_all = grads.shape[1]
    quarter = -(-rows_all // 64) * 16
    parts = []
    for hop in range(4):
        start = quarter_start(rows_all, quarter, group ^ hop)
        part = lax.dynamic_slice_in_dim(grads, start, quarter, 1)
        parts.append(swap(part, "grp", hop) if hop else part)
    return parts


def shards_traded(parts):
    return chips_traded(total_of([part.astype(F32) for part in parts]))


def chips_traded(total):
    low = lower(total)
    chip = lax.axis_index("shard") // 2
    own = lax.dynamic_index_in_dim(total, chip, 0, keepdims=False)
    return [own] + [
        swap(lax.dynamic_index_in_dim(low, chip ^ hop, 0, keepdims=False), "shard", 2 * hop) for hop in (1, 2, 3)
    ]


def shards_summed(parts):
    return lower(total_of([part.astype(F32) for part in parts]))


def quarters_joined(parts, *sizes):
    joined, first = [], 0
    for quarter, count in sizes:
        part = parts[:, first : first + quarter]
        first += quarter
        skipped = 4 * quarter - count // 8
        joined.append(jnp.concatenate([part[0], part[1], part[2], part[3, skipped:]]).astype(F32))
    return joined


def halves_added(part, bit):
    axis = part.ndim - 2
    half = part.shape[axis] // 2
    side = (lax.axis_index("grp") // bit) % 2
    ours = lax.dynamic_slice_in_dim(part, side * half, half, axis)
    theirs = lax.dynamic_slice_in_dim(part, (1 - side) * half, half, axis)
    return [ours, swap(theirs, "grp", bit)]


def matmul(formula, left, right):
    return jnp.einsum(formula, left, right, preferred_element_type=F32)


def lower(array_in):
    return array_in.astype(BF)


def summed(array_in, axes):
    return jnp.sum(array_in.astype(F32), axes)


def position_table():
    quarter = D // 4
    angular = np.exp(-math.log(10000.0) * np.arange(quarter) / quarter)
    position = np.arange(GRID * GRID)
    column = (position % GRID)[:, None] * angular
    row_pos = (position // GRID)[:, None] * angular
    table = np.concatenate([np.sin(column), np.cos(column), np.sin(row_pos), np.cos(row_pos)], 1)
    return jnp.asarray(table.astype(np.float32))


def pick_times(time_index, times):
    matches = time_index[:, None] == jnp.arange(times.shape[0], dtype=jnp.int32)[None, :]
    return jnp.sum(jnp.where(matches, times[None, :], 0.0), 1)


def condition_grads_plain(spot, marks, features, time_act, act, early_near, early_other, late, last):
    team, width = late[0].shape[0], act.shape[1]
    shards = D // width

    def in_exchange(part):
        part = part.reshape(2, shards, team // shards, width).transpose(1, 0, 2, 3)
        return ordered(part, "shard").transpose(1, 0, 2, 3).reshape(2 * team, width)

    early = jnp.stack([early_near, early_other], 1).transpose(2, 0, 1, 3, 4)
    early = early.reshape(len(late), team, 3 * D)
    early, late, last_all = [
        ordered(jnp.stack(parts), "grp").reshape(-1, parts[0].shape[1])
        for parts in (list(early), late, [in_exchange(part[: 2 * team]) for part in last])
    ]
    last_all = lower(last_all).reshape(-1, 2, team, width)
    grad_time, grad_condition = last_all[:, 0].reshape(-1, width), last_all[:, 1].reshape(-1, width)
    rest = total_of([part[2 * team :] for part in last])
    gada = jnp.concatenate([matmul("bd,be->de", act, late), matmul("bd,be->de", act, early)], 1)
    labels = (marks[:, 2:3] * 32.0 + marks[:, 3:4]).astype(jnp.int32)
    onehot = lower((labels == jnp.arange(NCLASS, dtype=jnp.int32)[None, :]).astype(F32))
    gtable = matmul("bd,bn->dn", grad_condition, onehot)
    gembed = jnp.concatenate(
        [
            rest[:PATCH].T,
            matmul("bd,bf->df", grad_time, features),
            matmul("be,sbd->esd", grad_condition, time_act).reshape(width, D),
        ],
        1,
    )
    bias = jnp.zeros((BIASES, D), F32)
    bias = bias.at[B_ADA : B_ADA + 5].set(summed(late, 0).reshape(5, D))
    early_sum = summed(early, 0).reshape(3, D)
    bias = bias.at[B_ADA + 5].set(early_sum[0]).at[B_FINAL:].set(early_sum[1:])
    parts = rest[PATCH : PATCH + len(BIAS_PARTS) * shards].reshape(len(BIAS_PARTS), D)
    for part, row in enumerate(BIAS_PARTS):
        bias = bias.at[row].set(parts[part])
    btime = jnp.stack([summed(grad_time, 0), summed(grad_condition, 0)])
    tail = rest[PATCH + len(BIAS_PARTS) * shards :]
    taken = tail.shape[0] // shards
    row = jnp.arange(tail.shape[0], dtype=jnp.int32)[:, None] // shards + spot[0] * taken
    head = jnp.where(row <= OUT, tail, 0.0)
    squares = sum(jnp.sum(part * part) for part in (gada, gembed, gtable, btime, head))
    return gada, gembed, gtable, bias, jnp.concatenate([btime, tail]), squares.reshape(1, 1)


def adamw(weight, moment_one, moment_two, gradient, factor):
    gradient = gradient * factor
    moment_one = BETA_ONE * moment_one + (1.0 - BETA_ONE) * gradient
    moment_two = BETA_TWO * moment_two + (1.0 - BETA_TWO) * gradient * gradient
    fix_one = 1.0 - BETA_ONE**STEP
    fix_two = 1.0 - BETA_TWO**STEP
    update = (
        moment_one / fix_one / (jnp.sqrt(moment_two / fix_two) + EPS_ADAM) + WEIGHT_DECAY * weight
    )
    return (weight - LEARN_RATE * update, moment_one, moment_two)


def per_device(
    latents, noise, velocity, labels, time_index, times,
    in_mats, out_mats, embed_mats, class_table, final_ada, head_mat, bias_vec,
    in_mats_first, out_mats_first, embed_first, table_first, final_first, head_first, bias_first,
    in_mats_second, out_mats_second, embed_second, table_second, final_second, head_second, bias_second,
):
    shards = lax.axis_size("shard")
    groups = lax.axis_size("grp")
    me = lax.axis_index("shard")
    mine = lax.axis_index("grp")
    batch = latents.shape[0]
    width = embed_mats.shape[1]
    team = shards * batch
    tuned = groups == 4 and shards == 8

    embed_low = lower(embed_mats)
    marks = jnp.stack([time_index // 32, time_index % 32, labels // 32, labels % 32], 1).astype(BF)
    marks = jnp.pad(marks, ((0, TFREQ - batch), (0, 128 - width - MARKS)))
    message = jnp.concatenate(
        [embed_low[PATCH : PATCH + TFREQ], embed_low[:PATCH], lower(bias_vec).reshape(BIASES, width)]
    )
    message = jnp.pad(message, ((0, MESSAGE - message.shape[0]), (0, 128 - width)))
    message = message + jnp.pad(marks, ((0, MESSAGE - TFREQ), (width, 0)))
    arrived = [swap(message, "shard", hop) for hop in range(2, shards, 2)]
    near_message = jnp.stack([message] + arrived)
    other_message = swap(near_message, "shard", 1)
    in_mats_early, out_mats_early = tie((in_mats, out_mats), message)

    def rows_of(first, count):
        return [lower(in_mats_early[0, :, first + part * D : first + (part + 1) * D]) for part in range(count)]

    own_qkv = jnp.concatenate(rows_of(6 * D, 3))
    own_feed = jnp.concatenate(rows_of(9 * D, FF // D) + [lower(out_mats_early[0])])
    spot = jnp.stack([me, mine]).astype(jnp.int32)
    if tuned:
        near_qkv = rows_near(own_qkv)
        traded = own_feed.shape[0] - DIRECT
        near_feed = rows_near(own_feed[:traded])
    else:
        qkv_pieces, feed_pieces = [[lax.all_gather(own, "shard")] for own in (own_qkv, own_feed)]
    times_row = jnp.pad(times, (0, -times.shape[0] % 128))[None]
    time_pre, condition, marks_team, wpatch, biases, near_mod, far_mod = condition_of_team(
        spot, near_message, other_message, times_row, embed_low, class_table.T, in_mats, final_ada, batch
    )
    if tuned:
        far_qkv = rows_far(tie(near_qkv, time_pre))
    near_mod = near_mod + swap(far_mod, "shard", 1)
    mods = lower(near_mod)
    mods = [near_mod[0]] + [swap(mods[hop], "shard", 2 * hop) for hop in range(1, shards // 2)]
    mod = total_of([part.astype(F32) for part in mods])[:, None, :]
    if tuned:
        far_feed = rows_far(tie(near_feed, (far_qkv, mod)))
    if tuned:
        direct = [swap(tie(own_feed[traded:], mod), "shard", hop) for hop in (2, 4, 6)]
    latents, noise, velocity, head_mat_late, marks_team = tie(
        (latents, noise, velocity, head_mat, marks_team), near_mod
    )
    if tuned:
        far_qkv = tie(far_qkv, near_mod)
        qkv_pieces = rows_all(own_qkv, far_qkv)
    moment = pick_times(time_index, times)
    noisy = lower((1.0 - moment)[:, None, None] * latents + moment[:, None, None] * noise)
    pos = position_table()
    a, qkv, o, wqkv = attend(spot, noisy, pos, wpatch, mod, biases, qkv_pieces, shards)
    if tuned:
        o, direct = lax.optimization_barrier((o, direct))
        direct = jnp.stack(direct)
        feed_pieces = rows_all(tie(own_feed, o), tie(far_feed, o)) + [direct, swap(direct, "shard", 1)]
    count_all = float(groups * shards * batch * SEQ * OUT)
    head_low = lower(head_mat_late)
    mid, y, m, g, slope, df, ds, dmod_feed, near_tail, far_tail, bdown, wup, wout = feed(
        spot, moment, noisy, pos, wpatch, o, mod, biases, head_low[:D],
        head_low[D:].astype(F32), velocity, feed_pieces, shards, count_all,
    )
    wout = wout.reshape(D + FF, D)
    tokens = batch * SEQ
    if tuned:
        marks_all = [marks_team] + [swap(marks_team, "grp", hop) for hop in (1, 2, 3)]
        mid, df, dmod_feed, marks_all = lax.optimization_barrier((mid, df, dmod_feed, marks_all))
    else:
        marks_all = from_groups(marks_team, tuned)
    early = lower(dmod_feed[:, 0])
    early = [early] + [swap(early, "grp", hop) for hop in range(1, groups)] if tuned else from_groups(early, tuned)
    gup, gout, bup, dm = feed_back(
        m.reshape(tokens, D), df.reshape(tokens, D), g, slope, wup, wout, 0, FF
    )
    gup, gout, bup, dm, early = lax.optimization_barrier((gup, gout, bup, dm, early))
    gup = lax.psum_scatter(gup, "shard", scatter_dimension=0)
    early = jnp.stack(early)
    early_far = [swap(early, "shard", hop) for hop in range(2, shards, 2)]
    dmid, do, dmod_mid, gout, bproj = middle_back(
        mid, dm.reshape(batch, SEQ, D), tie(ds, early), y, o, mod, biases, wout, gout
    )

    dmid, do, dmod_mid, gout, bproj, early, early_far = lax.optimization_barrier(
        (dmid, do, dmod_mid, gout, bproj, early, early_far)
    )

    marks_all, features, time_act, cond_act_all = condition_of_all(
        spot, near_message, other_message, times_row, embed_low, class_table.T, tie(marks_all, dmid)
    )
    gout = gout.reshape(shards, (D + FF) // shards, D)
    if tuned:
        gout = cores_summed(gout)
        early_near = jnp.stack([early] + early_far)
        near_tail, far_tail = [part.reshape(shards // 2, -1, width) for part in tie((near_tail, far_tail), dmid)]
        do = tie(do, (gout, early_near, near_tail, far_tail, features))
        gout_parts = groups_traded(gout)
    else:
        near_tail, far_tail = [part.reshape(shards // 2, -1, width) for part in (near_tail, far_tail)]
        early_near = jnp.stack([early] + early_far)
        gout = lax.psum_scatter(gout, "shard", scatter_dimension=0)
    early_other = swap(early_near, "shard", 1)
    dqkv, gqkv, gqkv_far, bqkv = attend_back(spot, qkv, do, a, shards)
    if tuned:
        dqkv, gqkv, gqkv_far, bqkv, gout_parts, early_other = lax.optimization_barrier(
            (dqkv, gqkv, gqkv_far, bqkv, gout_parts, early_other)
        )
    if tuned:
        gqkv = halves_added(lower(gqkv.astype(F32) + swap(gqkv_far, "shard", 1).astype(F32)), 2)
        gout_parts = shards_traded(gout_parts)
        dmid, dmod_mid, gup, bqkv, bproj, bup, bdown = tie(
            (dmid, dmod_mid, gup, bqkv, bproj, bup, bdown), gout_parts[0]
        )
        gup = halves_added(gup, 2)
    else:
        gqkv = jnp.stack([gqkv, gqkv_far], 1)
        gqkv = jnp.where(me % 2 == 0, gqkv, gqkv[:, ::-1]).reshape((shards,) + gqkv.shape[2:])
        gqkv = lax.psum_scatter(gqkv, "shard", scatter_dimension=0)
    dmod_attn, near_patch, far_patch, bpatch = stream_back(
        spot, dqkv, dmid, noisy, pos, wpatch, mod, biases, wqkv
    )
    if tuned:
        dmod_attn, near_patch, far_patch, bpatch, gup, gout_parts, gqkv = lax.optimization_barrier(
            (dmod_attn, near_patch, far_patch, bpatch, gup, gout_parts, gqkv)
        )
        gup, gout = shards_summed(gup), shards_summed(gout_parts)
        gqkv = halves_added(shards_summed(gqkv), 1)
    late = lower(jnp.concatenate([dmod_attn[:, 0], dmod_mid[:, 0]], 1))

    near_late = jnp.stack([late] + [swap(late, "shard", hop) for hop in range(2, shards, 2)])
    other_late = swap(near_late, "shard", 1)
    if tuned:
        other_late, gqkv = tie((other_late, gqkv), gout)
    late, grad_condition, near_act, far_act = condition_back(
        spot, near_late, other_late, early_near, early_other, condition, in_mats, final_ada, embed_low
    )
    bias_part = jnp.concatenate([bpatch, bqkv[:, :D], bqkv[:, 2 * D :], bproj, bup, bdown], 1)
    bias_part = jnp.broadcast_to(bias_part.reshape(1, -1, width), (shards // 2, len(BIAS_PARTS) * shards, width))

    far_act = jnp.concatenate([far_act, far_patch, bias_part, far_tail], 1)
    near_act = jnp.concatenate([near_act, near_patch, bias_part, near_tail], 1)
    near_act = near_act + swap(far_act, "shard", 1)
    acts = [near_act[0]] + [swap(near_act[hop], "shard", 2 * hop) for hop in range(1, near_act.shape[0])]

    def last_of(acts):
        act_part = total_of(acts)
        unused, time_pull = jax.vjp(jax.nn.silu, time_pre)
        grad_time = lower(time_pull(act_part[:team].reshape(time_pre.shape))[0]).reshape(team, width)
        return jnp.concatenate([grad_time.astype(F32), grad_condition.astype(F32), act_part[team:]])

    if tuned:
        late_x, late_y = swap(late, "grp", 1), swap(late, "grp", 2)
        acts, late_x, late_y, gqkv = lax.optimization_barrier((acts, late_x, late_y, gqkv))
        last = last_of(acts)
        gqkv = shards_traded(gqkv)
        gup = halves_added(tie(gup, last), 1)
        both = gout
        last_x, late_xy, both_x = swap(last, "grp", 1), swap(late_x, "grp", 2), swap(both, "grp", 1)
        last_x, late_xy, both_x, gqkv, gup = lax.optimization_barrier((last_x, late_xy, both_x, gqkv, gup))
        gup = shards_summed(gup)
        gqkv = jnp.concatenate([gup, shards_summed(gqkv)])
        pair = jnp.stack([last, last_x])
        both = jnp.stack([both, both_x])
        last_far, both_far, gqkv_x = swap(pair, "grp", 2), swap(both, "grp", 2), swap(gqkv, "grp", 1)
        last_far, gqkv_x = lax.optimization_barrier((last_far, gqkv_x))
        grads_last = [last, last_x, last_far[0], last_far[1]]
        grads_late = [late, late_x, late_y, late_xy]
        gqkv = jnp.stack([gqkv, gqkv_x])
        gqkv_far = swap(gqkv, "grp", 2)
        both = ordered(jnp.concatenate([both, both_far]), "grp")
        gqkv = ordered(jnp.concatenate([gqkv, gqkv_far]), "grp")
        gout = quarters_joined(both, (gout.shape[0], D + FF))[0]
        gup, gqkv = quarters_joined(gqkv, (gup.shape[0], FF), (gqkv.shape[1] - gup.shape[0], 3 * D))
        gfeed = [gup, gout]
    else:
        grads_last = from_groups(last_of(acts), tuned)
        grads_late = from_groups(late, tuned)
        gup, gout, gqkv = [
            total_of([part.astype(F32) for part in from_groups(grads, tuned)]) for grads in (gup, gout, gqkv)
        ]
        gfeed = [gup, gout]
    grads_of = condition_grads if tuned else condition_grads_plain
    gada, gembed, gtable, bias_grad, message, squares = grads_of(
        spot, marks_all, features, time_act, cond_act_all, early_near, early_other, grads_late, grads_last
    )
    gup, gout = gfeed
    share = bias_vec.shape[0]
    bias_grad = lax.dynamic_slice_in_dim(bias_grad.reshape(-1), me * share, share, 0)
    squares = squares + sum(jnp.sum(part * part) for part in (gup, gqkv, gout, bias_grad))
    message = jnp.concatenate([message, jnp.broadcast_to(squares, (6, width))])
    final = spread(message, "shard")
    grad_norm = jnp.sqrt(total_of([final[i, -1] for i in range(shards)]))
    factor = (CLIP_NORM / jnp.maximum(grad_norm, CLIP_NORM))[0]
    grad_norm = grad_norm[0]
    final = ordered(final, "shard")
    btime = jnp.concatenate([final[:, 0].reshape(-1), final[:, 1].reshape(-1)])
    tail = final[:, 2:-6].reshape(-1, D)
    head_grad = jnp.concatenate([tail[:OUT].T, tail[OUT : OUT + 1, :OUT]])
    loss_sum = tail[OUT + 1, 0]
    btime = jnp.concatenate([jnp.zeros((D,), F32), btime, jnp.zeros((12 * D + FF,), F32)])
    bias_grad = bias_grad + lax.dynamic_slice_in_dim(btime, me * share, share, 0)
    in_grad = jnp.concatenate(
        [gada[:, : 6 * D]]
        + [gqkv[part * width : (part + 1) * width] for part in range(3)]
        + [gup[part * width : (part + 1) * width] for part in range(FF // D)],
        1,
    )
    weights = (in_mats, out_mats, embed_mats, class_table, final_ada, head_mat, bias_vec)
    firsts = (in_mats_first, out_mats_first, embed_first, table_first, final_first, head_first, bias_first)
    seconds = (
        in_mats_second, out_mats_second, embed_second, table_second, final_second, head_second, bias_second
    )
    grads = (in_grad[None], gout[None], gembed.T, gtable.T, gada[:, 6 * D :], head_grad, bias_grad)
    stepped = [
        adamw(weight, moment_one, moment_two, gradient, factor)
        for weight, moment_one, moment_two, gradient in zip(weights, firsts, seconds, grads)
    ]
    return tuple(part[0] for part in stepped) + tuple(part[1] for part in stepped) + tuple(
        part[2] for part in stepped
    ) + (loss_sum, grad_norm)


def solution(mesh):
    images = P(("grp", "shard"))
    placed = (
        P(None, "shard", None),
        P(None, "shard", None),
        P(None, "shard"),
        P(None, "shard"),
        P("shard", None),
        P(),
        P("shard"),
    )
    return jax.shard_map(
        per_device,
        mesh=mesh,
        in_specs=(images,) * 5 + (P(),) + placed * 3,
        out_specs=placed * 3 + (P(), P()),
        check_vma=False,
    )
```
